128 devices in a mesh: seq: 32 (over y, x, core), ffn: 4 (over z).
Axes of the slice: x: 4, y: 4, z: 4, core: 2. Of those that a mesh axis runs over, the one named last changes fastest.
Arguments:
- stream_one: bfloat16 [4, 8192, 1024], P('ffn', 'seq'), may hold values from -6 to 6
- stream_two: bfloat16 [4, 8192, 1024], P('ffn', 'seq'), may hold values from -6 to 6
- doc_lengths: int32 [4, 9], P('ffn'), may hold values from 0 to 8192, as said below
- bucket_ids: int32 [4, 32, 8192], P('ffn', 'seq'), may hold values from 0 to 127
- norm1_gain: float32 [1024], replicated, may hold values from 0.5 to 1.5
- norm1_bias: float32 [1024], replicated, may hold values from -1.8 to 1.8
- w_qk: bfloat16 [1024, 1024], replicated, may hold values from -4 to 4
- w_value: bfloat16 [1024, 1024], replicated, may hold values from -0.1875 to 0.1875
- w_out: bfloat16 [1024, 1024], replicated, may hold values from -1.5 to 1.5
- norm2_gain: float32 [1024], replicated, may hold values from 0.5 to 1.5
- norm2_bias: float32 [1024], replicated, may hold values from -1.8 to 1.8
- w_up: bfloat16 [1024, 4096], P(None, 'ffn'), may hold values from -0.1875 to 0.1875
- w_down: bfloat16 [1024, 4096], P(None, 'ffn'), may hold values from -0.09375 to 0.09375
- grad_out_one: bfloat16 [4, 8192, 1024], P('ffn', 'seq'), may hold values from -6 to 6
- grad_out_two: bfloat16 [4, 8192, 1024], P('ffn', 'seq'), may hold values from -6 to 6
Outputs:
- output_one: bfloat16 [4, 8192, 1024], P('ffn', 'seq')
- output_two: bfloat16 [4, 8192, 1024], P('ffn', 'seq')
- grad_stream_one: float32 [4, 8192, 1024], P('ffn', 'seq')
- grad_stream_two: float32 [4, 8192, 1024], P('ffn', 'seq')
- grad_norm1_gain: float32 [1024], P(('seq', 'ffn'))
- grad_norm1_bias: float32 [1024], P(('seq', 'ffn'))
- grad_w_qk: float32 [1024, 1024], P(('seq', 'ffn'))
- grad_w_value: float32 [1024, 1024], P(('seq', 'ffn'))
- grad_w_out: float32 [1024, 1024], P(('seq', 'ffn'))
- grad_norm2_gain: float32 [1024], P(('seq', 'ffn'))
- grad_norm2_bias: float32 [1024], P(('seq', 'ffn'))
- grad_w_up: float32 [1024, 4096], P('seq', 'ffn')
- grad_w_down: float32 [1024, 4096], P('seq', 'ffn')
The draws below stay inside these ranges and needn't reach their ends.
Inputs may be any that keep to these rules, and one draw needn't show every extreme that they name: `doc_lengths`: each sequence's lengths sum to 8192; its fifth document starts before position 256 and ends after position 7936; the others may be empty.
All inputs are finite; a program needn't handle non-finite values.
Results may differ from the reference program's by a relative error of at most 0.017.
Values may be sent and summed in bfloat16 or wider, within the bound.
No kernel may reach another device: no remote copies, remote signals or barrier semaphores. Data moves between devices by JAX's collectives and lax.ppermute only.
A program may use at most 192 MiB of HBM per device.

```python
import jax
import jax.numpy as jnp
from jax import lax

HEADS = 8
DH = 128
D = 1024
FF = 4096
ROUNDS = 4
SPAN = 64
TOK_DEV = 256
LENGTH = 8192
SEQS = 4
NBUCKETS = 128


def draw_doc_lengths(key, part):
    key = jax.random.fold_in(key, 11)
    streams = jax.random.split(key, 4)
    opening = jax.random.randint(streams[0], (SEQS, 1), 1, TOK_DEV)
    closing = jax.random.randint(streams[1], (SEQS, 1), LENGTH - TOK_DEV + 1, LENGTH)
    lower_cuts = jax.random.randint(streams[2], (SEQS, 3), 0, 1 << 20) % (opening + 1)
    upper_cuts = closing + jax.random.randint(streams[3], (SEQS, 3), 0, 1 << 20) % (LENGTH - closing + 1)
    bounds = jnp.concatenate([jnp.zeros((SEQS, 1), jnp.int32), jnp.sort(lower_cuts, axis=1), opening, closing, jnp.sort(upper_cuts, axis=1), jnp.full((SEQS, 1), LENGTH, jnp.int32)], axis=1)
    return (bounds[:, 1:] - bounds[:, :-1]).astype(jnp.int32)


def set_ends(result, own_key, low, largest):
    shape = result.shape
    spot = [jax.random.randint(jax.random.fold_in(own_key, axis), (), 0, shape[axis]) for axis in range(len(shape))]
    result = result.at[tuple(spot)].set(low)
    longest = shape.index(max(shape))
    spot[longest] = (spot[longest] + 1) % shape[longest]
    return result.at[tuple(spot)].set(largest)


def levels(stream_key, shape, cuts, smallest, high):
    level, own = 1.0, jax.random.fold_in(stream_key, 6)
    for position, shards_of in cuts:
        steps = jnp.exp(jax.random.uniform(jax.random.fold_in(own, position), (shards_of,), jnp.float32, smallest / len(cuts), high / len(cuts)))
        level = level * jnp.repeat(steps, shape[position] // shards_of).reshape([-1 if axis == position else 1 for axis in range(len(shape))])
    return level


def gaussian(key, dims, scale, reach, shards=(), kind=jnp.bfloat16):
    result = scale * jax.random.normal(key, dims, jnp.float32)
    if shards:
        result = result * levels(key, dims, shards, -0.22, 0.18)
    return jnp.clip(result, -reach, reach).astype(kind)


def setup_inputs(seed: int = 0) -> dict:
    key_of = jax.random.split(jax.random.key(seed), 16)
    return {
        "stream_one": gaussian(key_of[0], (SEQS, LENGTH, D), 1.0, 6.0, ((0, 4), (1, 32))),
        "stream_two": gaussian(key_of[1], (SEQS, LENGTH, D), 1.0, 6.0, ((0, 4), (1, 32))),
        "doc_lengths": draw_doc_lengths(jax.random.fold_in(key_of[15], 71), 0),
        "bucket_ids": set_ends(jax.random.randint(key_of[3], (SEQS, HEADS * ROUNDS, LENGTH), 0, NBUCKETS), jax.random.fold_in(key_of[3], 1), 0, NBUCKETS - 1).astype(jnp.int32),
        "norm1_gain": jnp.clip(1.0 + 0.1 * jax.random.normal(key_of[4], (D,), jnp.float32), 0.5, 1.5),
        "norm1_bias": gaussian(key_of[5], (D,), 0.3, 1.8, (), jnp.float32),
        "w_qk": gaussian(key_of[6], (D, D), 0.7, 4.0),
        "w_value": gaussian(key_of[7], (D, D), D ** -0.5, 0.1875),
        "w_out": gaussian(key_of[8], (D, D), (D // 64) ** -0.5, 1.5),
        "norm2_gain": jnp.clip(1.0 + 0.1 * jax.random.normal(key_of[9], (D,), jnp.float32), 0.5, 1.5),
        "norm2_bias": gaussian(key_of[10], (D,), 0.3, 1.8, (), jnp.float32),
        "w_up": gaussian(key_of[11], (D, FF), D ** -0.5, 0.1875, ((1, 4),)),
        "w_down": gaussian(key_of[12], (D, FF), FF ** -0.5, 0.09375, ((1, 4),)),
        "grad_out_one": gaussian(key_of[13], (SEQS, LENGTH, D), 1.0, 6.0, ((0, 4), (1, 32))),
        "grad_out_two": gaussian(key_of[14], (SEQS, LENGTH, D), 1.0, 6.0, ((0, 4), (1, 32))),
    }


@jax.custom_vjp
def low(v):
    return lax.optimization_barrier(v.astype(jnp.bfloat16)).astype(jnp.float32)

@jax.custom_vjp
def low_back(v):
    return v

def low_keep(v):
    return (low(v), None)

def low_pass(kept, grad):
    return (grad,)

def back_keep(v):
    return (v, None)

def back_low(kept, grad):
    return (low(grad),)
low.defvjp(low_keep, low_pass)
low_back.defvjp(back_keep, back_low)
EPS_NORM = 1e-05
EPS_KEY = 1e-06
SELF_PENALTY = 1000.0
MASKED = -1000000000.0
PRECISE = lax.Precision.HIGHEST

def layer_norm(values, gain, offset):
    centre = lax.optimization_barrier(jnp.mean(values, axis=-1, keepdims=True))
    centred = values - centre
    spread = lax.optimization_barrier(jnp.mean(centred * centred, axis=-1, keepdims=True))
    return centred * lax.rsqrt(spread + EPS_NORM) * gain + offset

def segment_ids(lengths_row):
    ends = jnp.cumsum(lengths_row, dtype=jnp.int32)
    places = jnp.arange(LENGTH, dtype=jnp.int32)
    return lax.optimization_barrier(jnp.sum((places[:, None] >= ends[None, :]).astype(jnp.int32), axis=1, dtype=jnp.int32))

def span_view(array, blocks_per):
    spanned = array.reshape((-1, SPAN) + array.shape[1:])
    return spanned.reshape((-1, blocks_per) + spanned.shape[1:])

def key_view(array, blocks_per):
    spanned = array.reshape((-1, SPAN) + array.shape[1:])
    window = jnp.concatenate([jnp.roll(spanned, 1, 0), spanned], axis=1)
    return window.reshape((-1, blocks_per) + window.shape[1:])

def attend_block(pieces):
    queries, keys, key_values, query_pos, key_pos, query_seg, key_seg = pieces
    raw_dots = low_back(jnp.einsum('cqd,ckd->cqk', queries, keys, precision=PRECISE))
    scores = raw_dots * DH ** (-0.5)
    self_mask = (query_pos[:, :, None] == key_pos[:, None, :]).astype(jnp.float32)
    scores = scores - SELF_PENALTY * self_mask
    allowed = (query_seg[:, :, None] == key_seg[:, None, :]) & (key_pos[:, None, :] <= query_pos[:, :, None])
    scores = jnp.where(allowed, scores, MASKED)
    totals = jax.nn.logsumexp(scores, axis=-1)
    probabilities = low(jnp.exp(scores - totals[..., None]))
    outcome = jnp.einsum('cqk,ckd->cqd', probabilities, key_values, precision=PRECISE)
    return (outcome, totals)

def lsh_attention(qk_item, value_item, bucket_row, segment):
    span_count = LENGTH // SPAN
    blocks_per = min(span_count, max(1, 512 // SPAN))
    places = jnp.arange(LENGTH, dtype=jnp.int32)
    order = jnp.argsort(bucket_row * LENGTH + places).astype(jnp.int32)
    backward_index = jnp.zeros((LENGTH,), jnp.int32).at[order].set(places)
    normed = low(qk_item * lax.rsqrt(lax.optimization_barrier(jnp.sum(qk_item * qk_item, axis=-1, keepdims=True)) + EPS_KEY))
    queries = qk_item[order]
    unit_keys = normed[order]
    sorted_values = value_item[order]
    sorted_seg = segment[order]
    pieces = (span_view(queries, blocks_per), key_view(unit_keys, blocks_per), key_view(sorted_values, blocks_per), span_view(order, blocks_per), key_view(order, blocks_per), span_view(sorted_seg, blocks_per), key_view(sorted_seg, blocks_per))
    outcome, totals = lax.map(jax.checkpoint(attend_block), pieces)
    outcome = outcome.reshape(LENGTH, DH)[backward_index]
    totals = totals.reshape(LENGTH)[backward_index]
    return (outcome, totals)

def forward(weights, first_in, second_in, segment, bucket_rows):
    gain_one, bias_one, proj_qk, proj_value, proj_out, gain_two, bias_two, proj_up, proj_down = weights
    normed_one = low(layer_norm(second_in, gain_one, bias_one))
    shared_qk = low_back(low(jnp.dot(normed_one, proj_qk, precision=PRECISE)))
    value_rows = low_back(low(jnp.dot(normed_one, proj_value, precision=PRECISE)))

    def copies(array):
        head_rows = array.reshape(LENGTH, HEADS, DH).transpose(1, 0, 2)
        spread_out = jnp.broadcast_to(head_rows[:, None], (HEADS, ROUNDS, LENGTH, DH))
        return low_back(spread_out).reshape(HEADS * ROUNDS, LENGTH, DH)

    def attend_item(pieces):
        return lsh_attention(pieces[0], pieces[1], pieces[2], segment)
    attended, totals = lax.map(attend_item, (copies(shared_qk), copies(value_rows), bucket_rows))
    attended = low_back(low(attended)).reshape(HEADS, ROUNDS, LENGTH, DH)
    totals = totals.reshape(HEADS, ROUNDS, LENGTH)
    round_weight = jax.nn.softmax(totals, axis=1)
    mixture = lax.optimization_barrier(jnp.sum(round_weight[..., None] * attended, axis=1))
    mixture = low(mixture.transpose(1, 0, 2).reshape(LENGTH, HEADS * DH))
    sum_one = first_in + low_back(jnp.dot(mixture, proj_out, precision=PRECISE))
    normed_two = low(layer_norm(sum_one, gain_two, bias_two))
    pre_act = low_back(jnp.dot(normed_two, proj_up, precision=PRECISE))
    hidden = low(jax.nn.gelu(pre_act, approximate=False))
    sum_two = second_in + low_back(jnp.dot(hidden, proj_down.T, precision=PRECISE))
    return (sum_one, sum_two)

def reference(stream_one, stream_two, doc_lengths, bucket_ids, norm1_gain, norm1_bias, w_qk, w_value, w_out, norm2_gain, norm2_bias, w_up, w_down, grad_out_one, grad_out_two):
    params = (norm1_gain.astype(jnp.float32), norm1_bias.astype(jnp.float32), w_qk.astype(jnp.float32), w_value.astype(jnp.float32), w_out.astype(jnp.float32), norm2_gain.astype(jnp.float32), norm2_bias.astype(jnp.float32), w_up.astype(jnp.float32), w_down.astype(jnp.float32))

    def scan_step(running, seq_item):
        one_in, two_in, lengths_row, bucket_rows, grad_one_in, grad_two_in = seq_item
        segment = segment_ids(lengths_row)

        def forward_one(weights, first_in, second_in):
            return forward(weights, first_in, second_in, segment, bucket_rows)
        outputs, pullback = jax.vjp(forward_one, params, one_in.astype(jnp.float32), two_in.astype(jnp.float32))
        weight_grads, grad_one, grad_two = pullback((grad_one_in.astype(jnp.float32), grad_two_in.astype(jnp.float32)))
        running = jax.tree.map(lambda acc, extra: acc + extra, running, weight_grads)
        return (running, (outputs[0].astype(jnp.bfloat16), outputs[1].astype(jnp.bfloat16), grad_one, grad_two))
    zero_grads = jax.tree.map(jnp.zeros_like, params)
    gradients, results = lax.scan(scan_step, zero_grads, (stream_one, stream_two, doc_lengths, bucket_ids, grad_out_one, grad_out_two))
    return (results[0], results[1], results[2], results[3], gradients[0], gradients[1], gradients[2], gradients[3], gradients[4], gradients[5], gradients[6], gradients[7], gradients[8])
```

```python
import functools
import jax
import jax.numpy as jnp
from jax import lax
from jax.experimental import pallas as pl
from jax.experimental.pallas import tpu as pltpu
from jax.sharding import PartitionSpec as P
HEADS = 8
DH = 128
ROUNDS = 4
SPAN = 64
EPS_NORM = 1e-05
EPS_KEY = 1e-06
SCALE = DH ** (-0.5)
EXTRA = 16
F32, BF16 = jnp.float32, jnp.bfloat16
VMEM_LIMIT = 60 * 2**20

def vm(n):
    return [pl.BlockSpec(memory_space=pltpu.VMEM)] * n

def split3(x):
    a = x.astype(BF16)
    r = x - a.astype(F32)
    b = r.astype(BF16)
    c = (r - b.astype(F32)).astype(BF16)
    return a, b, c

def attend_kernel(order, rows, bias, msg, q_out, keys, vals, probs, xq, xv, sq, sv):
    length = rows.shape[0]
    own = msg.shape[0] // (length // 256) - EXTRA

    def widen(b, c):
        at = pl.ds(b * 256, 256)
        xq[at, :] = rows[at, :DH].astype(F32)
        xv[at, :] = rows[at, DH:].astype(F32)
        return c
    lax.fori_loop(0, length // 256, widen, 0)

    def gather(b, c):
        for u in range(64):
            i = b * 64 + u
            src = order[i]
            sq[pl.ds(i, 1), :] = xq[pl.ds(src, 1), :]
            sv[pl.ds(i, 1), :] = xv[pl.ds(src, 1), :]
        return c
    lax.fori_loop(0, length // 64, gather, 0)

    def keys_of(b, c):
        at = pl.ds(b * 256, 256)
        q = sq[at, :]
        unit = q * lax.rsqrt(jnp.sum(q * q, axis=1, keepdims=True) + EPS_KEY)
        q_out[at, :] = q.astype(BF16)
        ahead = pl.ds(b * 256 + SPAN, 256)
        keys[ahead, :] = unit.astype(BF16)
        vals[ahead, :] = sv[at, :].astype(BF16)
        return c
    lax.fori_loop(0, length // 256, keys_of, 0)
    keys[0:SPAN, :] = keys[length:length + SPAN, :]
    vals[0:SPAN, :] = vals[length:length + SPAN, :]

    def block(b, c):
        for u in range(8):
            base = pl.multiple_of((b * 8 + u) * SPAN, SPAN)
            at, win = pl.ds(base, SPAN), pl.ds(base, 2 * SPAN)
            s = lax.dot_general(q_out[at, :], keys[win, :], (((1,), (1,)), ((), ())), preferred_element_type=F32)
            s = s * SCALE + bias[at, :].astype(F32)
            top = jnp.max(s, axis=1, keepdims=True)
            e = jnp.exp(s - top)
            total = jnp.sum(e, axis=1, keepdims=True)
            p = (e * (1.0 / total)).astype(BF16)
            probs[at, :] = p
            sq[at, :] = jnp.dot(p, vals[win, :], preferred_element_type=F32)
            sv[at, :] = jnp.broadcast_to(top + jnp.log(total), (SPAN, DH))
        return c
    lax.fori_loop(0, length // (8 * SPAN), block, 0)

    def scatter(b, c):
        for u in range(64):
            i = b * 64 + u
            dst = order[i]
            xq[pl.ds(dst, 1), :] = sq[pl.ds(i, 1), :]
            xv[pl.ds(dst, 1), :] = sv[pl.ds(i, 1), :]
        return c
    lax.fori_loop(0, length // 64, scatter, 0)

    eye = (lax.broadcasted_iota(jnp.int32, (128, 128), 0) == lax.broadcasted_iota(jnp.int32, (128, 128), 1))

    def send(b, c):
        at = pl.ds(b * 256, 256)
        to = pl.multiple_of(b * (256 + EXTRA), EXTRA)
        msg[pl.ds(to, 256), :] = xq[at, :].astype(BF16)
        lo = jnp.sum(jnp.where(eye, xv[pl.ds(b * 256, 128), :], 0.0), axis=0, keepdims=True)
        hi = jnp.sum(jnp.where(eye, xv[pl.ds(b * 256 + 128, 128), :], 0.0), axis=0, keepdims=True)
        parts = split3(lo) + split3(hi)
        tail = jnp.concatenate([p.astype(F32) for p in parts] + [jnp.zeros((EXTRA - 6, 128), F32)], axis=0)
        msg[pl.ds(to + 256, EXTRA), :] = tail.astype(BF16)
        return c
    lax.fori_loop(0, length // 256, send, 0)

def attend(order, rows, bias):
    length = rows.shape[0]
    blocks = length // 256
    sd = jax.ShapeDtypeStruct
    return pl.pallas_call(
        attend_kernel,
        out_shape=[sd((blocks * (256 + EXTRA), DH), BF16), sd((length, DH), BF16), sd((length + SPAN, DH), BF16), sd((length + SPAN, DH), BF16), sd((length, DH), BF16)],
        in_specs=[pl.BlockSpec(memory_space=pltpu.SMEM)] + vm(2),
        out_specs=vm(5),
        scratch_shapes=[pltpu.VMEM((length, DH), F32)] * 4,
        compiler_params=pltpu.CompilerParams(vmem_limit_bytes=VMEM_LIMIT),
        name="attend",
    )(order, rows, bias)

def back_kernel(order, msg, q_in, keys, vals, probs, out, xg, xd, sg, sd_, du, dv):
    length = q_in.shape[0]

    def widen(b, c):
        at = pl.ds(b * 256, 256)
        frm = pl.multiple_of(b * (256 + EXTRA), EXTRA)
        xg[at, :] = msg[pl.ds(frm, 256), :].astype(F32)
        t = msg[pl.ds(frm + 256, EXTRA), :].astype(F32)
        lo = t[0:1] + t[1:2] + t[2:3]
        hi = t[3:4] + t[4:5] + t[5:6]
        xd[pl.ds(b * 256, 128), :] = jnp.transpose(jnp.broadcast_to(lo, (128, 128)))
        xd[pl.ds(b * 256 + 128, 128), :] = jnp.transpose(jnp.broadcast_to(hi, (128, 128)))
        return c
    lax.fori_loop(0, length // 256, widen, 0)

    def gather(b, c):
        for u in range(64):
            i = b * 64 + u
            src = order[i]
            sg[pl.ds(i, 1), :] = xg[pl.ds(src, 1), :]
            sd_[pl.ds(i, 1), :] = xd[pl.ds(src, 1), :]
        return c
    lax.fori_loop(0, length // 64, gather, 0)

    du[0:SPAN, :] = jnp.zeros((SPAN, DH), F32)
    dv[0:SPAN, :] = jnp.zeros((SPAN, DH), F32)

    def block(b, c):
        for u in range(8):
            base = pl.multiple_of((b * 8 + u) * SPAN, SPAN)
            at, win, nxt = pl.ds(base, SPAN), pl.ds(base, 2 * SPAN), pl.ds(base + SPAN, SPAN)
            g = sg[at, :].astype(BF16)
            p = probs[at, :]
            gp = lax.dot_general(g, vals[win, :], (((1,), (1,)), ((), ())), preferred_element_type=F32)
            gs = p.astype(F32) * (gp - sd_[at, :])
            gd = (gs * SCALE).astype(BF16)
            sg[at, :] = jnp.dot(gd, keys[win, :], preferred_element_type=F32)
            wu = lax.dot_general(gd, q_in[at, :], (((0,), (0,)), ((), ())), preferred_element_type=F32)
            wv = lax.dot_general(p, g, (((0,), (0,)), ((), ())), preferred_element_type=F32)
            du[at, :] += wu[:SPAN]
            du[nxt, :] = wu[SPAN:]
            dv[at, :] += wv[:SPAN]
            dv[nxt, :] = wv[SPAN:]
        return c
    lax.fori_loop(0, length // (8 * SPAN), block, 0)
    du[length:length + SPAN, :] += du[0:SPAN, :]
    dv[length:length + SPAN, :] += dv[0:SPAN, :]

    def norm(b, c):
        at, ahead = pl.ds(b * 256, 256), pl.ds(b * 256 + SPAN, 256)
        q = q_in[at, :].astype(F32)
        r = lax.rsqrt(jnp.sum(q * q, axis=1, keepdims=True) + EPS_KEY)
        d = du[ahead, :]
        along = jnp.sum(q * d, axis=1, keepdims=True)
        sg[at, :] = sg[at, :] + r * d - q * (r * r * r * along)
        return c
    lax.fori_loop(0, length // 256, norm, 0)

    def scatter(b, c):
        for u in range(64):
            i = b * 64 + u
            dst = order[i]
            xg[pl.ds(dst, 1), :] = sg[pl.ds(i, 1), :]
            xd[pl.ds(dst, 1), :] = dv[pl.ds(i + SPAN, 1), :]
        return c
    lax.fori_loop(0, length // 64, scatter, 0)

    def narrow(b, c):
        at = pl.ds(b * 256, 256)
        out[at, :DH] = xg[at, :].astype(BF16)
        out[at, DH:] = xd[at, :].astype(BF16)
        return c
    lax.fori_loop(0, length // 256, narrow, 0)

def attend_back(order, msg, q_in, keys, vals, probs):
    length = q_in.shape[0]
    return pl.pallas_call(
        back_kernel,
        out_shape=jax.ShapeDtypeStruct((length, 2 * DH), BF16),
        in_specs=[pl.BlockSpec(memory_space=pltpu.SMEM)] + vm(5),
        out_specs=pl.BlockSpec(memory_space=pltpu.VMEM),
        scratch_shapes=[pltpu.VMEM((length, DH), F32)] * 4 + [pltpu.VMEM((length + SPAN, DH), F32)] * 2,
        compiler_params=pltpu.CompilerParams(vmem_limit_bytes=VMEM_LIMIT),
        name="attend_back",
    )(order, msg, q_in, keys, vals, probs)

def prepare(bucket_row, ends):
    length = bucket_row.shape[0]
    places = jnp.arange(length, dtype=jnp.int32)
    _, order = lax.sort((bucket_row * length + places, places), num_keys=1)
    pos = order.reshape(-1, SPAN)
    start = jnp.max(jnp.where(ends <= pos[..., None], ends, 0), axis=-1)
    window = jnp.concatenate([jnp.roll(pos, 1, 0), pos], axis=1)
    k, q = window[:, None, :], pos[:, :, None]
    bias = jnp.where((k >= start[:, :, None]) & (k <= q), jnp.where(k == q, -1000.0, 0.0), -1e9)
    return order, bias.astype(BF16).reshape(length, 2 * SPAN)

def layer_rows(x, gain, offset):
    centred = x - jnp.mean(x, axis=1, keepdims=True)
    inverse = lax.rsqrt(jnp.mean(centred * centred, axis=1, keepdims=True) + EPS_NORM)
    return centred * inverse * gain + offset


def layer_back(x, grad, gain):
    centred = x - jnp.mean(x, axis=1, keepdims=True)
    inverse = lax.rsqrt(jnp.mean(centred * centred, axis=1, keepdims=True) + EPS_NORM)
    unit = centred * inverse
    grad_gain = jnp.sum(grad * unit, axis=0, keepdims=True)
    grad_offset = jnp.sum(grad, axis=0, keepdims=True)
    scaled = grad * gain
    inner = jnp.mean(scaled * unit, axis=1, keepdims=True)
    grad_x = inverse * (scaled - jnp.mean(scaled, axis=1, keepdims=True) - unit * inner)
    return grad_x, grad_gain, grad_offset


def project_kernel(x, gain, offset, w_qk, w_value, msg, normed_out):
    rows = x.shape[0]
    normed = layer_rows(x[...].astype(F32), gain[...], offset[...]).astype(BF16)
    normed_out[...] = normed
    for h in range(HEADS):
        at = slice(h * DH, (h + 1) * DH)
        q = jnp.dot(normed, w_qk[:, at], preferred_element_type=F32).astype(BF16)
        v = jnp.dot(normed, w_value[:, at], preferred_element_type=F32).astype(BF16)
        for r in range(ROUNDS):
            msg[h * ROUNDS + r, :, :DH] = q
            msg[h * ROUNDS + r, :, DH:] = v


def project(x, gain, offset, w_qk, w_value):
    rows, width = x.shape
    return pl.pallas_call(
        project_kernel,
        out_shape=[
            jax.ShapeDtypeStruct((HEADS * ROUNDS, rows, 2 * DH), BF16),
            jax.ShapeDtypeStruct((rows, width), BF16),
        ],
        in_specs=vm(5),
        out_specs=vm(2),
        compiler_params=pltpu.CompilerParams(vmem_limit_bytes=VMEM_LIMIT),
        name="project",
    )(x, gain, offset, w_qk, w_value)


def combine_kernel(msg, x, w_out, gain, offset, mix, low_mix, first, first_low, normed, weights):
    rows = x.shape[0]
    for half in range(2):
        logs = []
        for r in range(ROUNDS):
            lines = []
            for h in range(HEADS):
                tail = msg[h * ROUNDS + r, rows : rows + EXTRA, :].astype(F32)
                k = half * 3
                lines.append(tail[k : k + 1] + tail[k + 1 : k + 2] + tail[k + 2 : k + 3])
            logs.append(jnp.concatenate(lines, axis=0))
        top = jnp.maximum(jnp.maximum(logs[0], logs[1]), jnp.maximum(logs[2], logs[3]))
        powers = [jnp.exp(v - top) for v in logs]
        inverse = 1.0 / (powers[0] + powers[1] + powers[2] + powers[3])
        lines = [v * inverse for v in powers]
        lines.append(jnp.zeros((128 - HEADS * ROUNDS, 128), F32))
        weights[half * 128 : half * 128 + 128, :] = jnp.transpose(jnp.concatenate(lines, axis=0))
    for h in range(HEADS):
        total = jnp.zeros((rows, DH), F32)
        for r in range(ROUNDS):
            j = r * HEADS + h
            total = total + weights[:, j : j + 1] * msg[h * ROUNDS + r, 0:rows, :].astype(F32)
        mix[:, h * DH : (h + 1) * DH] = total
        low_mix[:, h * DH : (h + 1) * DH] = total.astype(BF16)
    summed = x[...].astype(F32) + jnp.dot(low_mix[...], w_out[...], preferred_element_type=F32)
    first[...] = summed
    first_low[...] = summed.astype(BF16)
    normed[...] = layer_rows(summed, gain[...], offset[...]).astype(BF16)


def combine(msg, x, w_out, gain, offset):
    rows, width = x.shape
    sd = jax.ShapeDtypeStruct
    return pl.pallas_call(
        combine_kernel,
        out_shape=[
            sd((rows, width), F32),
            sd((rows, width), BF16),
            sd((rows, width), F32),
            sd((rows, width), BF16),
            sd((rows, width), BF16),
            sd((rows, 128), F32),
        ],
        in_specs=vm(5),
        out_specs=vm(6),
        compiler_params=pltpu.CompilerParams(vmem_limit_bytes=VMEM_LIMIT),
        name="combine",
    )(msg, x, w_out, gain, offset)


def uncombine_kernel(
    grads, first, gain, grad_one, w_out, mix, weights, grad_first, low_first, msg, grad_gain, grad_offset
):
    rows = first.shape[0]
    total = grads[0].astype(F32)
    for k in range(1, grads.shape[0]):
        total = total + grads[k].astype(F32)
    grad_x, gg, go = layer_back(first[...], total, gain[...])
    grad_gain[...] = gg
    grad_offset[...] = go
    grad_x = grad_x + grad_one[...].astype(F32)
    grad_first[...] = grad_x
    low = grad_x.astype(BF16)
    low_first[...] = low
    lane = lax.broadcasted_iota(jnp.int32, (rows, 128), 1)
    inner = jnp.zeros((rows, 128), F32)
    for h in range(HEADS):
        at = slice(h * DH, (h + 1) * DH)
        grad_mix = lax.dot_general(low, w_out[at, :], (((1,), (1,)), ((), ())), preferred_element_type=F32)
        dots = jnp.sum(grad_mix * mix[:, at], axis=1, keepdims=True)
        inner = jnp.where(lane % HEADS == h, dots, inner)
        for r in range(ROUNDS):
            j = r * HEADS + h
            msg[h * ROUNDS + r, 0:rows, :] = (weights[:, j : j + 1] * grad_mix).astype(BF16)
    inner = inner * weights[...]
    low_lines = [p.astype(F32) for p in split3(jnp.transpose(inner[0:128]))]
    high_lines = [p.astype(F32) for p in split3(jnp.transpose(inner[128:256]))]
    blank = jnp.zeros((EXTRA - 6, 128), F32)
    for h in range(HEADS):
        for r in range(ROUNDS):
            j = r * HEADS + h
            tail = [p[j : j + 1] for p in low_lines + high_lines] + [blank]
            msg[h * ROUNDS + r, rows : rows + EXTRA, :] = jnp.concatenate(tail, axis=0).astype(BF16)


def uncombine(grads, first, gain, grad_one, w_out, mix, weights):
    rows, width = first.shape
    sd = jax.ShapeDtypeStruct
    return pl.pallas_call(
        uncombine_kernel,
        out_shape=[
            sd((rows, width), F32),
            sd((rows, width), BF16),
            sd((HEADS * ROUNDS, rows + EXTRA, DH), BF16),
            sd((1, width), F32),
            sd((1, width), F32),
        ],
        in_specs=vm(7),
        out_specs=vm(5),
        compiler_params=pltpu.CompilerParams(vmem_limit_bytes=VMEM_LIMIT),
        name="uncombine",
    )(grads, first, gain, grad_one, w_out, mix, weights)


def finish_kernel(
    msg, normed, x, gain, w_qk, w_value, grad_two, grad_second, part_qk, part_value, grad_gain, grad_offset, gq, gv
):
    rows = x.shape[0]
    for h in range(HEADS):
        at = slice(h * DH, (h + 1) * DH)
        total = msg[h * ROUNDS].astype(F32)
        for r in range(1, ROUNDS):
            total = total + msg[h * ROUNDS + r].astype(F32)
        gq[:, at] = total[:, :DH].astype(BF16)
        gv[:, at] = total[:, DH:].astype(BF16)
    flip = (((0,), (0,)), ((), ()))
    part_qk[...] = lax.dot_general(normed[...], gq[...], flip, preferred_element_type=F32).astype(BF16)
    part_value[...] = lax.dot_general(normed[...], gv[...], flip, preferred_element_type=F32).astype(BF16)
    across = (((1,), (1,)), ((), ()))
    grad_normed = lax.dot_general(gq[...], w_qk[...], across, preferred_element_type=F32)
    grad_normed = grad_normed + lax.dot_general(gv[...], w_value[...], across, preferred_element_type=F32)
    grad_x, gg, go = layer_back(x[...].astype(F32), grad_normed, gain[...])
    grad_gain[...] = gg
    grad_offset[...] = go
    grad_second[...] = grad_x + grad_two[...].astype(F32)


def finish(msg, normed, x, gain, w_qk, w_value, grad_two):
    rows, width = x.shape
    sd = jax.ShapeDtypeStruct
    return pl.pallas_call(
        finish_kernel,
        out_shape=[
            sd((rows, width), F32),
            sd((width, width), BF16),
            sd((width, width), BF16),
            sd((1, width), F32),
            sd((1, width), F32),
        ],
        in_specs=vm(7),
        out_specs=vm(5),
        scratch_shapes=[pltpu.VMEM((rows, width), BF16)] * 2,
        compiler_params=pltpu.CompilerParams(vmem_limit_bytes=VMEM_LIMIT),
        name="finish",
    )(msg, normed, x, gain, w_qk, w_value, grad_two)


def gelu_exact(values):
    return jax.nn.gelu(values, approximate=False)


def swap(array, axis):
    return lax.all_to_all(array, axis, split_axis=0, concat_axis=0, tiled=True)


def summed_rows(array):
    rows, width = array.shape
    seqs, ffns = lax.axis_size("seq"), lax.axis_size("ffn")
    near = swap(array.reshape(seqs, rows // seqs, width), "seq").astype(F32).sum(axis=0)
    near = near.astype(BF16).reshape(ffns, -1, width)
    return swap(near, "ffn").astype(F32).sum(axis=0)


def shards(
    stream_one,
    stream_two,
    doc_lengths,
    bucket_ids,
    norm1_gain,
    norm1_bias,
    w_qk,
    w_value,
    w_out,
    norm2_gain,
    norm2_bias,
    w_up,
    w_down,
    grad_out_one,
    grad_out_two,
):
    rows, width = stream_one.shape[1:]
    gain_one, bias_one = norm1_gain.reshape(1, -1), norm1_bias.reshape(1, -1)
    gain_two, bias_two = norm2_gain.reshape(1, -1), norm2_bias.reshape(1, -1)
    grad_rows = lax.all_gather(grad_out_two[0], "ffn", axis=0, tiled=True)
    msg, normed_one = project(stream_two[0], gain_one, bias_one, w_qk, w_value)
    received = swap(msg, "seq").reshape(-1, 2 * DH)
    order, bias = prepare(bucket_ids[0, 0], jnp.cumsum(doc_lengths[0]))
    sent, queries, keys, vals, probs = attend(order, received, bias)
    per_round = swap(sent.reshape(-1, rows + EXTRA, DH), "seq")
    mix, low_mix, first, first_low, normed_two, weights = combine(
        per_round, stream_one[0], w_out, gain_two, bias_two
    )

    gathered = lax.all_gather(normed_two, "ffn", axis=0, tiled=True)
    pre_act = jnp.dot(gathered, w_up, preferred_element_type=F32)
    hidden = gelu_exact(pre_act).astype(BF16)
    across = (((1,), (1,)), ((), ()))
    out_part = lax.dot_general(hidden, w_down, across, preferred_element_type=F32).astype(BF16)
    sum_two = stream_two[0].astype(F32) + swap(out_part.reshape(-1, rows, width), "ffn").astype(F32).sum(axis=0)
    grad_hidden = jnp.dot(grad_rows, w_down, preferred_element_type=F32)
    grad_pre = jax.vjp(gelu_exact, pre_act)[1](grad_hidden)[0].astype(BF16)
    flip = (((0,), (0,)), ((), ()))
    grad_down_part = lax.dot_general(grad_rows, hidden, flip, preferred_element_type=F32).astype(BF16)
    grad_up_part = lax.dot_general(gathered, grad_pre, flip, preferred_element_type=F32).astype(BF16)
    grad_part = lax.dot_general(grad_pre, w_up, across, preferred_element_type=F32).astype(BF16)
    arrived = swap(grad_part.reshape(-1, rows, width), "ffn")

    grad_first, low_first, msg, grad_gain_two, grad_bias_two = uncombine(
        arrived, first, gain_two, grad_out_one[0], w_out, mix, weights
    )
    part_out = lax.dot_general(low_mix, low_first, flip, preferred_element_type=F32).astype(BF16)
    far = swap(msg, "seq").reshape(-1, DH)
    copies = attend_back(order, far, queries, keys, vals, probs)
    back = swap(copies.reshape(-1, rows, 2 * DH), "seq")
    grad_second, part_qk, part_value, grad_gain_one, grad_bias_one = finish(
        back, normed_one, stream_two[0], gain_one, w_qk, w_value, grad_out_two[0]
    )
    small = jnp.concatenate([grad_gain_one, grad_bias_one, grad_gain_two, grad_bias_two], axis=0)
    small = lax.psum_scatter(small.T, ("seq", "ffn"), scatter_dimension=0, tiled=True)
    heavy = summed_rows(jnp.concatenate([part_qk, part_value], axis=1))
    grad_w_out = summed_rows(part_out)
    seqs = lax.axis_size("seq")
    grad_up = swap(grad_up_part.reshape(seqs, -1, width), "seq").astype(F32).sum(axis=0)
    grad_down = swap(grad_down_part.reshape(seqs, -1, width), "seq").astype(F32).sum(axis=0)
    return (
        first_low[None],
        sum_two.astype(BF16)[None],
        grad_first[None],
        grad_second[None],
        small[:, 0],
        small[:, 1],
        heavy[:, :width],
        heavy[:, width:],
        grad_w_out,
        small[:, 2],
        small[:, 3],
        grad_up,
        grad_down,
    )


def solution(mesh):
    return jax.shard_map(
        shards,
        mesh=mesh,
        in_specs=(
            P("ffn", "seq", None),
            P("ffn", "seq", None),
            P("ffn", None),
            P("ffn", "seq", None),
            P(),
            P(),
            P(),
            P(),
            P(),
            P(),
            P(),
            P(None, "ffn"),
            P(None, "ffn"),
            P("ffn", "seq", None),
            P("ffn", "seq", None),
        ),
        out_specs=(
            P("ffn", "seq", None),
            P("ffn", "seq", None),
            P("ffn", "seq", None),
            P("ffn", "seq", None),
            P(("seq", "ffn")),
            P(("seq", "ffn")),
            P(("seq", "ffn"), None),
            P(("seq", "ffn"), None),
            P(("seq", "ffn"), None),
            P(("seq", "ffn")),
            P(("seq", "ffn")),
            P("seq", "ffn"),
            P("seq", "ffn"),
        ),
        check_vma=False,
    )
```

```python
import jax
import jax.numpy as jnp
from jax import lax
from jax.experimental import pallas as pl
from jax.experimental.pallas import tpu as pltpu
from jax.sharding import PartitionSpec as P

HEADS = 8
DH = 128
ROUNDS = 4
SPAN = 64
EPS_NORM = 1e-05
EPS_KEY = 1e-06
SCALE = DH ** (-0.5)
EXTRA = 16
F32, BF16 = jnp.float32, jnp.bfloat16
VMEM_LIMIT = 60 * 2**20
ACROSS = (((1,), (1,)), ((), ()))
FLIP = (((0,), (0,)), ((), ()))


def vm(n):
    return [pl.BlockSpec(memory_space=pltpu.VMEM)] * n


def sd(shape, kind):
    return jax.ShapeDtypeStruct(shape, kind)


def params():
    return pltpu.CompilerParams(vmem_limit_bytes=VMEM_LIMIT)


def takes(us):
    return pl.CostEstimate(flops=0, transcendentals=0, bytes_accessed=int(us * 3.5e6))


def split3(x):
    a = x.astype(BF16)
    r = x - a.astype(F32)
    b = r.astype(BF16)
    c = (r - b.astype(F32)).astype(BF16)
    return a, b, c


def layer_rows(x, gain, offset):
    centred = x - jnp.mean(x, axis=1, keepdims=True)
    inverse = lax.rsqrt(jnp.mean(centred * centred, axis=1, keepdims=True) + EPS_NORM)
    return centred * inverse * gain + offset


def layer_back(x, grad, gain):
    centred = x - jnp.mean(x, axis=1, keepdims=True)
    inverse = lax.rsqrt(jnp.mean(centred * centred, axis=1, keepdims=True) + EPS_NORM)
    unit = centred * inverse
    grad_gain = jnp.sum(grad * unit, axis=0, keepdims=True)
    grad_offset = jnp.sum(grad, axis=0, keepdims=True)
    scaled = grad * gain
    inner = jnp.mean(scaled * unit, axis=1, keepdims=True)
    grad_x = inverse * (scaled - jnp.mean(scaled, axis=1, keepdims=True) - unit * inner)
    return grad_x, grad_gain, grad_offset


def split_by_core(turned, keep, give):
    core = lax.axis_index("seq") % 2
    for j in range(keep.shape[0]):
        keep[j] = turned[pl.ds(pl.multiple_of(j * 64 + core * 32, 32), 32), :]
        give[j] = turned[pl.ds(pl.multiple_of(j * 64 + (1 - core) * 32, 32), 32), :]


def project_kernel(x, gain, offset, w_qk, w_value, msg, normed_out, keep, give, turned):
    normed = layer_rows(x[...].astype(F32), gain[...], offset[...])
    low = normed.astype(BF16)
    normed_out[...] = low
    for h in range(HEADS):
        at = slice(h * DH, (h + 1) * DH)
        q = jnp.dot(low, w_qk[:, at], preferred_element_type=F32).astype(BF16)
        v = jnp.dot(low, w_value[:, at], preferred_element_type=F32).astype(BF16)
        for t in range(2):
            msg[h * 2 + t, :, :DH] = q
            msg[h * 2 + t, :, DH:] = v
    turned[...] = jnp.transpose(low.astype(F32)).astype(BF16)
    split_by_core(turned, keep, give)


def project(x, gain, offset, w_qk, w_value):
    rows, width = x.shape
    chips = 2 * HEADS
    return pl.pallas_call(
        project_kernel,
        out_shape=[
            sd((chips, rows, 2 * DH), BF16),
            sd((rows, width), BF16),
            sd((width // 64, 32, rows), BF16),
            sd((width // 64, 32, rows), BF16),
        ],
        in_specs=vm(5),
        out_specs=vm(4),
        scratch_shapes=[pltpu.VMEM((width, rows), BF16)],
        compiler_params=params(),
        name="project",
        cost_estimate=takes(7),
    )(x, gain, offset, w_qk, w_value)


BLOCK = 4 * SPAN


def shift_rows(order, base, pairs, gathers):
    for u in range(BLOCK):
        place = order[base + u]
        for src, dst in pairs:
            if gathers:
                dst[u : u + 1, :] = src[pl.ds(place, 1), :]
            else:
                dst[pl.ds(place, 1), :] = src[u : u + 1, :]


def by_core(array, keep, give):
    core = lax.axis_index("seq") % 2

    def narrow(j, c):
        for out, side in ((keep, core), (give, 1 - core)):
            at = pl.ds(pl.multiple_of((2 * j + side) * 256, 256), 256)
            out[j] = array[at, :].astype(BF16)
        return c

    lax.fori_loop(0, keep.shape[0], narrow, 0)


def attend_kernel(order, mine, other, bias, msg, q_out, keys, vals, probs, xq, xv, oq, ov, *slots):
    length = q_out.shape[0]
    blocks = length // BLOCK
    core = lax.axis_index("seq") % 2
    came, done = (slots[0:2], slots[2:4]), (slots[4:6], slots[6:8])

    def widen(j, c):
        for rows, side in ((mine, core), (other, 1 - core)):
            at = pl.ds(pl.multiple_of((2 * j + side) * 256, 256), 256)
            xq[at, :] = rows[j, :, :DH].astype(F32)
            xv[at, :] = rows[j, :, DH:].astype(F32)
        return c

    lax.fori_loop(0, length // 512, widen, 0)

    def gather(b, slot):
        shift_rows(order, b * BLOCK, list(zip((xq, xv), slot)), True)

    def scatter(b, slot):
        shift_rows(order, b * BLOCK, list(zip(slot, (oq, ov))), False)

    def ready(b, slot):
        q = slot[0][...]
        unit = q * lax.rsqrt(jnp.sum(q * q, axis=1, keepdims=True) + EPS_KEY)
        ahead = pl.ds(pl.multiple_of(b * BLOCK + SPAN, SPAN), BLOCK)
        keys[ahead, :] = unit.astype(BF16)
        vals[ahead, :] = slot[1][...].astype(BF16)
        return q.astype(BF16)

    gather(blocks - 1, came[1])
    ready(blocks - 1, came[1])
    keys[0:SPAN, :] = keys[length : length + SPAN, :]
    vals[0:SPAN, :] = vals[length : length + SPAN, :]
    gather(0, came[0])

    def compute(b, slot, out):
        base = pl.multiple_of(b * BLOCK, BLOCK)
        q = ready(b, slot)
        q_out[pl.ds(base, BLOCK), :] = q
        k = keys[pl.ds(base, BLOCK + SPAN), :]
        v = vals[pl.ds(base, BLOCK + SPAN), :]
        spans = range(BLOCK // SPAN)
        s = [
            lax.dot_general(
                q[u * SPAN : u * SPAN + SPAN], k[u * SPAN : u * SPAN + 2 * SPAN], ACROSS, preferred_element_type=F32
            )
            for u in spans
        ]
        s = jnp.concatenate(s, axis=0) * SCALE + bias[pl.ds(base, BLOCK), :].astype(F32)
        top = jnp.max(s, axis=1, keepdims=True)
        e = jnp.exp(s - top)
        total = jnp.sum(e, axis=1, keepdims=True)
        p = (e * (1.0 / total)).astype(BF16)
        probs[pl.ds(base, BLOCK), :] = p
        for u in spans:
            out[0][u * SPAN : u * SPAN + SPAN, :] = jnp.dot(
                p[u * SPAN : u * SPAN + SPAN], v[u * SPAN : u * SPAN + 2 * SPAN], preferred_element_type=F32
            )
        out[1][...] = jnp.broadcast_to(top + jnp.log(total), (BLOCK, DH))

    def step(i, c):
        b = 2 * i
        scatter(jnp.maximum(b - 1, 0), done[1])
        gather(b + 1, came[1])
        compute(b, came[0], done[0])
        scatter(b, done[0])
        gather(jnp.minimum(b + 2, blocks - 1), came[0])
        compute(b + 1, came[1], done[1])
        return c

    lax.fori_loop(0, blocks // 2, step, 0)
    scatter(blocks - 1, done[1])

    across = lax.broadcasted_iota(jnp.int32, (128, 128), 0)
    eye = across == lax.broadcasted_iota(jnp.int32, (128, 128), 1)

    def send(b, c):
        at = pl.ds(b * 256, 256)
        msg[b, 0:256, :] = oq[at, :].astype(BF16)
        lo = jnp.sum(jnp.where(eye, ov[pl.ds(b * 256, 128), :], 0.0), axis=0, keepdims=True)
        hi = jnp.sum(jnp.where(eye, ov[pl.ds(b * 256 + 128, 128), :], 0.0), axis=0, keepdims=True)
        parts = split3(lo) + split3(hi)
        tail = [p.astype(F32) for p in parts] + [jnp.zeros((EXTRA - 6, 128), F32)]
        msg[b, 256:, :] = jnp.concatenate(tail, axis=0).astype(BF16)
        return c

    lax.fori_loop(0, length // 256, send, 0)


def attend(order, mine, other, bias):
    length = order.shape[0]
    return pl.pallas_call(
        attend_kernel,
        out_shape=[
            sd((length // 256, 256 + EXTRA, DH), BF16),
            sd((length, DH), BF16),
            sd((length + SPAN, DH), BF16),
            sd((length + SPAN, DH), BF16),
            sd((length, DH), BF16),
        ],
        in_specs=[pl.BlockSpec(memory_space=pltpu.SMEM)] + vm(3),
        out_specs=vm(5),
        scratch_shapes=[pltpu.VMEM((length, DH), F32)] * 4 + [pltpu.VMEM((BLOCK, DH), F32)] * 8,
        compiler_params=params(),
        name="attend",
        cost_estimate=takes(37),
    )(order, mine, other, bias)


def back_value_kernel(order, msg, vals, probs, keep, give, gd_out, xg, xd, ov, saved, carry, *slots):
    length = probs.shape[0]
    blocks = length // BLOCK
    came, done = (slots[0:2], slots[2:4]), (slots[4:5], slots[5:6])

    def widen(b, c):
        xg[pl.ds(b * 256, 256), :] = msg[b, 0:256, :].astype(F32)
        t = msg[b, 256:, :].astype(F32)
        lo = t[0:1] + t[1:2] + t[2:3]
        hi = t[3:4] + t[4:5] + t[5:6]
        xd[pl.ds(b * 256, 128), :] = jnp.transpose(jnp.broadcast_to(lo, (128, 128)))
        xd[pl.ds(b * 256 + 128, 128), :] = jnp.transpose(jnp.broadcast_to(hi, (128, 128)))
        return c

    lax.fori_loop(0, length // 256, widen, 0)

    def gather(b, slot):
        shift_rows(order, b * BLOCK, list(zip((xg, xd), slot)), True)

    def scatter(b, slot):
        base = jnp.where(b == 0, length, b * BLOCK) - SPAN
        for u in range(BLOCK):
            if u == SPAN:
                base = b * BLOCK - SPAN
            ov[pl.ds(order[base + u], 1), :] = slot[0][u : u + 1, :]

    gather(0, came[0])
    carry[...] = jnp.zeros(carry.shape, F32)

    def compute(b, slot, out):
        base = pl.multiple_of(b * BLOCK, BLOCK)
        g = slot[0][...].astype(BF16)
        p = probs[pl.ds(base, BLOCK), :]
        v = vals[pl.ds(base, BLOCK + SPAN), :]
        spans = range(BLOCK // SPAN)
        cut = lambda a, u: a[u * SPAN : u * SPAN + SPAN]
        gp = [
            lax.dot_general(cut(g, u), v[u * SPAN : u * SPAN + 2 * SPAN], ACROSS, preferred_element_type=F32)
            for u in spans
        ]
        gs = p.astype(F32) * (jnp.concatenate(gp, axis=0) - slot[1][...])
        gd_out[pl.ds(base, BLOCK), :] = (gs * SCALE).astype(BF16)
        wide = [lax.dot_general(cut(p, u), cut(g, u), FLIP, preferred_element_type=F32) for u in spans]

        @pl.when(b == 0)
        def _():
            saved[...] = wide[0][:SPAN]

        out[0][0:SPAN, :] = carry[...] + wide[0][:SPAN]
        for u in spans[1:]:
            out[0][u * SPAN : u * SPAN + SPAN, :] = wide[u - 1][SPAN:] + wide[u][:SPAN]
        carry[...] = wide[-1][SPAN:]

    def step(i, c):
        b = 2 * i
        scatter(jnp.maximum(b - 1, 0), done[1])
        gather(b + 1, came[1])
        compute(b, came[0], done[0])
        scatter(b, done[0])
        gather(jnp.minimum(b + 2, blocks - 1), came[0])
        compute(b + 1, came[1], done[1])
        return c

    lax.fori_loop(0, blocks // 2, step, 0)
    scatter(blocks - 1, done[1])
    carry[...] += saved[...]
    for u in range(SPAN):
        ov[pl.ds(order[length - SPAN + u], 1), :] = carry[u : u + 1, :]
    by_core(ov, keep, give)


def back_value(order, msg, vals, probs):
    length = probs.shape[0]
    half = length // 512
    return pl.pallas_call(
        back_value_kernel,
        out_shape=[sd((half, 256, DH), BF16)] * 2 + [sd((length, DH), BF16)],
        in_specs=[pl.BlockSpec(memory_space=pltpu.SMEM)] + vm(3),
        out_specs=vm(3),
        scratch_shapes=[pltpu.VMEM((length, DH), F32)] * 3
        + [pltpu.VMEM((SPAN, DH), F32)] * 2
        + [pltpu.VMEM((BLOCK, DH), F32)] * 6,
        compiler_params=params(),
        name="back_value",
        cost_estimate=takes(26),
    )(order, msg, vals, probs)


def back_query_kernel(order, gd, q_in, keys, keep, give, oq, saved, carry, waiting, *done):
    length = q_in.shape[0]
    blocks = length // BLOCK

    def scatter(b, slot):
        base = jnp.where(b == 0, length, b * BLOCK) - SPAN
        for u in range(BLOCK):
            if u == SPAN:
                base = b * BLOCK - SPAN
            oq[pl.ds(order[base + u], 1), :] = slot[u : u + 1, :]

    carry[...] = jnp.zeros(carry.shape, F32)
    waiting[...] = jnp.zeros(waiting.shape, F32)

    def whole(direct, unit_grad, q):
        q = q.astype(F32)
        r = lax.rsqrt(jnp.sum(q * q, axis=1, keepdims=True) + EPS_KEY)
        along = jnp.sum(q * unit_grad, axis=1, keepdims=True)
        return direct + r * unit_grad - q * (r * r * r * along)

    def compute(b, out):
        base = pl.multiple_of(b * BLOCK, BLOCK)
        d = gd[pl.ds(base, BLOCK), :]
        q = q_in[pl.ds(base, BLOCK), :]
        k = keys[pl.ds(base, BLOCK + SPAN), :]
        back = q_in[pl.ds(pl.multiple_of(jnp.maximum(base - SPAN, 0), SPAN), SPAN), :]
        spans = range(BLOCK // SPAN)
        cut = lambda a, u: a[u * SPAN : u * SPAN + SPAN]
        direct = [jnp.dot(cut(d, u), k[u * SPAN : u * SPAN + 2 * SPAN], preferred_element_type=F32) for u in spans]
        wide = [lax.dot_general(cut(d, u), cut(q, u), FLIP, preferred_element_type=F32) for u in spans]

        @pl.when(b == 0)
        def _():
            saved[...] = wide[0][:SPAN]

        folded = [carry[...] + wide[0][:SPAN]] + [wide[u - 1][SPAN:] + wide[u][:SPAN] for u in spans[1:]]
        straight = [waiting[...]] + direct[:-1]
        behind = jnp.concatenate([back, q[: BLOCK - SPAN]], axis=0)
        out[...] = whole(jnp.concatenate(straight, axis=0), jnp.concatenate(folded, axis=0), behind)
        carry[...] = wide[-1][SPAN:]
        waiting[...] = direct[-1]

    def step(i, c):
        b = 2 * i
        scatter(jnp.maximum(b - 1, 0), done[1])
        compute(b, done[0])
        scatter(b, done[0])
        compute(b + 1, done[1])
        return c

    lax.fori_loop(0, blocks // 2, step, 0)
    scatter(blocks - 1, done[1])
    waiting[...] = whole(waiting[...], carry[...] + saved[...], q_in[length - SPAN : length, :])
    for u in range(SPAN):
        oq[pl.ds(order[length - SPAN + u], 1), :] = waiting[u : u + 1, :]
    by_core(oq, keep, give)


def back_query(order, gd, q_in, keys):
    length = q_in.shape[0]
    half = length // 512
    return pl.pallas_call(
        back_query_kernel,
        out_shape=[sd((half, 256, DH), BF16)] * 2,
        in_specs=[pl.BlockSpec(memory_space=pltpu.SMEM)] + vm(3),
        out_specs=vm(2),
        scratch_shapes=[pltpu.VMEM((length, DH), F32)]
        + [pltpu.VMEM((SPAN, DH), F32)] * 3
        + [pltpu.VMEM((BLOCK, DH), F32)] * 2,
        compiler_params=params(),
        name="back_query",
        cost_estimate=takes(17),
    )(order, gd, q_in, keys)


def prepare(bucket_row, ends):
    length = bucket_row.shape[0]
    places = jnp.arange(length, dtype=jnp.int32)
    _, order = lax.sort((bucket_row * length + places, places), num_keys=1)
    pos = order.reshape(-1, SPAN)
    start = jnp.max(jnp.where(ends <= pos[..., None], ends, 0), axis=-1)
    window = jnp.concatenate([jnp.roll(pos, 1, 0), pos], axis=1)
    k, q = window[:, None, :], pos[:, :, None]
    bias = jnp.where((k >= start[:, :, None]) & (k <= q), jnp.where(k == q, -1000.0, 0.0), -1e9)
    return order, bias.astype(BF16).reshape(length, 2 * SPAN)


def combine_kernel(msg, x, w_out, gain, offset, mix, low_mix, first_out, first_low, normed, weights):
    rows = x.shape[0]
    for half in range(2):
        logs = []
        for r in range(ROUNDS):
            lines = []
            for h in range(HEADS):
                tail = msg[h * ROUNDS + r, rows : rows + EXTRA, :].astype(F32)
                k = half * 3
                lines.append(tail[k : k + 1] + tail[k + 1 : k + 2] + tail[k + 2 : k + 3])
            logs.append(jnp.concatenate(lines, axis=0))
        top = jnp.maximum(jnp.maximum(logs[0], logs[1]), jnp.maximum(logs[2], logs[3]))
        powers = [jnp.exp(v - top) for v in logs]
        inverse = 1.0 / (powers[0] + powers[1] + powers[2] + powers[3])
        lines = [v * inverse for v in powers]
        lines.append(jnp.zeros((128 - HEADS * ROUNDS, 128), F32))
        weights[half * 128 : half * 128 + 128, :] = jnp.transpose(jnp.concatenate(lines, axis=0))
    for h in range(HEADS):
        total = jnp.zeros((rows, DH), F32)
        for r in range(ROUNDS):
            j = r * HEADS + h
            total = total + weights[:, j : j + 1] * msg[h * ROUNDS + r, 0:rows, :].astype(F32)
        mix[:, h * DH : (h + 1) * DH] = total
        low_mix[:, h * DH : (h + 1) * DH] = total.astype(BF16)
    first = x[...].astype(F32) + jnp.dot(low_mix[...], w_out[...], preferred_element_type=F32)
    first_out[...] = first
    first_low[...] = first.astype(BF16)
    normed[...] = layer_rows(first, gain[...], offset[...]).astype(BF16)


def combine(msg, x, w_out, gain, offset):
    rows, width = x.shape
    return pl.pallas_call(
        combine_kernel,
        out_shape=[
            sd((rows, width), F32),
            sd((rows, width), BF16),
            sd((rows, width), F32),
            sd((rows, width), BF16),
            sd((rows, width), BF16),
            sd((rows, 128), F32),
        ],
        in_specs=vm(5),
        out_specs=vm(6),
        compiler_params=params(),
        name="combine",
        cost_estimate=takes(6),
    )(msg, x, w_out, gain, offset)


def gelu_both(act, grad):
    share = 0.5 + 0.5 * lax.erf(act * 0.7071067811865476)
    slope = share + act * (jnp.exp(act * act * -0.5) * 0.3989422804014327)
    return (act * share).astype(BF16), (grad * slope).astype(BF16)


def middle_kernel(*refs):
    (mix, low_mix, first, normed, weights, x_two, g_one, g_two, w_out, gain, up0, down0) = refs[:12]
    far = refs[12:24]
    (two_low, grad_first, sent, grad_gain, grad_offset, keep_mix, give_mix, low_first, hid0, pre0) = refs[24:34]
    (turned, up, down, hid, pre, summed, sems) = refs[34:]
    rows = x_two.shape[0]
    core = lax.axis_index("seq") % 2

    def copies(flip):
        out = [pltpu.make_async_copy(up0, up.at[0], sems.at[0]), pltpu.make_async_copy(down0, down.at[0], sems.at[1])]
        for i in range(6):
            a, b = (far[i + 6], far[i]) if flip else (far[i], far[i + 6])
            at = pl.ds(i % 2 * 512, 512)
            out.append(pltpu.make_async_copy(a, up.at[1 + i // 2, at], sems.at[2 + 2 * i]))
            out.append(pltpu.make_async_copy(b, down.at[1 + i // 2, at], sems.at[3 + 2 * i]))
        return out

    @pl.when(core == 0)
    def _():
        for c in copies(False):
            c.start()

    @pl.when(core == 1)
    def _():
        for c in copies(True):
            c.start()

    for c in copies(False):
        c.wait()

    def hidden_part(i, c):
        k = i // 4
        at = pl.ds(pl.multiple_of((i % 4) * 256, 256), 256)
        act = jnp.dot(normed[...], up[k, :, at], preferred_element_type=F32)
        grad = jnp.dot(g_two[...], down[k, :, at], preferred_element_type=F32)
        hid[k, :, at], pre[k, :, at] = gelu_both(act, grad)
        return c

    lax.fori_loop(0, 16, hidden_part, 0)
    hid0[...] = hid[0]
    pre0[...] = pre[0]
    summed[...] = jnp.zeros(summed.shape, F32)

    def up_back(k, c):
        summed[...] += lax.dot_general(pre[k], up[k], ACROSS, preferred_element_type=F32)
        return c

    lax.fori_loop(0, 4, up_back, 0)
    grad_x, gg, go = layer_back(first[...], summed[...], gain[...])
    grad_gain[...] = gg
    grad_offset[...] = go
    grad_x = grad_x + g_one[...].astype(F32)
    grad_first[...] = grad_x
    low_first[...] = grad_x.astype(BF16)
    lane = lax.broadcasted_iota(jnp.int32, (rows, 128), 1)
    inner = jnp.zeros((rows, 128), F32)
    for h in range(HEADS):
        at = slice(h * DH, (h + 1) * DH)
        grad_mix = lax.dot_general(low_first[...], w_out[at, :], ACROSS, preferred_element_type=F32)
        dots = jnp.sum(grad_mix * mix[:, at], axis=1, keepdims=True)
        inner = jnp.where(lane % HEADS == h, dots, inner)
        for r in range(ROUNDS):
            j = r * HEADS + h
            sent[h * ROUNDS + r, 0:rows, :] = (weights[:, j : j + 1] * grad_mix).astype(BF16)
    inner = inner * weights[...]
    low_lines = [p.astype(F32) for p in split3(jnp.transpose(inner[0:128]))]
    high_lines = [p.astype(F32) for p in split3(jnp.transpose(inner[128:256]))]
    blank = jnp.zeros((EXTRA - 6, 128), F32)
    for h in range(HEADS):
        for r in range(ROUNDS):
            j = r * HEADS + h
            tail = [p[j : j + 1] for p in low_lines + high_lines] + [blank]
            sent[h * ROUNDS + r, rows : rows + EXTRA, :] = jnp.concatenate(tail, axis=0).astype(BF16)

    summed[...] = x_two[...].astype(F32)

    def down_out(k, c):
        summed[...] += lax.dot_general(hid[k], down[k], ACROSS, preferred_element_type=F32)
        return c

    lax.fori_loop(0, 4, down_out, 0)
    two_low[...] = summed[...].astype(BF16)
    turned[...] = jnp.transpose(low_mix[...].astype(F32)).astype(BF16)
    split_by_core(turned, keep_mix, give_mix)


def middle(mix, low_mix, first, normed, weights, x_two, g_one, g_two, w_out, gain, up0, down0, mine, other):
    rows, width = x_two.shape
    anywhere = [pl.BlockSpec(memory_space=pl.ANY)] * 14
    return pl.pallas_call(
        middle_kernel,
        out_shape=[
            sd((rows, width), BF16),
            sd((rows, width), F32),
            sd((HEADS * ROUNDS, rows + EXTRA, DH), BF16),
            sd((1, width), F32),
            sd((1, width), F32),
            sd((width // 64, 32, rows), BF16),
            sd((width // 64, 32, rows), BF16),
            sd((rows, width), BF16),
            sd((rows, 1024), BF16),
            sd((rows, 1024), BF16),
        ],
        in_specs=vm(10) + anywhere,
        out_specs=vm(10),
        scratch_shapes=[
            pltpu.VMEM((width, rows), BF16),
            pltpu.VMEM((4, width, 1024), BF16),
            pltpu.VMEM((4, width, 1024), BF16),
            pltpu.VMEM((4, rows, 1024), BF16),
            pltpu.VMEM((4, rows, 1024), BF16),
            pltpu.VMEM((rows, width), F32),
            pltpu.SemaphoreType.DMA((14,)),
        ],
        compiler_params=params(),
        name="middle",
        cost_estimate=takes(25),
    )(mix, low_mix, first, normed, weights, x_two, g_one, g_two, w_out, gain, up0, down0, *mine, *other)


def feed_kernel(normed, grads, hid0, pre0, n1, n2, n3, g1, g2, g3, up, down, keep, give, hid, pre, turned, total):
    core = lax.axis_index("seq") % 2
    hid[0] = hid0[...]
    pre[0] = pre0[...]
    for k, (n, g) in enumerate(((n1, g1), (n2, g2), (n3, g3)), start=1):

        def hidden_part(i, c):
            at = pl.ds(pl.multiple_of(i * 256, 256), 256)
            act = jnp.dot(n[...], up[:, at], preferred_element_type=F32)
            grad = jnp.dot(g[...], down[:, at], preferred_element_type=F32)
            hid[k, :, at], pre[k, :, at] = gelu_both(act, grad)
            return c

        lax.fori_loop(0, 4, hidden_part, 0)
    for first, lefts, rights in ((0, (normed, n1, n2, n3), pre), (1024, (grads, g1, g2, g3), hid)):
        left = jnp.concatenate([x[...] for x in lefts], axis=0)
        turned[...] = jnp.transpose(left.astype(F32)).astype(BF16)

        def piece(i, c):
            left = turned[pl.ds(pl.multiple_of(i * 256, 256), 256), :]
            total[...] = jnp.dot(left, rights[...].reshape(4 * n1.shape[0], 1024), preferred_element_type=F32)
            for out, side in ((keep, core), (give, 1 - core)):
                for j in range(4):
                    rows = total[pl.ds(pl.multiple_of(j * 64 + side * 32, 32), 32), :]
                    out[i * 4 + j, :, first : first + 1024] = rows.astype(BF16)
            return c

        lax.fori_loop(0, keep.shape[0] // 4, piece, 0)


def feed(normed, grads, hid0, pre0, normed_far, grads_far, up, down):
    rows, width = normed.shape
    return pl.pallas_call(
        feed_kernel,
        out_shape=[sd((width // 64, 32, 2048), BF16)] * 2,
        in_specs=vm(12),
        out_specs=vm(2),
        scratch_shapes=[pltpu.VMEM((4, rows, 1024), BF16)] * 2
        + [pltpu.VMEM((width, 4 * rows), BF16), pltpu.VMEM((256, 1024), F32)],
        compiler_params=params(),
        name="feed",
        cost_estimate=takes(18),
    )(normed, grads, hid0, pre0, *normed_far, *grads_far, up, down)


def sum_rounds_kernel(back, out):
    for h in range(HEADS):
        total = back[2 * h].astype(F32) + back[2 * h + 1].astype(F32)
        for half in range(2):
            at = slice(half * HEADS * DH + h * DH, half * HEADS * DH + (h + 1) * DH)
            out[:, at] = total[:, half * DH : (half + 1) * DH].astype(BF16)


def sum_rounds(back):
    rows = back.shape[1]
    return pl.pallas_call(
        sum_rounds_kernel,
        out_shape=sd((rows, 2 * HEADS * DH), BF16),
        in_specs=vm(1),
        out_specs=pl.BlockSpec(memory_space=pltpu.VMEM),
        compiler_params=params(),
        name="sum_rounds",
        cost_estimate=takes(3),
    )(back)


def finish_kernel(grads, x, gain, w_qk, w_value, grad_two, gain_two, offset_two, grad_second, small, near, far):
    width = x.shape[1]
    grad_normed = lax.dot_general(grads[:, :width], w_qk[...], ACROSS, preferred_element_type=F32)
    grad_normed = grad_normed + lax.dot_general(grads[:, width:], w_value[...], ACROSS, preferred_element_type=F32)
    grad_x, gg, go = layer_back(x[...].astype(F32), grad_normed, gain[...])
    grad_second[...] = grad_x + grad_two[...].astype(F32)
    lines = []
    for line in (gg, go, gain_two[...], offset_two[...]):
        high = line.astype(BF16).astype(F32)
        lines += [high, line - high]
    blank = jnp.zeros((8, width), F32)
    rest = jnp.zeros((112, width), F32)
    near[...] = jnp.transpose(jnp.concatenate(lines + [blank, rest], axis=0))
    far[...] = jnp.transpose(jnp.concatenate([blank] + lines + [rest], axis=0))
    core = lax.axis_index("seq") % 2
    for j in range(small.shape[0]):
        a = near[pl.ds(pl.multiple_of(j * 64 + core * 32, 32), 32), :]
        b = far[pl.ds(pl.multiple_of(j * 64 + (1 - core) * 32, 32), 32), :]
        small[j] = (a + b).astype(BF16)


def finish(grads, x, gain, w_qk, w_value, grad_two, gain_two, offset_two):
    rows, width = x.shape
    return pl.pallas_call(
        finish_kernel,
        out_shape=[sd((rows, width), F32), sd((width // 64, 32, 128), BF16)],
        in_specs=vm(8),
        out_specs=vm(2),
        scratch_shapes=[pltpu.VMEM((width, 128), F32)] * 2,
        compiler_params=params(),
        name="finish",
        cost_estimate=takes(5),
    )(grads, x, gain, w_qk, w_value, grad_two, gain_two, offset_two)


def pair_kernel(left, left_other, right, right_other, *rest):
    blocks, lines, rows = left.shape
    out, width = rest[-1], right.shape[1]
    total = jnp.dot(left[...].reshape(blocks * lines, rows), right[...], preferred_element_type=F32)
    total = total + jnp.dot(left_other[...].reshape(blocks * lines, rows), right_other[...], preferred_element_type=F32)
    out[:, :, :width] = total.astype(BF16).reshape(blocks, lines, width)
    if len(rest) == 2:
        out[:, :, width:] = rest[0][...]


def pair(left, left_other, right, right_other, *extra):
    blocks, lines, rows = left.shape
    width = right.shape[1] + sum(e.shape[2] for e in extra)
    return pl.pallas_call(
        pair_kernel,
        out_shape=sd((blocks, lines, width), BF16),
        in_specs=vm(4 + len(extra)),
        out_specs=pl.BlockSpec(memory_space=pltpu.VMEM),
        compiler_params=params(),
        name="pair",
        cost_estimate=takes(3),
    )(left, left_other, right, right_other, *extra)


def swap_seq(array):
    return lax.all_to_all(array, "seq", split_axis=0, concat_axis=0, tiled=True)


def same_core():
    count = lax.axis_size("seq")
    return [list(range(c, count, 2)) for c in range(2)]


def swap_chips(array):
    return lax.all_to_all(
        array, "seq", split_axis=0, concat_axis=0, tiled=True, axis_index_groups=same_core()
    )


def flip_bit(array, axis, bit):
    return lax.ppermute(array, axis, [(i, i ^ bit) for i in range(lax.axis_size(axis))])


def swap_cores(array):
    return flip_bit(array, "seq", 1)


def from_ahead(array, step):
    count = lax.axis_size("ffn")
    return lax.ppermute(array, "ffn", [((i + step) % count, i) for i in range(count)])


def tied(array, *others):
    return lax.optimization_barrier((array, others))[0]


def add_low(a, b):
    return (a.astype(F32) + b.astype(F32)).astype(BF16)


def shards(
    stream_one,
    stream_two,
    doc_lengths,
    bucket_ids,
    norm1_gain,
    norm1_bias,
    w_qk,
    w_value,
    w_out,
    norm2_gain,
    norm2_bias,
    w_up,
    w_down,
    grad_out_one,
    grad_out_two,
):
    rows, width = stream_one.shape[1:]
    seq, ffn = lax.axis_index("seq"), lax.axis_index("ffn")
    core = seq % 2
    gain_one, bias_one = norm1_gain.reshape(1, -1), norm1_bias.reshape(1, -1)
    gain_two, bias_two = norm2_gain.reshape(1, -1), norm2_bias.reshape(1, -1)

    msg, normed_one, keep_rows, give_rows = project(stream_two[0], gain_one, bias_one, w_qk, w_value)
    received = swap_chips(msg)
    order, bias = prepare(bucket_ids[0, 0], jnp.cumsum(doc_lengths[0]))
    top, low = [jnp.where(core == 0, w_up[at], w_down[at]) for at in (slice(0, 512), slice(512, 1024))]
    top1, low3 = from_ahead(top, 1), from_ahead(low, 3)
    received, order, bias, top, low, top1, low3 = lax.optimization_barrier(
        (received, order, bias, top, low, top1, low3)
    )
    low1, top3 = from_ahead(low, 1), from_ahead(top, 3)
    grads1, grads3 = from_ahead(grad_out_two[0], 1), from_ahead(grad_out_two[0], 3)
    other_rows = swap_cores(give_rows)
    top1_other, low3_other = swap_cores(top1), swap_cores(low3)
    sent, queries, keys, vals, probs = attend(order, received, swap_cores(received), bias)
    (sent, top1, low3, low1, top3, grads1, grads3, grad_rows, top1_other, low3_other) = lax.optimization_barrier(
        (sent, top1, low3, low1, top3, grads1, grads3, grad_out_two[0], top1_other, low3_other)
    )
    per_round = swap_seq(sent)
    top2, low2 = from_ahead(top1, 1), from_ahead(low3, 3)
    grads2 = from_ahead(grad_rows, 2)
    low1_other, top3_other = swap_cores(low1), swap_cores(top3)
    per_round, top2, low2, low1_other, top3_other, grads2 = lax.optimization_barrier(
        (per_round, top2, low2, low1_other, top3_other, grads2)
    )
    mine = [top1, low1, top2, low2, top3, low3]
    other = [top1_other, low1_other, swap_cores(top2), swap_cores(low2), top3_other, low3_other]
    mix, low_mix, first, one_low, normed_two, weights = combine(per_round, stream_one[0], w_out, gain_two, bias_two)
    normed_far = [from_ahead(normed_two, k) for k in (1, 2, 3)]
    two_low, grad_first, msg, grad_gain_two, grad_bias_two, keep_mix, give_mix, low_first, hid0, pre0 = middle(
        mix,
        low_mix,
        first,
        normed_two,
        weights,
        stream_two[0],
        grad_out_one[0],
        grad_rows,
        w_out,
        gain_two,
        w_up,
        w_down,
        mine,
        other,
    )
    far = swap_seq(msg)
    keep_feed, give_feed = feed(normed_two, grad_rows, hid0, pre0, normed_far, [grads1, grads2, grads3], w_up, w_down)
    part_out = pair(keep_mix, swap_cores(give_mix), low_first, swap_cores(low_first))
    part_feed = add_low(keep_feed, swap_cores(give_feed))
    far, part_feed, part_out = lax.optimization_barrier((far, part_feed, part_out))
    near_feed = swap_chips(jnp.concatenate([part_feed, part_out], axis=2))

    keep_v, give_v, grad_dots = back_value(order, far, vals, probs)
    keep_q, give_q = back_query(order, grad_dots, queries, keys)
    came_v, came_q = swap_cores(give_v), swap_cores(give_q)
    back = swap_chips(jnp.concatenate([add_low(keep_q, came_q), add_low(keep_v, came_v)], axis=2))
    grads = sum_rounds(back)
    grads_other = swap_cores(grads)
    near_feed = near_feed.astype(F32).sum(axis=0)
    grad_second, small = finish(
        grads, stream_two[0], gain_one, w_qk, w_value, grad_out_two[0], grad_gain_two, grad_bias_two
    )
    part = pair(keep_rows, other_rows, grads, grads_other, small)
    near = swap_chips(part).astype(F32).sum(axis=0)
    near = jnp.concatenate([near, near_feed[:, 2048:]], axis=1).reshape(4, 8, -1)
    whole = lax.dynamic_index_in_dim(near, ffn, 0, keepdims=False)
    for k in (1, 2, 3):
        whole = whole + from_ahead(lax.dynamic_index_in_dim(near, (ffn + 4 - k) % 4, 0, keepdims=False), k)
    small = whole[:, 2 * width : 2 * width + 128]
    lines = small[:, :8] + swap_cores(small)[:, 8:16]
    lines = lines[:, 0::2] + lines[:, 1::2]
    return (
        one_low[None],
        two_low[None],
        grad_first[None],
        grad_second[None],
        lines[:, 0],
        lines[:, 1],
        whole[:, :width],
        whole[:, width : 2 * width],
        whole[:, 2 * width + 128 :],
        lines[:, 2],
        lines[:, 3],
        near_feed[:, :1024],
        near_feed[:, 1024:2048],
    )


def solution(mesh):
    return jax.shard_map(
        shards,
        mesh=mesh,
        in_specs=(
            P("ffn", "seq", None),
            P("ffn", "seq", None),
            P("ffn", None),
            P("ffn", "seq", None),
            P(),
            P(),
            P(),
            P(),
            P(),
            P(),
            P(),
            P(None, "ffn"),
            P(None, "ffn"),
            P("ffn", "seq", None),
            P("ffn", "seq", None),
        ),
        out_specs=(
            P("ffn", "seq", None),
            P("ffn", "seq", None),
            P("ffn", "seq", None),
            P("ffn", "seq", None),
            P(("seq", "ffn")),
            P(("seq", "ffn")),
            P(("seq", "ffn"), None),
            P(("seq", "ffn"), None),
            P(("seq", "ffn"), None),
            P(("seq", "ffn")),
            P(("seq", "ffn")),
            P("seq", "ffn"),
            P("seq", "ffn"),
        ),
        check_vma=False,
    )
```

```python
import jax
import jax.numpy as jnp
from jax import lax
from jax.experimental import pallas as pl
from jax.experimental.pallas import tpu as pltpu
from jax.sharding import PartitionSpec as P

HEADS = 8
DH = 128
ROUNDS = 4
SPAN = 64
EPS_NORM = 1e-05
EPS_KEY = 1e-06
SCALE = DH ** (-0.5)
EXTRA = 16
F32, BF16 = jnp.float32, jnp.bfloat16
VMEM_LIMIT = 60 * 2**20
ACROSS = (((1,), (1,)), ((), ()))
FLIP = (((0,), (0,)), ((), ()))


def vm(n):
    return [pl.BlockSpec(memory_space=pltpu.VMEM)] * n


def sd(shape, kind):
    return jax.ShapeDtypeStruct(shape, kind)


def params():
    return pltpu.CompilerParams(vmem_limit_bytes=VMEM_LIMIT)


def takes(us):
    return pl.CostEstimate(flops=0, transcendentals=0, bytes_accessed=int(us * 3.5e6))


def split3(x):
    a = x.astype(BF16)
    r = x - a.astype(F32)
    b = r.astype(BF16)
    c = (r - b.astype(F32)).astype(BF16)
    return a, b, c


def layer_rows(x, gain, offset):
    centred = x - jnp.mean(x, axis=1, keepdims=True)
    inverse = lax.rsqrt(jnp.mean(centred * centred, axis=1, keepdims=True) + EPS_NORM)
    return centred * inverse * gain + offset


def layer_back(x, grad, gain):
    centred = x - jnp.mean(x, axis=1, keepdims=True)
    inverse = lax.rsqrt(jnp.mean(centred * centred, axis=1, keepdims=True) + EPS_NORM)
    unit = centred * inverse
    grad_gain = jnp.sum(grad * unit, axis=0, keepdims=True)
    grad_offset = jnp.sum(grad, axis=0, keepdims=True)
    scaled = grad * gain
    inner = jnp.mean(scaled * unit, axis=1, keepdims=True)
    grad_x = inverse * (scaled - jnp.mean(scaled, axis=1, keepdims=True) - unit * inner)
    return grad_x, grad_gain, grad_offset


def split_by_core(turned, keep, give):
    core = lax.axis_index("seq") % 2
    for j in range(keep.shape[0]):
        keep[j] = turned[pl.ds(pl.multiple_of(j * 64 + core * 32, 32), 32), :]
        give[j] = turned[pl.ds(pl.multiple_of(j * 64 + (1 - core) * 32, 32), 32), :]


def project_kernel(x, gain, offset, w_qk, w_value, msg, normed_out, keep, give, turned):
    normed = layer_rows(x[...].astype(F32), gain[...], offset[...])
    low = normed.astype(BF16)
    normed_out[...] = low
    for h in range(HEADS):
        at = slice(h * DH, (h + 1) * DH)
        q = jnp.dot(low, w_qk[:, at], preferred_element_type=F32).astype(BF16)
        v = jnp.dot(low, w_value[:, at], preferred_element_type=F32).astype(BF16)
        for t in range(2):
            msg[h * 2 + t, :, :DH] = q
            msg[h * 2 + t, :, DH:] = v
    turned[...] = jnp.transpose(low.astype(F32)).astype(BF16)
    split_by_core(turned, keep, give)


def project(x, gain, offset, w_qk, w_value):
    rows, width = x.shape
    chips = 2 * HEADS
    return pl.pallas_call(
        project_kernel,
        out_shape=[
            sd((chips, rows, 2 * DH), BF16),
            sd((rows, width), BF16),
            sd((width // 64, 32, rows), BF16),
            sd((width // 64, 32, rows), BF16),
        ],
        in_specs=vm(5),
        out_specs=vm(4),
        scratch_shapes=[pltpu.VMEM((width, rows), BF16)],
        compiler_params=params(),
        name="project",
        cost_estimate=takes(7),
    )(x, gain, offset, w_qk, w_value)


BLOCK = 4 * SPAN


def shift_rows(order, base, pairs, gathers):
    for u in range(BLOCK):
        place = order[base + u]
        for src, dst in pairs:
            if gathers:
                dst[u : u + 1, :] = src[pl.ds(place, 1), :]
            else:
                dst[pl.ds(place, 1), :] = src[u : u + 1, :]


def by_core(array, keep, give):
    core = lax.axis_index("seq") % 2

    def narrow(j, c):
        for out, side in ((keep, core), (give, 1 - core)):
            at = pl.ds(pl.multiple_of((2 * j + side) * 256, 256), 256)
            out[j] = array[at, :].astype(BF16)
        return c

    lax.fori_loop(0, keep.shape[0], narrow, 0)


def attend_kernel(order, mine, other, bias, msg, q_out, keys, vals, probs, xq, xv, oq, ov, *slots):
    length = q_out.shape[0]
    blocks = length // BLOCK
    core = lax.axis_index("seq") % 2
    came, done = (slots[0:2], slots[2:4]), (slots[4:6], slots[6:8])

    def widen(j, c):
        for rows, side in ((mine, core), (other, 1 - core)):
            at = pl.ds(pl.multiple_of((2 * j + side) * 256, 256), 256)
            xq[at, :] = rows[j, :, :DH].astype(F32)
            xv[at, :] = rows[j, :, DH:].astype(F32)
        return c

    lax.fori_loop(0, length // 512, widen, 0)

    def gather(b, slot):
        shift_rows(order, b * BLOCK, list(zip((xq, xv), slot)), True)

    def scatter(b, slot):
        shift_rows(order, b * BLOCK, list(zip(slot, (oq, ov))), False)

    def ready(b, slot):
        q = slot[0][...]
        unit = q * lax.rsqrt(jnp.sum(q * q, axis=1, keepdims=True) + EPS_KEY)
        ahead = pl.ds(pl.multiple_of(b * BLOCK + SPAN, SPAN), BLOCK)
        keys[ahead, :] = unit.astype(BF16)
        vals[ahead, :] = slot[1][...].astype(BF16)
        return q.astype(BF16)

    gather(blocks - 1, came[1])
    ready(blocks - 1, came[1])
    keys[0:SPAN, :] = keys[length : length + SPAN, :]
    vals[0:SPAN, :] = vals[length : length + SPAN, :]
    gather(0, came[0])

    def compute(b, slot, out):
        base = pl.multiple_of(b * BLOCK, BLOCK)
        q = ready(b, slot)
        q_out[pl.ds(base, BLOCK), :] = q
        k = keys[pl.ds(base, BLOCK + SPAN), :]
        v = vals[pl.ds(base, BLOCK + SPAN), :]
        spans = range(BLOCK // SPAN)
        s = [
            lax.dot_general(
                q[u * SPAN : u * SPAN + SPAN], k[u * SPAN : u * SPAN + 2 * SPAN], ACROSS, preferred_element_type=F32
            )
            for u in spans
        ]
        s = jnp.concatenate(s, axis=0) * SCALE + bias[pl.ds(base, BLOCK), :].astype(F32)
        top = jnp.max(s, axis=1, keepdims=True)
        e = jnp.exp(s - top)
        total = jnp.sum(e, axis=1, keepdims=True)
        p = (e * (1.0 / total)).astype(BF16)
        probs[pl.ds(base, BLOCK), :] = p
        for u in spans:
            out[0][u * SPAN : u * SPAN + SPAN, :] = jnp.dot(
                p[u * SPAN : u * SPAN + SPAN], v[u * SPAN : u * SPAN + 2 * SPAN], preferred_element_type=F32
            )
        out[1][...] = jnp.broadcast_to(top + jnp.log(total), (BLOCK, DH))

    def step(i, c):
        b = 2 * i
        scatter(jnp.maximum(b - 1, 0), done[1])
        gather(b + 1, came[1])
        compute(b, came[0], done[0])
        scatter(b, done[0])
        gather(jnp.minimum(b + 2, blocks - 1), came[0])
        compute(b + 1, came[1], done[1])
        return c

    lax.fori_loop(0, blocks // 2, step, 0)
    scatter(blocks - 1, done[1])

    across = lax.broadcasted_iota(jnp.int32, (128, 128), 0)
    eye = across == lax.broadcasted_iota(jnp.int32, (128, 128), 1)

    def send(b, c):
        at = pl.ds(b * 256, 256)
        msg[b, 0:256, :] = oq[at, :].astype(BF16)
        lo = jnp.sum(jnp.where(eye, ov[pl.ds(b * 256, 128), :], 0.0), axis=0, keepdims=True)
        hi = jnp.sum(jnp.where(eye, ov[pl.ds(b * 256 + 128, 128), :], 0.0), axis=0, keepdims=True)
        parts = split3(lo) + split3(hi)
        tail = [p.astype(F32) for p in parts] + [jnp.zeros((EXTRA - 6, 128), F32)]
        msg[b, 256:, :] = jnp.concatenate(tail, axis=0).astype(BF16)
        return c

    lax.fori_loop(0, length // 256, send, 0)


def attend(order, mine, other, bias):
    length = order.shape[0]
    return pl.pallas_call(
        attend_kernel,
        out_shape=[
            sd((length // 256, 256 + EXTRA, DH), BF16),
            sd((length, DH), BF16),
            sd((length + SPAN, DH), BF16),
            sd((length + SPAN, DH), BF16),
            sd((length, DH), BF16),
        ],
        in_specs=[pl.BlockSpec(memory_space=pltpu.SMEM)] + vm(3),
        out_specs=vm(5),
        scratch_shapes=[pltpu.VMEM((length, DH), F32)] * 4 + [pltpu.VMEM((BLOCK, DH), F32)] * 8,
        compiler_params=params(),
        name="attend",
        cost_estimate=takes(37),
    )(order, mine, other, bias)


def back_value_kernel(order, msg, vals, probs, keep, give, gd_out, xg, xd, ov, saved, carry, *slots):
    length = probs.shape[0]
    blocks = length // BLOCK
    came, done = (slots[0:2], slots[2:4]), (slots[4:5], slots[5:6])

    def widen(b, c):
        xg[pl.ds(b * 256, 256), :] = msg[b, 0:256, :].astype(F32)
        t = msg[b, 256:, :].astype(F32)
        lo = t[0:1] + t[1:2] + t[2:3]
        hi = t[3:4] + t[4:5] + t[5:6]
        xd[pl.ds(b * 256, 128), :] = jnp.transpose(jnp.broadcast_to(lo, (128, 128)))
        xd[pl.ds(b * 256 + 128, 128), :] = jnp.transpose(jnp.broadcast_to(hi, (128, 128)))
        return c

    lax.fori_loop(0, length // 256, widen, 0)

    def gather(b, slot):
        shift_rows(order, b * BLOCK, list(zip((xg, xd), slot)), True)

    def scatter(b, slot):
        base = jnp.where(b == 0, length, b * BLOCK) - SPAN
        for u in range(BLOCK):
            if u == SPAN:
                base = b * BLOCK - SPAN
            ov[pl.ds(order[base + u], 1), :] = slot[0][u : u + 1, :]

    gather(0, came[0])
    carry[...] = jnp.zeros(carry.shape, F32)

    def compute(b, slot, out):
        base = pl.multiple_of(b * BLOCK, BLOCK)
        g = slot[0][...].astype(BF16)
        p = probs[pl.ds(base, BLOCK), :]
        v = vals[pl.ds(base, BLOCK + SPAN), :]
        spans = range(BLOCK // SPAN)
        cut = lambda a, u: a[u * SPAN : u * SPAN + SPAN]
        gp = [
            lax.dot_general(cut(g, u), v[u * SPAN : u * SPAN + 2 * SPAN], ACROSS, preferred_element_type=F32)
            for u in spans
        ]
        gs = p.astype(F32) * (jnp.concatenate(gp, axis=0) - slot[1][...])
        gd_out[pl.ds(base, BLOCK), :] = (gs * SCALE).astype(BF16)
        wide = [lax.dot_general(cut(p, u), cut(g, u), FLIP, preferred_element_type=F32) for u in spans]

        @pl.when(b == 0)
        def _():
            saved[...] = wide[0][:SPAN]

        out[0][0:SPAN, :] = carry[...] + wide[0][:SPAN]
        for u in spans[1:]:
            out[0][u * SPAN : u * SPAN + SPAN, :] = wide[u - 1][SPAN:] + wide[u][:SPAN]
        carry[...] = wide[-1][SPAN:]

    def step(i, c):
        b = 2 * i
        scatter(jnp.maximum(b - 1, 0), done[1])
        gather(b + 1, came[1])
        compute(b, came[0], done[0])
        scatter(b, done[0])
        gather(jnp.minimum(b + 2, blocks - 1), came[0])
        compute(b + 1, came[1], done[1])
        return c

    lax.fori_loop(0, blocks // 2, step, 0)
    scatter(blocks - 1, done[1])
    carry[...] += saved[...]
    for u in range(SPAN):
        ov[pl.ds(order[length - SPAN + u], 1), :] = carry[u : u + 1, :]
    by_core(ov, keep, give)


def back_value(order, msg, vals, probs):
    length = probs.shape[0]
    half = length // 512
    return pl.pallas_call(
        back_value_kernel,
        out_shape=[sd((half, 256, DH), BF16)] * 2 + [sd((length, DH), BF16)],
        in_specs=[pl.BlockSpec(memory_space=pltpu.SMEM)] + vm(3),
        out_specs=vm(3),
        scratch_shapes=[pltpu.VMEM((length, DH), F32)] * 3
        + [pltpu.VMEM((SPAN, DH), F32)] * 2
        + [pltpu.VMEM((BLOCK, DH), F32)] * 6,
        compiler_params=params(),
        name="back_value",
        cost_estimate=takes(26),
    )(order, msg, vals, probs)


def back_query_kernel(order, gd, q_in, keys, keep, give, oq, saved, carry, waiting, *done):
    length = q_in.shape[0]
    blocks = length // BLOCK

    def scatter(b, slot):
        base = jnp.where(b == 0, length, b * BLOCK) - SPAN
        for u in range(BLOCK):
            if u == SPAN:
                base = b * BLOCK - SPAN
            oq[pl.ds(order[base + u], 1), :] = slot[u : u + 1, :]

    carry[...] = jnp.zeros(carry.shape, F32)
    waiting[...] = jnp.zeros(waiting.shape, F32)

    def whole(direct, unit_grad, q):
        q = q.astype(F32)
        r = lax.rsqrt(jnp.sum(q * q, axis=1, keepdims=True) + EPS_KEY)
        along = jnp.sum(q * unit_grad, axis=1, keepdims=True)
        return direct + r * unit_grad - q * (r * r * r * along)

    def compute(b, out):
        base = pl.multiple_of(b * BLOCK, BLOCK)
        d = gd[pl.ds(base, BLOCK), :]
        q = q_in[pl.ds(base, BLOCK), :]
        k = keys[pl.ds(base, BLOCK + SPAN), :]
        back = q_in[pl.ds(pl.multiple_of(jnp.maximum(base - SPAN, 0), SPAN), SPAN), :]
        spans = range(BLOCK // SPAN)
        cut = lambda a, u: a[u * SPAN : u * SPAN + SPAN]
        direct = [jnp.dot(cut(d, u), k[u * SPAN : u * SPAN + 2 * SPAN], preferred_element_type=F32) for u in spans]
        wide = [lax.dot_general(cut(d, u), cut(q, u), FLIP, preferred_element_type=F32) for u in spans]

        @pl.when(b == 0)
        def _():
            saved[...] = wide[0][:SPAN]

        folded = [carry[...] + wide[0][:SPAN]] + [wide[u - 1][SPAN:] + wide[u][:SPAN] for u in spans[1:]]
        straight = [waiting[...]] + direct[:-1]
        behind = jnp.concatenate([back, q[: BLOCK - SPAN]], axis=0)
        out[...] = whole(jnp.concatenate(straight, axis=0), jnp.concatenate(folded, axis=0), behind)
        carry[...] = wide[-1][SPAN:]
        waiting[...] = direct[-1]

    def step(i, c):
        b = 2 * i
        scatter(jnp.maximum(b - 1, 0), done[1])
        compute(b, done[0])
        scatter(b, done[0])
        compute(b + 1, done[1])
        return c

    lax.fori_loop(0, blocks // 2, step, 0)
    scatter(blocks - 1, done[1])
    waiting[...] = whole(waiting[...], carry[...] + saved[...], q_in[length - SPAN : length, :])
    for u in range(SPAN):
        oq[pl.ds(order[length - SPAN + u], 1), :] = waiting[u : u + 1, :]
    by_core(oq, keep, give)


def back_query(order, gd, q_in, keys):
    length = q_in.shape[0]
    half = length // 512
    return pl.pallas_call(
        back_query_kernel,
        out_shape=[sd((half, 256, DH), BF16)] * 2,
        in_specs=[pl.BlockSpec(memory_space=pltpu.SMEM)] + vm(3),
        out_specs=vm(2),
        scratch_shapes=[pltpu.VMEM((length, DH), F32)]
        + [pltpu.VMEM((SPAN, DH), F32)] * 3
        + [pltpu.VMEM((BLOCK, DH), F32)] * 2,
        compiler_params=params(),
        name="back_query",
        cost_estimate=takes(17),
    )(order, gd, q_in, keys)


def prepare(bucket_row, ends):
    length = bucket_row.shape[0]
    places = jnp.arange(length, dtype=jnp.int32)
    _, order = lax.sort((bucket_row * length + places, places), num_keys=1)
    pos = order.reshape(-1, SPAN)
    start = jnp.max(jnp.where(ends <= pos[..., None], ends, 0), axis=-1)
    window = jnp.concatenate([jnp.roll(pos, 1, 0), pos], axis=1)
    k, q = window[:, None, :], pos[:, :, None]
    bias = jnp.where((k >= start[:, :, None]) & (k <= q), jnp.where(k == q, -1000.0, 0.0), -1e9)
    return order, bias.astype(BF16).reshape(length, 2 * SPAN)


def combine_kernel(
    msg, x, w_out, gain, offset, mix, first_out, first_low, normed, weights, keep, give, normed_a, normed_b, low_mix, turned
):
    rows = x.shape[0]
    for half in range(2):
        logs = []
        for r in range(ROUNDS):
            lines = []
            for h in range(HEADS):
                tail = msg[h * ROUNDS + r, rows : rows + EXTRA, :].astype(F32)
                k = half * 3
                lines.append(tail[k : k + 1] + tail[k + 1 : k + 2] + tail[k + 2 : k + 3])
            logs.append(jnp.concatenate(lines, axis=0))
        top = jnp.maximum(jnp.maximum(logs[0], logs[1]), jnp.maximum(logs[2], logs[3]))
        powers = [jnp.exp(v - top) for v in logs]
        inverse = 1.0 / (powers[0] + powers[1] + powers[2] + powers[3])
        lines = [v * inverse for v in powers]
        lines.append(jnp.zeros((128 - HEADS * ROUNDS, 128), F32))
        weights[half * 128 : half * 128 + 128, :] = jnp.transpose(jnp.concatenate(lines, axis=0))
    for h in range(HEADS):
        total = jnp.zeros((rows, DH), F32)
        for r in range(ROUNDS):
            j = r * HEADS + h
            total = total + weights[:, j : j + 1] * msg[h * ROUNDS + r, 0:rows, :].astype(F32)
        mix[:, h * DH : (h + 1) * DH] = total
        low_mix[:, h * DH : (h + 1) * DH] = total.astype(BF16)
    first = x[...].astype(F32) + jnp.dot(low_mix[...], w_out[...], preferred_element_type=F32)
    first_out[...] = first
    first_low[...] = first.astype(BF16)
    normed[...] = layer_rows(first, gain[...], offset[...]).astype(BF16)
    normed_a[...] = normed[: rows // 2, :]
    normed_b[...] = normed[rows // 2 :, :]
    turned[...] = jnp.transpose(mix[...]).astype(BF16)
    split_by_core(turned, keep, give)


def combine(msg, x, w_out, gain, offset):
    rows, width = x.shape
    return pl.pallas_call(
        combine_kernel,
        out_shape=[
            sd((rows, width), F32),
            sd((rows, width), F32),
            sd((rows, width), BF16),
            sd((rows, width), BF16),
            sd((rows, 128), F32),
            sd((width // 64, 32, rows), BF16),
            sd((width // 64, 32, rows), BF16),
            sd((rows // 2, width), BF16),
            sd((rows // 2, width), BF16),
        ],
        in_specs=vm(5),
        out_specs=vm(9),
        scratch_shapes=[pltpu.VMEM((rows, width), BF16), pltpu.VMEM((width, rows), BF16)],
        compiler_params=params(),
        name="combine",
        cost_estimate=takes(6),
    )(msg, x, w_out, gain, offset)


def anywhere(n):
    return [pl.BlockSpec(memory_space=pl.ANY)] * n


def far_copies(own, far, to, sems, first, flip, pieces):
    out = []
    for i in pieces:
        dst = to.at[(i + 1) // 2, pl.ds((i - 1) % 2 * 512, 512)] if i else to.at[0]
        src = (far[i + 5] if flip else far[i - 1]).at[pl.ds(0, 512)] if i else own
        out.append(pltpu.make_async_copy(src, dst, sems.at[first + i]))
    return out


def start_copies(copies):
    core = lax.axis_index("seq") % 2
    for side in range(2):

        @pl.when(core == side)
        def _():
            for c in copies(side == 1):
                c.start()


def wait_copies(own, far, to, sems, first, k):
    for c in far_copies(own, far, to, sems, first, False, (2 * k - 1, 2 * k) if k else (0,)):
        c.wait()


def gelu_both(act, grad):
    share = 0.5 + 0.5 * lax.erf(act * 0.7071067811865476)
    slope = share + act * (jnp.exp(act * act * -0.5) * 0.3989422804014327)
    return (act * share).astype(BF16), (grad * slope).astype(BF16)


def middle_kernel(*refs):
    normed, g_two, up0, down0, far = refs[0], refs[1], refs[2], refs[3], refs[4:16]
    grad_normed, hid, pre0, up, down, pre, sems = refs[16:]
    pieces = range(7)
    start_copies(
        lambda flip: far_copies(up0, far, up, sems, 0, flip, pieces)
        + far_copies(down0, far, down, sems, 7, not flip, pieces)
    )
    for k in range(4):
        wait_copies(up0, far, up, sems, 0, k)
        wait_copies(down0, far, down, sems, 7, k)

        def hidden_part(i, c):
            for u in range(2):
                at = pl.ds(pl.multiple_of(i * 512 + u * 256, 256), 256)
                act = jnp.dot(normed[...], up[k, :, at], preferred_element_type=F32)
                grad = jnp.dot(g_two[...], down[k, :, at], preferred_element_type=F32)
                hid[k, :, at], pre[k, :, at] = gelu_both(act, grad)
            return c

        lax.fori_loop(0, 2, hidden_part, 0)
    pre0[...] = pre[0]
    grad_normed[...] = jnp.zeros(grad_normed.shape, F32)

    def up_back(k, c):
        grad_normed[...] += lax.dot_general(pre[k], up[k], ACROSS, preferred_element_type=F32)
        return c

    lax.fori_loop(0, 4, up_back, 0)


def middle(normed, g_two, up0, down0, far):
    rows, width = normed.shape
    return pl.pallas_call(
        middle_kernel,
        out_shape=[sd((rows, width), F32), sd((4, rows, 1024), BF16), sd((rows, 1024), BF16)],
        in_specs=vm(2) + anywhere(14),
        out_specs=vm(3),
        scratch_shapes=[
            pltpu.VMEM((4, width, 1024), BF16),
            pltpu.VMEM((4, width, 1024), BF16),
            pltpu.VMEM((4, rows, 1024), BF16),
            pltpu.SemaphoreType.DMA((14,)),
        ],
        compiler_params=params(),
        name="middle",
        cost_estimate=takes(16),
    )(normed, g_two, up0, down0, *far)


def uncombine_kernel(
    grad_normed, mix, first, weights, g_one, w_out, gain, grad_first, sent, grad_gain, grad_offset, low_first
):
    rows = g_one.shape[0]
    grad_x, gg, go = layer_back(first[...], grad_normed[...], gain[...])
    grad_gain[...] = gg
    grad_offset[...] = go
    grad_x = grad_x + g_one[...].astype(F32)
    grad_first[...] = grad_x
    low_first[...] = grad_x.astype(BF16)
    lane = lax.broadcasted_iota(jnp.int32, (rows, 128), 1)
    inner = jnp.zeros((rows, 128), F32)
    for h in range(HEADS):
        at = slice(h * DH, (h + 1) * DH)
        grad_mix = lax.dot_general(low_first[...], w_out[at, :], ACROSS, preferred_element_type=F32)
        dots = jnp.sum(grad_mix * mix[:, at], axis=1, keepdims=True)
        inner = jnp.where(lane % HEADS == h, dots, inner)
        for r in range(ROUNDS):
            j = r * HEADS + h
            sent[h * ROUNDS + r, 0:rows, :] = (weights[:, j : j + 1] * grad_mix).astype(BF16)
    inner = inner * weights[...]
    low_lines = [p.astype(F32) for p in split3(jnp.transpose(inner[0:128]))]
    high_lines = [p.astype(F32) for p in split3(jnp.transpose(inner[128:256]))]
    blank = jnp.zeros((EXTRA - 6, 128), F32)
    for h in range(HEADS):
        for r in range(ROUNDS):
            j = r * HEADS + h
            tail = [p[j : j + 1] for p in low_lines + high_lines] + [blank]
            sent[h * ROUNDS + r, rows : rows + EXTRA, :] = jnp.concatenate(tail, axis=0).astype(BF16)


def uncombine(grad_normed, mix, first, weights, g_one, w_out, gain):
    rows, width = g_one.shape
    return pl.pallas_call(
        uncombine_kernel,
        out_shape=[
            sd((rows, width), F32),
            sd((HEADS * ROUNDS, rows + EXTRA, DH), BF16),
            sd((1, width), F32),
            sd((1, width), F32),
            sd((rows, width), BF16),
        ],
        in_specs=vm(7),
        out_specs=vm(5),
        compiler_params=params(),
        name="uncombine",
        cost_estimate=takes(8),
    )(grad_normed, mix, first, weights, g_one, w_out, gain)


def down_out_kernel(*refs):
    hid, x, down0, far = refs[0], refs[1], refs[2], refs[3:15]
    out, down, summed, sems = refs[15:]
    start_copies(lambda flip: far_copies(down0, far, down, sems, 0, not flip, range(7)))
    summed[...] = x[...].astype(F32)
    for k in range(4):
        wait_copies(down0, far, down, sems, 0, k)
        summed[...] += lax.dot_general(hid[k], down[k], ACROSS, preferred_element_type=F32)
    out[...] = summed[...].astype(BF16)


def down_out(hid, x, down0, far):
    rows, width = x.shape
    return pl.pallas_call(
        down_out_kernel,
        out_shape=sd((rows, width), BF16),
        in_specs=vm(2) + anywhere(13),
        out_specs=pl.BlockSpec(memory_space=pltpu.VMEM),
        scratch_shapes=[
            pltpu.VMEM((4, width, 1024), BF16),
            pltpu.VMEM((rows, width), F32),
            pltpu.SemaphoreType.DMA((7,)),
        ],
        compiler_params=params(),
        name="down_out",
        cost_estimate=takes(6),
    )(hid, x, down0, *far)


def feed_kernel(normed, grads, hid_own, pre0, *refs):
    halves, (g1, g2, g3, up, down, keep, give, hid, pre, rest, turned, total) = refs[:6], refs[6:]
    rows = normed.shape[0]
    core = lax.axis_index("seq") % 2
    hid[0] = hid_own[0]
    pre[0] = pre0[...]
    for i, half in enumerate(halves):
        rest[i // 2, i % 2 * (rows // 2) : (i % 2 + 1) * (rows // 2), :] = half[...]
    n1, n2, n3 = rest.at[0], rest.at[1], rest.at[2]
    for k, (n, g) in enumerate(((n1, g1), (n2, g2), (n3, g3)), start=1):

        def hidden_part(i, c):
            at = pl.ds(pl.multiple_of(i * 256, 256), 256)
            act = jnp.dot(n[...], up[:, at], preferred_element_type=F32)
            grad = jnp.dot(last_rows(g, rows), down[:, at], preferred_element_type=F32)
            hid[k, :, at], pre[k, :, at] = gelu_both(act, grad)
            return c

        lax.fori_loop(0, 4, hidden_part, 0)
    for first, lefts, rights in ((0, (normed, n1, n2, n3), pre), (1024, (grads, g1, g2, g3), hid)):
        left = jnp.concatenate([last_rows(x, rows) for x in lefts], axis=0)
        turned[...] = jnp.transpose(left.astype(F32)).astype(BF16)

        def piece(i, c):
            left = turned[pl.ds(pl.multiple_of(i * 256, 256), 256), :]
            total[...] = jnp.dot(left, rights[...].reshape(4 * rows, 1024), preferred_element_type=F32)
            for out, side in ((keep, core), (give, 1 - core)):
                for j in range(4):
                    lines = total[pl.ds(pl.multiple_of(j * 64 + side * 32, 32), 32), :]
                    out[j * 4 + i, :, first : first + 1024] = lines.astype(BF16)
            return c

        lax.fori_loop(0, keep.shape[0] // 4, piece, 0)


def last_rows(ref, rows):
    return ref[ref.shape[0] - rows :, :]


def feed(normed, grads, hid_own, pre0, normed_far, grads_far, up, down):
    rows, width = normed.shape
    return pl.pallas_call(
        feed_kernel,
        out_shape=[sd((width // 64, 32, 2048), BF16)] * 2,
        in_specs=vm(15),
        out_specs=vm(2),
        scratch_shapes=[pltpu.VMEM((4, rows, 1024), BF16)] * 2
        + [pltpu.VMEM((3, rows, width), BF16), pltpu.VMEM((width, 4 * rows), BF16), pltpu.VMEM((256, 1024), F32)],
        compiler_params=params(),
        name="feed",
        cost_estimate=takes(20),
    )(normed, grads, hid_own, pre0, *normed_far, *grads_far, up, down)


def sum_rounds_kernel(back, out):
    for h in range(HEADS):
        total = back[2 * h].astype(F32) + back[2 * h + 1].astype(F32)
        for half in range(2):
            at = slice(half * HEADS * DH + h * DH, half * HEADS * DH + (h + 1) * DH)
            out[:, at] = total[:, half * DH : (half + 1) * DH].astype(BF16)


def sum_rounds(back):
    rows = back.shape[1]
    return pl.pallas_call(
        sum_rounds_kernel,
        out_shape=sd((rows, 2 * HEADS * DH), BF16),
        in_specs=vm(1),
        out_specs=pl.BlockSpec(memory_space=pltpu.VMEM),
        compiler_params=params(),
        name="sum_rounds",
        cost_estimate=takes(3),
    )(back)


def finish_kernel(grads, x, gain, w_qk, w_value, grad_two, gain_two, offset_two, grad_second, small, near, far):
    width = x.shape[1]
    grad_normed = lax.dot_general(grads[:, :width], w_qk[...], ACROSS, preferred_element_type=F32)
    grad_normed = grad_normed + lax.dot_general(grads[:, width:], w_value[...], ACROSS, preferred_element_type=F32)
    grad_x, gg, go = layer_back(x[...].astype(F32), grad_normed, gain[...])
    grad_second[...] = grad_x + grad_two[...].astype(F32)
    lines = []
    for line in (gg, go, gain_two[...], offset_two[...]):
        high = line.astype(BF16).astype(F32)
        lines += [high, line - high]
    blank = jnp.zeros((8, width), F32)
    rest = jnp.zeros((112, width), F32)
    near[...] = jnp.transpose(jnp.concatenate(lines + [blank, rest], axis=0))
    far[...] = jnp.transpose(jnp.concatenate([blank] + lines + [rest], axis=0))
    core = lax.axis_index("seq") % 2
    for j in range(small.shape[0]):
        a = near[pl.ds(pl.multiple_of(j * 64 + core * 32, 32), 32), :]
        b = far[pl.ds(pl.multiple_of(j * 64 + (1 - core) * 32, 32), 32), :]
        small[j] = (a + b).astype(BF16)


def finish(grads, x, gain, w_qk, w_value, grad_two, gain_two, offset_two):
    rows, width = x.shape
    return pl.pallas_call(
        finish_kernel,
        out_shape=[sd((rows, width), F32), sd((width // 64, 32, 128), BF16)],
        in_specs=vm(8),
        out_specs=vm(2),
        scratch_shapes=[pltpu.VMEM((width, 128), F32)] * 2,
        compiler_params=params(),
        name="finish",
        cost_estimate=takes(5),
    )(grads, x, gain, w_qk, w_value, grad_two, gain_two, offset_two)


def pair_kernel(left, left_other, right, right_other, *rest):
    blocks, lines, rows = left.shape
    out, width = rest[-1], right.shape[1]
    total = jnp.dot(left[...].reshape(blocks * lines, rows), right[...], preferred_element_type=F32)
    total = total + jnp.dot(left_other[...].reshape(blocks * lines, rows), right_other[...], preferred_element_type=F32)
    out[:, :, :width] = total.astype(BF16).reshape(blocks, lines, width)
    for extra in rest[:-1]:
        out[:, :, width : width + extra.shape[2]] = extra[...]
        width += extra.shape[2]


def pair(left, left_other, right, right_other, *extra):
    blocks, lines, rows = left.shape
    width = right.shape[1] + sum(e.shape[2] for e in extra)
    return pl.pallas_call(
        pair_kernel,
        out_shape=sd((blocks, lines, width), BF16),
        in_specs=vm(4 + len(extra)),
        out_specs=pl.BlockSpec(memory_space=pltpu.VMEM),
        compiler_params=params(),
        name="pair",
        cost_estimate=takes(3),
    )(left, left_other, right, right_other, *extra)


def swap_seq(array):
    return lax.all_to_all(array, "seq", split_axis=0, concat_axis=0, tiled=True)


def same_core():
    count = lax.axis_size("seq")
    return [list(range(c, count, 2)) for c in range(2)]


def along_x():
    return [[y * 8 + x * 2 + c for x in range(4)] for y in range(4) for c in range(2)]


def along_y():
    return [[y * 8 + x * 2 + c for y in range(4)] for x in range(4) for c in range(2)]


def swap_chips(array):
    return lax.all_to_all(
        array, "seq", split_axis=0, concat_axis=0, tiled=True, axis_index_groups=same_core()
    )


def flip_bit(array, axis, bit):
    return lax.ppermute(array, axis, [(i, i ^ bit) for i in range(lax.axis_size(axis))])


def swap_cores(array):
    return flip_bit(array, "seq", 1)


def from_ahead(array, step):
    count = lax.axis_size("ffn")
    return lax.ppermute(array, "ffn", [((i + step) % count, i) for i in range(count)])


def tied(array, *others):
    return lax.optimization_barrier((array, others))[0]


def add_low(a, b):
    return (a.astype(F32) + b.astype(F32)).astype(BF16)


def shards(
    stream_one,
    stream_two,
    doc_lengths,
    bucket_ids,
    norm1_gain,
    norm1_bias,
    w_qk,
    w_value,
    w_out,
    norm2_gain,
    norm2_bias,
    w_up,
    w_down,
    grad_out_one,
    grad_out_two,
):
    rows, width = stream_one.shape[1:]
    seq, ffn = lax.axis_index("seq"), lax.axis_index("ffn")
    core = seq % 2
    gain_one, bias_one = norm1_gain.reshape(1, -1), norm1_bias.reshape(1, -1)
    gain_two, bias_two = norm2_gain.reshape(1, -1), norm2_bias.reshape(1, -1)

    msg, normed_one, keep_rows, give_rows = project(stream_two[0], gain_one, bias_one, w_qk, w_value)
    received = swap_chips(msg)
    top, low = [jnp.where(core == 0, w_up[at], w_down[at]) for at in (slice(0, 512), slice(512, 1024))]
    buckets, top, low = lax.optimization_barrier((bucket_ids[0, 0], top, low))
    top1, low3 = from_ahead(top, 1), from_ahead(low, 3)
    order, bias = prepare(buckets, jnp.cumsum(doc_lengths[0]))
    received, order, bias, top, low, top1, low3 = lax.optimization_barrier(
        (received, order, bias, top, low, top1, low3)
    )
    lowg1 = from_ahead(jnp.concatenate([low, grad_out_two[0]], axis=0), 1)
    topg3 = from_ahead(jnp.concatenate([top, grad_out_two[0]], axis=0), 3)
    other_rows = swap_cores(give_rows)
    top1_other, low3_other = swap_cores(top1), swap_cores(low3)
    sent, queries, keys, vals, probs = attend(order, received, swap_cores(received), bias)
    sent, top1, low3, lowg1, topg3, top1_other, low3_other, other_rows = lax.optimization_barrier(
        (sent, top1, low3, lowg1, topg3, top1_other, low3_other, other_rows)
    )
    per_round = swap_seq(sent)
    top2, low2 = from_ahead(top1, 1), from_ahead(low3, 3)
    lowg1_other, topg3_other = swap_cores(lowg1), swap_cores(topg3)
    per_round, top2, low2, lowg1_other, topg3_other = lax.optimization_barrier(
        (per_round, top2, low2, lowg1_other, topg3_other)
    )
    far_weights = [top1, lowg1, top2, low2, topg3, low3]
    far_weights += [top1_other, lowg1_other, swap_cores(top2), swap_cores(low2), topg3_other, low3_other]
    grads2 = from_ahead(topg3[512:], 3)
    mix, first, one_low, normed_two, weights, keep_mix, give_mix, *halves = combine(per_round, stream_one[0], w_out, gain_two, bias_two)
    ahead, behind = [from_ahead(half, 1) for half in halves], [from_ahead(half, 3) for half in halves]
    grad_normed, hid, pre0 = middle(normed_two, grad_out_two[0], w_up, w_down, far_weights)
    grad_normed, ahead, behind, grads2 = lax.optimization_barrier((grad_normed, ahead, behind, grads2))
    normed_far = ahead + [from_ahead(ahead[0], 1), from_ahead(behind[1], 3)] + behind
    grad_first, msg, grad_gain_two, grad_bias_two, low_first = uncombine(
        grad_normed, mix, first, weights, grad_out_one[0], w_out, gain_two
    )
    far = swap_seq(msg)
    keep_feed, give_feed = feed(
        normed_two, grad_out_two[0], hid, pre0, normed_far, [lowg1, grads2, topg3], w_up, w_down
    )
    part_out = pair(keep_mix, swap_cores(give_mix), low_first, swap_cores(low_first)).reshape(-1, 4, 8, width)
    far, keep_feed, give_feed, part_out = lax.optimization_barrier((far, keep_feed, give_feed, part_out))
    came_feed = swap_cores(give_feed)
    keep_v, give_v, grad_dots = back_value(order, far, vals, probs)
    keep_q, give_q = back_query(order, grad_dots, queries, keys)
    part_feed = add_low(keep_feed, came_feed)
    near_feed = part_feed.reshape(-1, part_feed.shape[2])
    for groups in (along_x(), along_y()):
        near_feed = lax.psum_scatter(near_feed, "seq", tiled=True, axis_index_groups=groups)
    part_out = tied(part_out, keep_q)
    blocks = [
        from_ahead(lax.dynamic_index_in_dim(part_out, (ffn + 4 - k) % 4, 1, keepdims=False), k) for k in (1, 2, 3)
    ]
    came_v, came_q = swap_cores(give_v), swap_cores(give_q)
    back = swap_chips(jnp.concatenate([add_low(keep_q, came_q), add_low(keep_v, came_v)], axis=2))
    back, blocks = lax.optimization_barrier((back, blocks))
    sums_out = lax.dynamic_index_in_dim(part_out, ffn, 1, keepdims=False).astype(F32)
    for block in blocks:
        sums_out = sums_out + block.astype(F32)
    sums_out = sums_out.astype(BF16).reshape(-1, 32, width // 4)
    hid = tied(hid, keep_q)
    two_low = down_out(hid, stream_two[0], w_down, far_weights)
    grads = sum_rounds(back)
    grads_other = swap_cores(grads)
    grad_second, small = finish(
        grads, stream_two[0], gain_one, w_qk, w_value, grad_out_two[0], grad_gain_two, grad_bias_two
    )
    part = pair(keep_rows, other_rows, grads, grads_other, small, sums_out)
    near = swap_chips(part)
    near, near_feed = lax.optimization_barrier((near, near_feed))
    near = near.astype(F32).sum(axis=0)
    near, near_out = near[:, : 2 * width + 128].reshape(4, 8, -1), near[:, 2 * width + 128 :]
    whole = lax.dynamic_index_in_dim(near, ffn, 0, keepdims=False)
    for k in (1, 2, 3):
        whole = whole + from_ahead(lax.dynamic_index_in_dim(near, (ffn + 4 - k) % 4, 0, keepdims=False), k)
    small = whole[:, 2 * width :]
    lines = small[:, :8] + swap_cores(small)[:, 8:16]
    lines = lines[:, 0::2] + lines[:, 1::2]
    near_feed = near_feed.astype(F32)
    return (
        one_low[None],
        two_low[None],
        grad_first[None],
        grad_second[None],
        lines[:, 0],
        lines[:, 1],
        whole[:, :width],
        whole[:, width : 2 * width],
        near_out.reshape(8, width),
        lines[:, 2],
        lines[:, 3],
        near_feed[:, :1024],
        near_feed[:, 1024:2048],
    )


def solution(mesh):
    return jax.shard_map(
        shards,
        mesh=mesh,
        in_specs=(
            P("ffn", "seq", None),
            P("ffn", "seq", None),
            P("ffn", None),
            P("ffn", "seq", None),
            P(),
            P(),
            P(),
            P(),
            P(),
            P(),
            P(),
            P(None, "ffn"),
            P(None, "ffn"),
            P("ffn", "seq", None),
            P("ffn", "seq", None),
        ),
        out_specs=(
            P("ffn", "seq", None),
            P("ffn", "seq", None),
            P("ffn", "seq", None),
            P("ffn", "seq", None),
            P(("seq", "ffn")),
            P(("seq", "ffn")),
            P(("seq", "ffn"), None),
            P(("seq", "ffn"), None),
            P(("seq", "ffn"), None),
            P(("seq", "ffn")),
            P(("seq", "ffn")),
            P("seq", "ffn"),
            P("seq", "ffn"),
        ),
        check_vma=False,
    )
```

```python
import jax
import jax.numpy as jnp
from jax import lax
from jax.experimental import pallas as pl
from jax.experimental.pallas import tpu as pltpu
from jax.sharding import PartitionSpec as P

HEADS = 8
DH = 128
ROUNDS = 4
SPAN = 64
EPS_NORM = 1e-05
EPS_KEY = 1e-06
SELF_PENALTY = 1000.0
SCALE = DH ** (-0.5)
EXTRA = 16
F32, BF16 = jnp.float32, jnp.bfloat16
VMEM_LIMIT = 60 * 2**20
ACROSS = (((1,), (1,)), ((), ()))
FLIP = (((0,), (0,)), ((), ()))


def vm(n):
    return [pl.BlockSpec(memory_space=pltpu.VMEM)] * n


def sd(shape, kind):
    return jax.ShapeDtypeStruct(shape, kind)


def params():
    return pltpu.CompilerParams(vmem_limit_bytes=VMEM_LIMIT)


def takes(us):
    return pl.CostEstimate(flops=0, transcendentals=0, bytes_accessed=int(us * 3.5e6))


def split3(x):
    a = x.astype(BF16)
    r = x - a.astype(F32)
    b = r.astype(BF16)
    c = (r - b.astype(F32)).astype(BF16)
    return a, b, c


def layer_rows(x, gain, offset):
    centred = x - jnp.mean(x, axis=1, keepdims=True)
    inverse = lax.rsqrt(jnp.mean(centred * centred, axis=1, keepdims=True) + EPS_NORM)
    return centred * inverse * gain + offset


def layer_back(x, grad, gain):
    centred = x - jnp.mean(x, axis=1, keepdims=True)
    inverse = lax.rsqrt(jnp.mean(centred * centred, axis=1, keepdims=True) + EPS_NORM)
    unit = centred * inverse
    grad_gain = jnp.sum(grad * unit, axis=0, keepdims=True)
    grad_offset = jnp.sum(grad, axis=0, keepdims=True)
    scaled = grad * gain
    inner = jnp.mean(scaled * unit, axis=1, keepdims=True)
    grad_x = inverse * (scaled - jnp.mean(scaled, axis=1, keepdims=True) - unit * inner)
    return grad_x, grad_gain, grad_offset


def split_by_core(turned, keep, give):
    core = lax.axis_index("seq") % 2
    for j in range(keep.shape[0]):
        keep[j] = turned[pl.ds(pl.multiple_of(j * 64 + core * 32, 32), 32), :]
        give[j] = turned[pl.ds(pl.multiple_of(j * 64 + (1 - core) * 32, 32), 32), :]


def project_kernel(x, gain, offset, w_qk, w_value, msg, normed_out, keep, give, turned):
    normed = layer_rows(x[...].astype(F32), gain[...], offset[...])
    low = normed.astype(BF16)
    normed_out[...] = low
    for h in range(HEADS):
        at = slice(h * DH, (h + 1) * DH)
        q = jnp.dot(low, w_qk[:, at], preferred_element_type=F32).astype(BF16)
        v = jnp.dot(low, w_value[:, at], preferred_element_type=F32).astype(BF16)
        for t in range(2):
            msg[h * 2 + t, :, :DH] = q
            msg[h * 2 + t, :, DH:] = v
    turned[...] = jnp.transpose(low.astype(F32)).astype(BF16)
    split_by_core(turned, keep, give)


def project(x, gain, offset, w_qk, w_value):
    rows, width = x.shape
    chips = 2 * HEADS
    return pl.pallas_call(
        project_kernel,
        out_shape=[
            sd((chips, rows, 2 * DH), BF16),
            sd((rows, width), BF16),
            sd((width // 64, 32, rows), BF16),
            sd((width // 64, 32, rows), BF16),
        ],
        in_specs=vm(5),
        out_specs=vm(4),
        scratch_shapes=[pltpu.VMEM((width, rows), BF16)],
        compiler_params=params(),
        name="project",
        cost_estimate=takes(7),
    )(x, gain, offset, w_qk, w_value)


BLOCK = 4 * SPAN
SAFE = 60.0


def repeat(count, body, width=4):
    def several(i, c):
        for u in range(width):
            body(i * width + u)
        return c

    lax.fori_loop(0, count // width, several, 0)


def even(first, count):
    return pl.ds(2 * first, count, stride=2)


def odd(first, count):
    return pl.ds(2 * first + 1, count, stride=2)


def gather_pairs(order, base, src, slot):
    for u in range(BLOCK):
        place = 2 * order[base + u]
        slot[2 * u : 2 * u + 1, :] = src[pl.ds(place, 1), :]
        slot[2 * u + 1 : 2 * u + 2, :] = src[pl.ds(place + 1, 1), :]


def scatter_pairs(order, base, slot, dst):
    for u in range(BLOCK):
        place = 2 * order[base + u]
        dst[pl.ds(place, 1), :] = slot[2 * u : 2 * u + 1, :]
        dst[pl.ds(place + 1, 1), :] = slot[2 * u + 1 : 2 * u + 2, :]


def by_core(array, keep, give):
    core = lax.axis_index("seq") % 2

    def narrow(j):
        for out, side in ((keep, core), (give, 1 - core)):
            at = pl.ds(pl.multiple_of((2 * j + side) * 256, 256), 256)
            out[j] = array[at, :].astype(BF16)

    repeat(keep.shape[0], narrow)


def attend_kernel(order, mine, other, bias, msg, q_out, keys, vals, probs, came_all, sent_all, *slots):
    length = q_out.shape[0]
    blocks = length // BLOCK
    core = lax.axis_index("seq") % 2
    came, done = slots[0:2], slots[2:4]

    def widen(j):
        for rows, side in ((mine, core), (other, 1 - core)):
            first = pl.multiple_of((2 * j + side) * 256, 256)
            came_all[even(first, 256), :] = rows[j, :, :DH].astype(F32)
            came_all[odd(first, 256), :] = rows[j, :, DH:].astype(F32)

    repeat(length // 512, widen, 2)

    def gather(b, slot):
        gather_pairs(order, b * BLOCK, came_all, slot)

    def scatter(b, slot):
        scatter_pairs(order, b * BLOCK, slot, sent_all)

    def ready(b, slot):
        q = slot[even(0, BLOCK), :]
        unit = q * lax.rsqrt(jnp.sum(q * q, axis=1, keepdims=True) + EPS_KEY)
        ahead = pl.ds(pl.multiple_of(b * BLOCK + SPAN, SPAN), BLOCK)
        keys[ahead, :] = unit.astype(BF16)
        vals[ahead, :] = slot[odd(0, BLOCK), :].astype(BF16)
        return q.astype(BF16)

    gather(blocks - 1, came[1])
    ready(blocks - 1, came[1])
    keys[0:SPAN, :] = keys[length : length + SPAN, :]
    vals[0:SPAN, :] = vals[length : length + SPAN, :]
    gather(0, came[0])

    def compute(b, slot, out):
        base = pl.multiple_of(b * BLOCK, BLOCK)
        q = ready(b, slot)
        q_out[pl.ds(base, BLOCK), :] = q
        k = keys[pl.ds(base, BLOCK + SPAN), :]
        v = vals[pl.ds(base, BLOCK + SPAN), :]
        spans = range(BLOCK // SPAN)
        s = [
            lax.dot_general(
                q[u * SPAN : u * SPAN + SPAN], k[u * SPAN : u * SPAN + 2 * SPAN], ACROSS, preferred_element_type=F32
            )
            for u in spans
        ]
        s = jnp.concatenate(s, axis=0) * SCALE + bias[pl.ds(base, BLOCK), :].astype(F32)
        top = jnp.max(s, axis=1, keepdims=True)
        e = jnp.exp(s - top)
        total = jnp.sum(e, axis=1, keepdims=True)
        p = (e * (1.0 / total)).astype(BF16)
        probs[pl.ds(base, BLOCK), :] = p
        for u in spans:
            out[even(u * SPAN, SPAN), :] = jnp.dot(
                p[u * SPAN : u * SPAN + SPAN], v[u * SPAN : u * SPAN + 2 * SPAN], preferred_element_type=F32
            )
        out[odd(0, BLOCK), :] = jnp.broadcast_to(top + jnp.log(total), (BLOCK, DH))

    def step(i, c):
        b = 2 * i
        scatter(jnp.maximum(b - 1, 0), done[1])
        gather(b + 1, came[1])
        compute(b, came[0], done[0])
        scatter(b, done[0])
        gather(jnp.minimum(b + 2, blocks - 1), came[0])
        compute(b + 1, came[1], done[1])
        return c

    lax.fori_loop(0, blocks // 2, step, 0)
    scatter(blocks - 1, done[1])

    across = lax.broadcasted_iota(jnp.int32, (128, 128), 0)
    eye = across == lax.broadcasted_iota(jnp.int32, (128, 128), 1)

    line = lax.broadcasted_iota(jnp.int32, (EXTRA, 6 * 128), 0)
    lane = lax.broadcasted_iota(jnp.int32, (EXTRA, 6 * 128), 1)
    pick = jnp.where(line == lane // 128, 1.0, 0.0).astype(BF16)

    def send(b):
        msg[b, 0:256, :] = sent_all[even(b * 256, 256), :].astype(BF16)
        parts = []
        for half in range(2):
            parts += split3(jnp.where(eye, sent_all[odd(b * 256 + half * 128, 128), :], 0.0))
        tail = jnp.dot(pick, jnp.concatenate(parts, axis=0), preferred_element_type=F32)
        msg[b, 256:, :] = tail.astype(BF16)

    repeat(length // 256, send)


def attend(order, mine, other, bias):
    length = order.shape[0]
    return pl.pallas_call(
        attend_kernel,
        out_shape=[
            sd((length // 256, 256 + EXTRA, DH), BF16),
            sd((length, DH), BF16),
            sd((length + SPAN, DH), BF16),
            sd((length + SPAN, DH), BF16),
            sd((length, DH), BF16),
        ],
        in_specs=[pl.BlockSpec(memory_space=pltpu.SMEM)] + vm(3),
        out_specs=vm(5),
        scratch_shapes=[pltpu.VMEM((2 * length, DH), F32)] * 2 + [pltpu.VMEM((2 * BLOCK, DH), F32)] * 4,
        compiler_params=params(),
        name="attend",
        cost_estimate=takes(37),
    )(order, mine, other, bias)


def back_value_kernel(order, msg, vals, probs, keep, give, gd_out, came_all, ov, saved, carry, *slots):
    length = probs.shape[0]
    blocks = length // BLOCK
    came, done = slots[0:2], slots[2:4]

    across = lax.broadcasted_iota(jnp.int32, (128, 128), 0)
    eye = across == lax.broadcasted_iota(jnp.int32, (128, 128), 1)
    ones = jnp.ones((128, 128), BF16)

    def widen(b):
        came_all[even(b * 256, 256), :] = msg[b, 0:256, :].astype(F32)
        t = msg[b, 256:, :].astype(F32)
        for half in range(2):
            total = jnp.zeros((128, 128), F32)
            for k in range(3):
                row = half * 3 + k
                spot = jnp.where(eye, jnp.broadcast_to(t[row : row + 1], (128, 128)), 0.0).astype(BF16)
                total = total + jnp.dot(spot, ones, preferred_element_type=F32)
            came_all[odd(b * 256 + half * 128, 128), :] = total

    repeat(length // 256, widen)

    def gather(b, slot):
        gather_pairs(order, b * BLOCK, came_all, slot)

    def scatter(b, slot):
        base = jnp.where(b == 0, length, b * BLOCK) - SPAN
        for u in range(BLOCK):
            if u == SPAN:
                base = b * BLOCK - SPAN
            ov[pl.ds(order[base + u], 1), :] = slot[u : u + 1, :]

    gather(0, came[0])
    carry[...] = jnp.zeros(carry.shape, F32)

    def compute(b, slot, out):
        base = pl.multiple_of(b * BLOCK, BLOCK)
        g = slot[even(0, BLOCK), :].astype(BF16)
        p = probs[pl.ds(base, BLOCK), :]
        v = vals[pl.ds(base, BLOCK + SPAN), :]
        spans = range(BLOCK // SPAN)
        cut = lambda a, u: a[u * SPAN : u * SPAN + SPAN]
        gp = [
            lax.dot_general(cut(g, u), v[u * SPAN : u * SPAN + 2 * SPAN], ACROSS, preferred_element_type=F32)
            for u in spans
        ]
        gs = p.astype(F32) * (jnp.concatenate(gp, axis=0) - slot[odd(0, BLOCK), :])
        gd_out[pl.ds(base, BLOCK), :] = (gs * SCALE).astype(BF16)
        wide = [lax.dot_general(cut(p, u), cut(g, u), FLIP, preferred_element_type=F32) for u in spans]

        @pl.when(b == 0)
        def _():
            saved[...] = wide[0][:SPAN]

        out[0:SPAN, :] = carry[...] + wide[0][:SPAN]
        for u in spans[1:]:
            out[u * SPAN : u * SPAN + SPAN, :] = wide[u - 1][SPAN:] + wide[u][:SPAN]
        carry[...] = wide[-1][SPAN:]

    def step(i, c):
        b = 2 * i
        scatter(jnp.maximum(b - 1, 0), done[1])
        gather(b + 1, came[1])
        compute(b, came[0], done[0])
        scatter(b, done[0])
        gather(jnp.minimum(b + 2, blocks - 1), came[0])
        compute(b + 1, came[1], done[1])
        return c

    lax.fori_loop(0, blocks // 2, step, 0)
    scatter(blocks - 1, done[1])
    carry[...] += saved[...]
    for u in range(SPAN):
        ov[pl.ds(order[length - SPAN + u], 1), :] = carry[u : u + 1, :]
    by_core(ov, keep, give)


def back_value(order, msg, vals, probs):
    length = probs.shape[0]
    half = length // 512
    return pl.pallas_call(
        back_value_kernel,
        out_shape=[sd((half, 256, DH), BF16)] * 2 + [sd((length, DH), BF16)],
        in_specs=[pl.BlockSpec(memory_space=pltpu.SMEM)] + vm(3),
        out_specs=vm(3),
        scratch_shapes=[pltpu.VMEM((2 * length, DH), F32), pltpu.VMEM((length, DH), F32)]
        + [pltpu.VMEM((SPAN, DH), F32)] * 2
        + [pltpu.VMEM((2 * BLOCK, DH), F32)] * 2
        + [pltpu.VMEM((BLOCK, DH), F32)] * 2,
        compiler_params=params(),
        name="back_value",
        cost_estimate=takes(26),
    )(order, msg, vals, probs)


def back_query_kernel(order, gd, q_in, keys, keep, give, oq, saved, carry, waiting, *done):
    length = q_in.shape[0]
    blocks = length // BLOCK

    def scatter(b, slot):
        base = jnp.where(b == 0, length, b * BLOCK) - SPAN
        for u in range(BLOCK):
            if u == SPAN:
                base = b * BLOCK - SPAN
            oq[pl.ds(order[base + u], 1), :] = slot[u : u + 1, :]

    carry[...] = jnp.zeros(carry.shape, F32)
    waiting[...] = jnp.zeros(waiting.shape, F32)

    def whole(direct, unit_grad, q):
        q = q.astype(F32)
        r = lax.rsqrt(jnp.sum(q * q, axis=1, keepdims=True) + EPS_KEY)
        along = jnp.sum(q * unit_grad, axis=1, keepdims=True)
        return direct + r * unit_grad - q * (r * r * r * along)

    def compute(b, out):
        base = pl.multiple_of(b * BLOCK, BLOCK)
        d = gd[pl.ds(base, BLOCK), :]
        q = q_in[pl.ds(base, BLOCK), :]
        k = keys[pl.ds(base, BLOCK + SPAN), :]
        back = q_in[pl.ds(pl.multiple_of(jnp.maximum(base - SPAN, 0), SPAN), SPAN), :]
        spans = range(BLOCK // SPAN)
        cut = lambda a, u: a[u * SPAN : u * SPAN + SPAN]
        direct = [jnp.dot(cut(d, u), k[u * SPAN : u * SPAN + 2 * SPAN], preferred_element_type=F32) for u in spans]
        wide = [lax.dot_general(cut(d, u), cut(q, u), FLIP, preferred_element_type=F32) for u in spans]

        @pl.when(b == 0)
        def _():
            saved[...] = wide[0][:SPAN]

        folded = [carry[...] + wide[0][:SPAN]] + [wide[u - 1][SPAN:] + wide[u][:SPAN] for u in spans[1:]]
        straight = [waiting[...]] + direct[:-1]
        behind = jnp.concatenate([back, q[: BLOCK - SPAN]], axis=0)
        out[...] = whole(jnp.concatenate(straight, axis=0), jnp.concatenate(folded, axis=0), behind)
        carry[...] = wide[-1][SPAN:]
        waiting[...] = direct[-1]

    def step(i, c):
        b = 2 * i
        scatter(jnp.maximum(b - 1, 0), done[1])
        compute(b, done[0])
        scatter(b, done[0])
        compute(b + 1, done[1])
        return c

    lax.fori_loop(0, blocks // 2, step, 0)
    scatter(blocks - 1, done[1])
    waiting[...] = whole(waiting[...], carry[...] + saved[...], q_in[length - SPAN : length, :])
    for u in range(SPAN):
        oq[pl.ds(order[length - SPAN + u], 1), :] = waiting[u : u + 1, :]
    by_core(oq, keep, give)


def back_query(order, gd, q_in, keys):
    length = q_in.shape[0]
    half = length // 512
    return pl.pallas_call(
        back_query_kernel,
        out_shape=[sd((half, 256, DH), BF16)] * 2,
        in_specs=[pl.BlockSpec(memory_space=pltpu.SMEM)] + vm(3),
        out_specs=vm(2),
        scratch_shapes=[pltpu.VMEM((length, DH), F32)]
        + [pltpu.VMEM((SPAN, DH), F32)] * 3
        + [pltpu.VMEM((BLOCK, DH), F32)] * 2,
        compiler_params=params(),
        name="back_query",
        cost_estimate=takes(17),
    )(order, gd, q_in, keys)


def prepare(bucket_row, ends):
    length = bucket_row.shape[0]
    places = jnp.arange(length, dtype=jnp.int32)
    _, order = lax.sort((bucket_row * length + places, places), num_keys=1)
    pos = order.reshape(-1, SPAN)
    start = jnp.max(jnp.where(ends <= pos[..., None], ends, 0), axis=-1)
    window = jnp.concatenate([jnp.roll(pos, 1, 0), pos], axis=1)
    k, q = window[:, None, :], pos[:, :, None]
    bias = jnp.where((k >= start[:, :, None]) & (k <= q), jnp.where(k == q, -1000.0, 0.0), -1e9)
    return order, bias.astype(BF16).reshape(length, 2 * SPAN)


def combine_kernel(
    msg, x, w_out, gain, offset, mix, first_out, first_low, normed, weights, keep, give, low_mix, turned
):
    rows = x.shape[0]
    for half in range(2):
        logs = []
        for r in range(ROUNDS):
            lines = []
            for h in range(HEADS):
                tail = msg[h * ROUNDS + r, rows : rows + EXTRA, :].astype(F32)
                k = half * 3
                lines.append(tail[k : k + 1] + tail[k + 1 : k + 2] + tail[k + 2 : k + 3])
            logs.append(jnp.concatenate(lines, axis=0))
        top = jnp.maximum(jnp.maximum(logs[0], logs[1]), jnp.maximum(logs[2], logs[3]))
        powers = [jnp.exp(v - top) for v in logs]
        inverse = 1.0 / (powers[0] + powers[1] + powers[2] + powers[3])
        lines = [v * inverse for v in powers]
        lines.append(jnp.zeros((128 - HEADS * ROUNDS, 128), F32))
        weights[half * 128 : half * 128 + 128, :] = jnp.transpose(jnp.concatenate(lines, axis=0))
    for h in range(HEADS):
        total = jnp.zeros((rows, DH), F32)
        for r in range(ROUNDS):
            j = r * HEADS + h
            total = total + weights[:, j : j + 1] * msg[h * ROUNDS + r, 0:rows, :].astype(F32)
        mix[:, h * DH : (h + 1) * DH] = total
        low_mix[:, h * DH : (h + 1) * DH] = total.astype(BF16)
    first = x[...].astype(F32) + jnp.dot(low_mix[...], w_out[...], preferred_element_type=F32)
    first_out[...] = first
    first_low[...] = first.astype(BF16)
    normed[...] = layer_rows(first, gain[...], offset[...]).astype(BF16)
    turned[...] = jnp.transpose(mix[...]).astype(BF16)
    split_by_core(turned, keep, give)


def combine(msg, x, w_out, gain, offset):
    rows, width = x.shape
    return pl.pallas_call(
        combine_kernel,
        out_shape=[
            sd((rows, width), F32),
            sd((rows, width), F32),
            sd((rows, width), BF16),
            sd((rows, width), BF16),
            sd((rows, 128), F32),
            sd((width // 64, 32, rows), BF16),
            sd((width // 64, 32, rows), BF16),
        ],
        in_specs=vm(5),
        out_specs=vm(7),
        scratch_shapes=[pltpu.VMEM((rows, width), BF16), pltpu.VMEM((width, rows), BF16)],
        compiler_params=params(),
        name="combine",
        cost_estimate=takes(6),
    )(msg, x, w_out, gain, offset)


def anywhere(n):
    return [pl.BlockSpec(memory_space=pl.ANY)] * n


def far_copies(own, far, to, sems, first, flip, pieces):
    out = []
    for i in pieces:
        dst = to.at[(i + 1) // 2, pl.ds((i - 1) % 2 * 512, 512)] if i else to.at[0]
        src = (far[i + 5] if flip else far[i - 1]).at[pl.ds(0, 512)] if i else own
        out.append(pltpu.make_async_copy(src, dst, sems.at[first + i]))
    return out


def start_copies(copies):
    core = lax.axis_index("seq") % 2
    for side in range(2):

        @pl.when(core == side)
        def _():
            for c in copies(side == 1):
                c.start()


def wait_copies(own, far, to, sems, first, k):
    for c in far_copies(own, far, to, sems, first, False, (2 * k - 1, 2 * k) if k else (0,)):
        c.wait()


def gelu_both(act, grad):
    share = 0.5 + 0.5 * lax.erf(act * 0.7071067811865476)
    slope = share + act * (jnp.exp(act * act * -0.5) * 0.3989422804014327)
    return (act * share).astype(BF16), (grad * slope).astype(BF16)


def middle_kernel(*refs):
    normed, g_two, up0, down0, far = refs[0], refs[1], refs[2], refs[3], refs[4:16]
    grad_normed, hid, pre0, up, down, pre, sems = refs[16:]
    pieces = range(7)
    start_copies(
        lambda flip: far_copies(up0, far, up, sems, 0, flip, pieces)
        + far_copies(down0, far, down, sems, 7, not flip, pieces)
    )
    for k in range(4):
        wait_copies(up0, far, up, sems, 0, k)
        wait_copies(down0, far, down, sems, 7, k)

        def hidden_part(i, c):
            for u in range(2):
                at = pl.ds(pl.multiple_of(i * 512 + u * 256, 256), 256)
                act = jnp.dot(normed[...], up[k, :, at], preferred_element_type=F32)
                grad = jnp.dot(g_two[...], down[k, :, at], preferred_element_type=F32)
                hid[k, :, at], pre[k, :, at] = gelu_both(act, grad)
            return c

        lax.fori_loop(0, 2, hidden_part, 0)
    pre0[...] = pre[0]
    grad_normed[...] = jnp.zeros(grad_normed.shape, F32)

    def up_back(k, c):
        grad_normed[...] += lax.dot_general(pre[k], up[k], ACROSS, preferred_element_type=F32)
        return c

    lax.fori_loop(0, 4, up_back, 0)


def middle(normed, g_two, up0, down0, far):
    rows, width = normed.shape
    return pl.pallas_call(
        middle_kernel,
        out_shape=[sd((rows, width), F32), sd((4, rows, 1024), BF16), sd((rows, 1024), BF16)],
        in_specs=vm(2) + anywhere(14),
        out_specs=vm(3),
        scratch_shapes=[
            pltpu.VMEM((4, width, 1024), BF16),
            pltpu.VMEM((4, width, 1024), BF16),
            pltpu.VMEM((4, rows, 1024), BF16),
            pltpu.SemaphoreType.DMA((14,)),
        ],
        compiler_params=params(),
        name="middle",
        cost_estimate=takes(16),
    )(normed, g_two, up0, down0, *far)


def uncombine_kernel(
    grad_normed, mix, first, weights, g_one, w_out, gain, grad_first, sent, grad_gain, grad_offset, low_first
):
    rows = g_one.shape[0]
    grad_x, gg, go = layer_back(first[...], grad_normed[...], gain[...])
    grad_gain[...] = gg
    grad_offset[...] = go
    grad_x = grad_x + g_one[...].astype(F32)
    grad_first[...] = grad_x
    low_first[...] = grad_x.astype(BF16)
    lane = lax.broadcasted_iota(jnp.int32, (rows, 128), 1)
    inner = jnp.zeros((rows, 128), F32)
    for h in range(HEADS):
        at = slice(h * DH, (h + 1) * DH)
        grad_mix = lax.dot_general(low_first[...], w_out[at, :], ACROSS, preferred_element_type=F32)
        dots = jnp.sum(grad_mix * mix[:, at], axis=1, keepdims=True)
        inner = jnp.where(lane % HEADS == h, dots, inner)
        for r in range(ROUNDS):
            j = r * HEADS + h
            sent[h * ROUNDS + r, 0:rows, :] = (weights[:, j : j + 1] * grad_mix).astype(BF16)
    inner = inner * weights[...]
    low_lines = [p.astype(F32) for p in split3(jnp.transpose(inner[0:128]))]
    high_lines = [p.astype(F32) for p in split3(jnp.transpose(inner[128:256]))]
    blank = jnp.zeros((EXTRA - 6, 128), F32)
    for h in range(HEADS):
        for r in range(ROUNDS):
            j = r * HEADS + h
            tail = [p[j : j + 1] for p in low_lines + high_lines] + [blank]
            sent[h * ROUNDS + r, rows : rows + EXTRA, :] = jnp.concatenate(tail, axis=0).astype(BF16)


def uncombine(grad_normed, mix, first, weights, g_one, w_out, gain):
    rows, width = g_one.shape
    return pl.pallas_call(
        uncombine_kernel,
        out_shape=[
            sd((rows, width), F32),
            sd((HEADS * ROUNDS, rows + EXTRA, DH), BF16),
            sd((1, width), F32),
            sd((1, width), F32),
            sd((rows, width), BF16),
        ],
        in_specs=vm(7),
        out_specs=vm(5),
        compiler_params=params(),
        name="uncombine",
        cost_estimate=takes(8),
    )(grad_normed, mix, first, weights, g_one, w_out, gain)


def down_out_kernel(*refs):
    hid, x, down0, far = refs[0], refs[1], refs[2], refs[3:15]
    out, down, summed, sems = refs[15:]
    start_copies(lambda flip: far_copies(down0, far, down, sems, 0, not flip, range(7)))
    summed[...] = x[...].astype(F32)
    for k in range(4):
        wait_copies(down0, far, down, sems, 0, k)
        summed[...] += lax.dot_general(hid[k], down[k], ACROSS, preferred_element_type=F32)
    out[...] = summed[...].astype(BF16)


def down_out(hid, x, down0, far):
    rows, width = x.shape
    return pl.pallas_call(
        down_out_kernel,
        out_shape=sd((rows, width), BF16),
        in_specs=vm(2) + anywhere(13),
        out_specs=pl.BlockSpec(memory_space=pltpu.VMEM),
        scratch_shapes=[
            pltpu.VMEM((4, width, 1024), BF16),
            pltpu.VMEM((rows, width), F32),
            pltpu.SemaphoreType.DMA((7,)),
        ],
        compiler_params=params(),
        name="down_out",
        cost_estimate=takes(6),
    )(hid, x, down0, *far)


def begin(moves, sems):
    copies = [pltpu.make_async_copy(src, dst, sems.at[i]) for i, (src, dst) in enumerate(moves)]
    for c in copies:
        c.start()
    return copies


def last_rows(array, to, k):
    rows = to.shape[1]
    return (array.at[pl.ds(array.shape[0] - rows, rows)], to.at[k])


def peer_hidden(rows_in, grads_in, k, up, down, hid, pre, to):
    def hidden_part(i, c):
        for u in range(2):
            at = pl.ds(pl.multiple_of(i * 512 + u * 256, 256), 256)
            act = jnp.dot(rows_in[k], up[:, at], preferred_element_type=F32)
            grad = jnp.dot(grads_in[k], down[:, at], preferred_element_type=F32)
            hid[to, :, at], pre[to, :, at] = gelu_both(act, grad)
        return c

    lax.fori_loop(0, 2, hidden_part, 0)


def peers_kernel(*refs):
    normed, grads, ahead, behind, g1, g3, g2, weights_up, weights_down = refs[:9]
    hid, pre, turned_grads, turned_rows, rows_in, grads_in, up, down, sems = refs[9:]
    moves = [(weights_up, up), (weights_down, down)]
    moves += [(ahead, rows_in.at[1]), last_rows(g1, grads_in, 1)]
    moves += [(behind, rows_in.at[2]), last_rows(g3, grads_in, 2)]
    moves += [(normed, rows_in.at[0]), (grads, grads_in.at[0]), last_rows(g2, grads_in, 3)]
    copies = begin(moves, sems)
    for k, ready in ((1, copies[:4]), (2, copies[4:6])):
        for c in ready:
            c.wait()
        peer_hidden(rows_in, grads_in, k, up, down, hid, pre, k - 1)
    for c in copies[6:]:
        c.wait()
    count, rows, width = grads_in.shape
    turned_grads[...] = jnp.transpose(grads_in[...].reshape(count * rows, width))
    turned_rows[...] = jnp.transpose(rows_in[...].reshape((count - 1) * rows, width))


def peers(normed, grads, ahead, behind, g1, g3, g2, up, down):
    rows, width = normed.shape
    return pl.pallas_call(
        peers_kernel,
        out_shape=[sd((2, rows, 1024), BF16)] * 2 + [sd((width, 4 * rows), BF16), sd((width, 3 * rows), BF16)],
        in_specs=anywhere(9),
        out_specs=vm(4),
        scratch_shapes=[pltpu.VMEM((3, rows, 1024), BF16), pltpu.VMEM((4, rows, 1024), BF16)]
        + [pltpu.VMEM((width, 1024), BF16)] * 2
        + [pltpu.SemaphoreType.DMA((9,))],
        compiler_params=params(),
        name="peers",
        cost_estimate=takes(9),
    )(normed, grads, ahead, behind, g1, g3, g2, up, down)


def feed_kernel(*refs):
    (hid_own, pre_own, hid_near, pre_near, left_grads, left_rows, g2) = refs[:7]
    across, weights_up, weights_down, out = refs[7:11]
    rows_in, grads_in, hid, pre, up, down, turned_grads, turned_rows, sems = refs[11:]
    rows = pre_own.shape[0]
    moves = [(weights_up, up), (weights_down, down), (across, rows_in.at[0]), last_rows(g2, grads_in, 0)]
    moves += [(left_rows, turned_rows.at[:, pl.ds(0, 3 * rows)]), (pre_own, pre.at[0])]
    moves += [(pre_near, pre.at[pl.ds(1, 2)]), (left_grads, turned_grads), (hid_own.at[0], hid.at[0])]
    moves += [(hid_near, hid.at[pl.ds(1, 2)])]
    copies = begin(moves, sems)
    for c in copies[:4]:
        c.wait()
    peer_hidden(rows_in, grads_in, 0, up, down, hid, pre, 3)
    for c in copies[4:7]:
        c.wait()
    turned_rows[:, 3 * rows :] = jnp.transpose(rows_in[0])
    for first, turned, rights in ((0, turned_rows, pre), (1024, turned_grads, hid)):
        if first:
            for c in copies[7:]:
                c.wait()

        def piece(i, c):
            left = turned[pl.ds(pl.multiple_of(i * 256, 256), 256), :]
            total = jnp.dot(left, rights[...].reshape(4 * rows, 1024), preferred_element_type=F32).astype(BF16)
            for j in range(8):
                out[j * 4 + i, :, first : first + 1024] = total[j * 32 : j * 32 + 32]
            return c

        lax.fori_loop(0, 4, piece, 0)


def feed(hid_own, pre_own, hid_near, pre_near, left_grads, left_rows, g2, across, up, down):
    rows, width = pre_own.shape[0], up.shape[0]
    return pl.pallas_call(
        feed_kernel,
        out_shape=sd((width // 32, 32, 2048), BF16),
        in_specs=anywhere(10),
        out_specs=pl.BlockSpec(memory_space=pltpu.VMEM),
        scratch_shapes=[pltpu.VMEM((1, rows, 1024), BF16)] * 2
        + [pltpu.VMEM((4, rows, 1024), BF16)] * 2
        + [pltpu.VMEM((width, 1024), BF16)] * 2
        + [pltpu.VMEM((width, 4 * rows), BF16)] * 2
        + [pltpu.SemaphoreType.DMA((10,))],
        compiler_params=params(),
        name="feed",
        cost_estimate=takes(12),
    )(hid_own, pre_own, hid_near, pre_near, left_grads, left_rows, g2, across, up, down)


def sum_rounds_kernel(back, out):
    for h in range(HEADS):
        total = back[2 * h].astype(F32) + back[2 * h + 1].astype(F32)
        for half in range(2):
            at = slice(half * HEADS * DH + h * DH, half * HEADS * DH + (h + 1) * DH)
            out[:, at] = total[:, half * DH : (half + 1) * DH].astype(BF16)


def sum_rounds(back):
    rows = back.shape[1]
    return pl.pallas_call(
        sum_rounds_kernel,
        out_shape=sd((rows, 2 * HEADS * DH), BF16),
        in_specs=vm(1),
        out_specs=pl.BlockSpec(memory_space=pltpu.VMEM),
        compiler_params=params(),
        name="sum_rounds",
        cost_estimate=takes(3),
    )(back)


def finish_kernel(grads, x, gain, w_qk, w_value, grad_two, gain_two, offset_two, grad_second, small, near, far):
    width = x.shape[1]
    grad_normed = lax.dot_general(grads[:, :width], w_qk[...], ACROSS, preferred_element_type=F32)
    grad_normed = grad_normed + lax.dot_general(grads[:, width:], w_value[...], ACROSS, preferred_element_type=F32)
    grad_x, gg, go = layer_back(x[...].astype(F32), grad_normed, gain[...])
    grad_second[...] = grad_x + grad_two[...].astype(F32)
    lines = []
    for line in (gg, go, gain_two[...], offset_two[...]):
        high = line.astype(BF16).astype(F32)
        lines += [high, line - high]
    blank = jnp.zeros((8, width), F32)
    rest = jnp.zeros((112, width), F32)
    near[...] = jnp.transpose(jnp.concatenate(lines + [blank, rest], axis=0))
    far[...] = jnp.transpose(jnp.concatenate([blank] + lines + [rest], axis=0))
    core = lax.axis_index("seq") % 2
    for j in range(small.shape[0]):
        a = near[pl.ds(pl.multiple_of(j * 64 + core * 32, 32), 32), :]
        b = far[pl.ds(pl.multiple_of(j * 64 + (1 - core) * 32, 32), 32), :]
        small[j] = (a + b).astype(BF16)


def finish(grads, x, gain, w_qk, w_value, grad_two, gain_two, offset_two):
    rows, width = x.shape
    return pl.pallas_call(
        finish_kernel,
        out_shape=[sd((rows, width), F32), sd((width // 64, 32, 128), BF16)],
        in_specs=vm(8),
        out_specs=vm(2),
        scratch_shapes=[pltpu.VMEM((width, 128), F32)] * 2,
        compiler_params=params(),
        name="finish",
        cost_estimate=takes(5),
    )(grads, x, gain, w_qk, w_value, grad_two, gain_two, offset_two)


def pair_kernel(left, left_other, right, right_other, *rest):
    blocks, lines, rows = left.shape
    out, width = rest[-1], right.shape[1]
    total = jnp.dot(left[...].reshape(blocks * lines, rows), right[...], preferred_element_type=F32)
    total = total + jnp.dot(left_other[...].reshape(blocks * lines, rows), right_other[...], preferred_element_type=F32)
    out[:, :, :width] = total.astype(BF16).reshape(blocks, lines, width)
    for extra in rest[:-1]:
        out[:, :, width : width + extra.shape[2]] = extra[...]
        width += extra.shape[2]


def pair(left, left_other, right, right_other, *extra):
    blocks, lines, rows = left.shape
    width = right.shape[1] + sum(e.shape[2] for e in extra)
    return pl.pallas_call(
        pair_kernel,
        out_shape=sd((blocks, lines, width), BF16),
        in_specs=vm(4 + len(extra)),
        out_specs=pl.BlockSpec(memory_space=pltpu.VMEM),
        compiler_params=params(),
        name="pair",
        cost_estimate=takes(3),
    )(left, left_other, right, right_other, *extra)


def swap_seq(array):
    return lax.all_to_all(array, "seq", split_axis=0, concat_axis=0, tiled=True)


def same_core():
    count = lax.axis_size("seq")
    return [list(range(c, count, 2)) for c in range(2)]


def along_x_and_core():
    return [[y * 8 + x * 2 + c for x in range(4) for c in range(2)] for y in range(4)]


def along_y():
    return [[y * 8 + x * 2 + c for y in range(4)] for x in range(4) for c in range(2)]


def swap_chips(array):
    return lax.all_to_all(
        array, "seq", split_axis=0, concat_axis=0, tiled=True, axis_index_groups=same_core()
    )


def flip_bit(array, axis, bit):
    return lax.ppermute(array, axis, [(i, i ^ bit) for i in range(lax.axis_size(axis))])


def swap_cores(array):
    return flip_bit(array, "seq", 1)


def from_ahead(array, step):
    count = lax.axis_size("ffn")
    return lax.ppermute(array, "ffn", [((i + step) % count, i) for i in range(count)])


def tied(array, *others):
    return lax.optimization_barrier((array, others))[0]


def add_low(a, b):
    return (a.astype(F32) + b.astype(F32)).astype(BF16)


def shards(
    stream_one,
    stream_two,
    doc_lengths,
    bucket_ids,
    norm1_gain,
    norm1_bias,
    w_qk,
    w_value,
    w_out,
    norm2_gain,
    norm2_bias,
    w_up,
    w_down,
    grad_out_one,
    grad_out_two,
):
    rows, width = stream_one.shape[1:]
    seq, ffn = lax.axis_index("seq"), lax.axis_index("ffn")
    core = seq % 2
    gain_one, bias_one = norm1_gain.reshape(1, -1), norm1_bias.reshape(1, -1)
    gain_two, bias_two = norm2_gain.reshape(1, -1), norm2_bias.reshape(1, -1)

    msg, normed_one, keep_rows, give_rows = project(stream_two[0], gain_one, bias_one, w_qk, w_value)
    received = swap_chips(msg)
    top, low = [jnp.where(core == 0, w_up[at], w_down[at]) for at in (slice(0, 512), slice(512, 1024))]
    buckets, top, low = lax.optimization_barrier((bucket_ids[0, 0], top, low))
    top1, low3 = from_ahead(top, 1), from_ahead(low, 3)
    order, bias = prepare(buckets, jnp.cumsum(doc_lengths[0]))
    received, order, bias, top, low, top1, low3 = lax.optimization_barrier(
        (received, order, bias, top, low, top1, low3)
    )
    came = swap_cores(received)
    lowg1 = from_ahead(jnp.concatenate([low, grad_out_two[0]], axis=0), 1)
    topg3 = from_ahead(jnp.concatenate([top, grad_out_two[0]], axis=0), 3)
    other_rows = swap_cores(give_rows)
    top1_other, low3_other = swap_cores(top1), swap_cores(low3)
    sent, queries, keys, vals, probs = attend(order, received, came, bias)
    sent, top1, low3, lowg1, topg3, top1_other, low3_other, other_rows = lax.optimization_barrier(
        (sent, top1, low3, lowg1, topg3, top1_other, low3_other, other_rows)
    )
    per_round = swap_seq(sent)
    top2, low2 = from_ahead(top1, 1), from_ahead(low3, 3)
    lowg1_other, topg3_other = swap_cores(lowg1), swap_cores(topg3)
    per_round, top2, low2, lowg1_other, topg3_other = lax.optimization_barrier(
        (per_round, top2, low2, lowg1_other, topg3_other)
    )
    far_weights = [top1, lowg1, top2, low2, topg3, low3]
    far_weights += [top1_other, lowg1_other, swap_cores(top2), swap_cores(low2), topg3_other, low3_other]
    grads2 = from_ahead(topg3[512:], 3)
    mix, first, one_low, normed_two, weights, keep_mix, give_mix = combine(per_round, stream_one[0], w_out, gain_two, bias_two)
    ahead, behind = from_ahead(normed_two, 1), from_ahead(normed_two, 3)
    grad_normed, hid, pre0 = middle(normed_two, grad_out_two[0], w_up, w_down, far_weights)
    grad_normed, ahead, behind, grads2 = lax.optimization_barrier((grad_normed, ahead, behind, grads2))
    across = from_ahead(ahead, 1)
    grad_first, msg, grad_gain_two, grad_bias_two, low_first = uncombine(
        grad_normed, mix, first, weights, grad_out_one[0], w_out, gain_two
    )
    far = swap_seq(msg)
    part_out = pair(keep_mix, swap_cores(give_mix), low_first, swap_cores(low_first))
    peer_parts = peers(normed_two, grad_out_two[0], ahead, behind, lowg1, topg3, grads2, w_up, w_down)
    peer_parts, part_out = lax.optimization_barrier((peer_parts, part_out))
    part_out = part_out.reshape(-1, 4, 8, width)
    part_feed = feed(hid, pre0, *peer_parts, grads2, across, w_up, w_down)
    far, part_feed, part_out = lax.optimization_barrier((far, part_feed, part_out))
    keep_v, give_v, grad_dots = back_value(order, far, vals, probs)
    keep_q, give_q = back_query(order, grad_dots, queries, keys)
    near_feed = part_feed.reshape(-1, part_feed.shape[2])
    near_feed = lax.psum_scatter(near_feed, "seq", tiled=True, axis_index_groups=along_x_and_core())
    keep_q, give_q, near_feed = lax.optimization_barrier((keep_q, give_q, near_feed))
    near_feed = lax.psum_scatter(near_feed, "seq", tiled=True, axis_index_groups=along_y())
    part_out = tied(part_out, keep_q)
    blocks = [
        from_ahead(lax.dynamic_index_in_dim(part_out, (ffn + 4 - k) % 4, 1, keepdims=False), k) for k in (1, 2, 3)
    ]
    came_v, came_q = swap_cores(give_v), swap_cores(give_q)
    back = swap_chips(jnp.concatenate([add_low(keep_q, came_q), add_low(keep_v, came_v)], axis=2))
    sums_out = lax.dynamic_index_in_dim(part_out, ffn, 1, keepdims=False).astype(F32)
    for block in blocks:
        sums_out = sums_out + block.astype(F32)
    sums_out = sums_out.astype(BF16).reshape(-1, 32, width // 4)
    back, sums_out, near_feed = lax.optimization_barrier((back, sums_out, near_feed))
    hid = tied(hid, keep_q)
    two_low = down_out(hid, stream_two[0], w_down, far_weights)
    grads = sum_rounds(back)
    grads_other = swap_cores(grads)
    grad_second, small = finish(
        grads, stream_two[0], gain_one, w_qk, w_value, grad_out_two[0], grad_gain_two, grad_bias_two
    )
    part = pair(keep_rows, other_rows, grads, grads_other, small, sums_out)
    near = swap_chips(part)
    near, near_feed = lax.optimization_barrier((near, near_feed))
    near = near.astype(F32).sum(axis=0)
    near, near_out = near[:, : 2 * width + 128].reshape(4, 8, -1), near[:, 2 * width + 128 :]
    whole = lax.dynamic_index_in_dim(near, ffn, 0, keepdims=False)
    for k in (1, 2, 3):
        whole = whole + from_ahead(lax.dynamic_index_in_dim(near, (ffn + 4 - k) % 4, 0, keepdims=False), k)
    small = whole[:, 2 * width :]
    lines = small[:, :8] + swap_cores(small)[:, 8:16]
    lines = lines[:, 0::2] + lines[:, 1::2]
    near_feed = near_feed.astype(F32)
    return (
        one_low[None],
        two_low[None],
        grad_first[None],
        grad_second[None],
        lines[:, 0],
        lines[:, 1],
        whole[:, :width],
        whole[:, width : 2 * width],
        near_out.reshape(8, width),
        lines[:, 2],
        lines[:, 3],
        near_feed[:, :1024],
        near_feed[:, 1024:2048],
    )


def solution(mesh):
    return jax.shard_map(
        shards,
        mesh=mesh,
        in_specs=(
            P("ffn", "seq", None),
            P("ffn", "seq", None),
            P("ffn", None),
            P("ffn", "seq", None),
            P(),
            P(),
            P(),
            P(),
            P(),
            P(),
            P(),
            P(None, "ffn"),
            P(None, "ffn"),
            P("ffn", "seq", None),
            P("ffn", "seq", None),
        ),
        out_specs=(
            P("ffn", "seq", None),
            P("ffn", "seq", None),
            P("ffn", "seq", None),
            P("ffn", "seq", None),
            P(("seq", "ffn")),
            P(("seq", "ffn")),
            P(("seq", "ffn"), None),
            P(("seq", "ffn"), None),
            P(("seq", "ffn"), None),
            P(("seq", "ffn")),
            P(("seq", "ffn")),
            P("seq", "ffn"),
            P("seq", "ffn"),
        ),
        check_vma=False,
    )
```

```python
import jax
import jax.numpy as jnp
from jax import lax
from jax.experimental import pallas as pl
from jax.experimental.pallas import tpu as pltpu
from jax.sharding import PartitionSpec as P

HEADS = 8
DH = 128
ROUNDS = 4
SPAN = 64
EPS_NORM = 1e-05
EPS_KEY = 1e-06
SELF_PENALTY = 1000.0
SCALE = DH ** (-0.5)
EXTRA = 16
F32, BF16 = jnp.float32, jnp.bfloat16
ACROSS = (((1,), (1,)), ((), ()))
FLIP = (((0,), (0,)), ((), ()))


def vm(n):
    return [pl.BlockSpec(memory_space=pltpu.VMEM)] * n


def anywhere(n):
    return [pl.BlockSpec(memory_space=pl.ANY)] * n


def sd(shape, kind):
    return jax.ShapeDtypeStruct(shape, kind)


def params(mebibytes):
    return pltpu.CompilerParams(vmem_limit_bytes=mebibytes * 2**20)


def takes(us):
    return pl.CostEstimate(flops=0, transcendentals=0, bytes_accessed=int(us * 3.5e6))


def split3(x):
    a = x.astype(BF16)
    r = x - a.astype(F32)
    b = r.astype(BF16)
    c = (r - b.astype(F32)).astype(BF16)
    return a, b, c


def layer_rows(x, gain, offset):
    centred = x - jnp.mean(x, axis=1, keepdims=True)
    inverse = lax.rsqrt(jnp.mean(centred * centred, axis=1, keepdims=True) + EPS_NORM)
    return centred * inverse * gain + offset


def layer_back(x, grad, gain):
    centred = x - jnp.mean(x, axis=1, keepdims=True)
    inverse = lax.rsqrt(jnp.mean(centred * centred, axis=1, keepdims=True) + EPS_NORM)
    unit = centred * inverse
    grad_gain = jnp.sum(grad * unit, axis=0, keepdims=True)
    grad_offset = jnp.sum(grad, axis=0, keepdims=True)
    scaled = grad * gain
    inner = jnp.mean(scaled * unit, axis=1, keepdims=True)
    grad_x = inverse * (scaled - jnp.mean(scaled, axis=1, keepdims=True) - unit * inner)
    return grad_x, grad_gain, grad_offset


def split_by_core(turned, keep, give):
    core = lax.axis_index("seq") % 2
    for j in range(keep.shape[0]):
        keep[j] = turned[pl.ds(pl.multiple_of(j * 64 + core * 32, 32), 32), :]
        give[j] = turned[pl.ds(pl.multiple_of(j * 64 + (1 - core) * 32, 32), 32), :]


def project_kernel(x, gain, offset, w_qk, w_value, msg, normed_out, keep, give, turned):
    normed = layer_rows(x[...].astype(F32), gain[...], offset[...])
    low = normed.astype(BF16)
    normed_out[...] = low
    for h in range(HEADS):
        at = slice(h * DH, (h + 1) * DH)
        q = jnp.dot(low, w_qk[:, at], preferred_element_type=F32).astype(BF16)
        v = jnp.dot(low, w_value[:, at], preferred_element_type=F32).astype(BF16)
        for t in range(2):
            msg[h * 2 + t, :, :DH] = q
            msg[h * 2 + t, :, DH:] = v
    turned[...] = jnp.transpose(low.astype(F32)).astype(BF16)
    split_by_core(turned, keep, give)


def project(x, gain, offset, w_qk, w_value):
    rows, width = x.shape
    chips = 2 * HEADS
    return pl.pallas_call(
        project_kernel,
        out_shape=[
            sd((chips, rows, 2 * DH), BF16),
            sd((rows, width), BF16),
            sd((width // 64, 32, rows), BF16),
            sd((width // 64, 32, rows), BF16),
        ],
        in_specs=vm(5),
        out_specs=vm(4),
        scratch_shapes=[pltpu.VMEM((width, rows), BF16)],
        compiler_params=params(60),
        name="project",
        cost_estimate=takes(7),
    )(x, gain, offset, w_qk, w_value)


BLOCK = 8 * SPAN
SAFE = 60.0


def repeat(count, body, width=4):
    def several(i, c):
        for u in range(width):
            body(i * width + u)
        return c

    lax.fori_loop(0, count // width, several, 0)


def even(first, count):
    return pl.ds(2 * first, count, stride=2)


def odd(first, count):
    return pl.ds(2 * first + 1, count, stride=2)


def gather_pairs(order, base, src, slot):
    for u in range(BLOCK):
        place = 2 * order[base + u]
        slot[2 * u : 2 * u + 1, :] = src[pl.ds(place, 1), :]
        slot[2 * u + 1 : 2 * u + 2, :] = src[pl.ds(place + 1, 1), :]


def scatter_pairs(order, base, slot, dst):
    for u in range(BLOCK):
        dst[pl.ds(pl.multiple_of(2 * order[base + u], 2), 2), :] = slot[2 * u : 2 * u + 2, :]


def attend_kernel(order, mine, other, bias_in, msg, q_far, keys_far, vals_far, probs_far, came_all, sent_all, *rest):
    slots, (q_out, keys, vals, probs, bias, sems) = rest[:4], rest[4:]
    load = pltpu.make_async_copy(bias_in, bias, sems.at[0])
    load.start()
    length = q_out.shape[0]
    blocks = length // BLOCK
    core = lax.axis_index("seq") % 2
    came, done = slots[0:2], slots[2:4]

    def widen(j):
        for rows, side in ((mine, core), (other, 1 - core)):
            first = pl.multiple_of((2 * j + side) * 256, 256)
            came_all[even(first, 256), :] = rows[j, :, :DH].astype(F32)
            came_all[odd(first, 256), :] = rows[j, :, DH:].astype(F32)

    repeat(length // 512, widen, 2)

    def gather(b, slot):
        gather_pairs(order, b * BLOCK, came_all, slot)

    def scatter(b, slot):
        scatter_pairs(order, b * BLOCK, slot, sent_all)

    def ready(b, slot):
        q = slot[even(0, BLOCK), :]
        unit = q * lax.rsqrt(jnp.sum(q * q, axis=1, keepdims=True) + EPS_KEY)
        ahead = pl.ds(pl.multiple_of(b * BLOCK + SPAN, SPAN), BLOCK)
        keys[ahead, :] = unit.astype(BF16)
        vals[ahead, :] = slot[odd(0, BLOCK), :].astype(BF16)
        return q.astype(BF16)

    load.wait()
    gather(blocks - 1, came[1])
    ready(blocks - 1, came[1])
    keys[0:SPAN, :] = keys[length : length + SPAN, :]
    vals[0:SPAN, :] = vals[length : length + SPAN, :]
    gather(0, came[0])

    def compute(b, slot, out):
        base = pl.multiple_of(b * BLOCK, BLOCK)
        q = ready(b, slot)
        q_out[pl.ds(base, BLOCK), :] = q
        k = keys[pl.ds(base, BLOCK + SPAN), :]
        v = vals[pl.ds(base, BLOCK + SPAN), :]
        spans = range(BLOCK // SPAN)
        s = [
            lax.dot_general(
                q[u * SPAN : u * SPAN + SPAN], k[u * SPAN : u * SPAN + 2 * SPAN], ACROSS, preferred_element_type=F32
            )
            for u in spans
        ]
        s = jnp.concatenate(s, axis=0) * SCALE + bias[pl.ds(base, BLOCK), :].astype(F32)
        top = jnp.max(s, axis=1, keepdims=True)
        e = jnp.exp(s - top)
        total = jnp.sum(e, axis=1, keepdims=True)
        p = (e * (1.0 / total)).astype(BF16)
        probs[pl.ds(base, BLOCK), :] = p
        for u in spans:
            out[even(u * SPAN, SPAN), :] = jnp.dot(
                p[u * SPAN : u * SPAN + SPAN], v[u * SPAN : u * SPAN + 2 * SPAN], preferred_element_type=F32
            )
        out[odd(0, BLOCK), :] = jnp.broadcast_to(top + jnp.log(total), (BLOCK, DH))

    def step(i, c):
        b = 2 * i
        scatter(jnp.maximum(b - 1, 0), done[1])
        gather(b + 1, came[1])
        compute(b, came[0], done[0])
        scatter(b, done[0])
        gather(jnp.minimum(b + 2, blocks - 1), came[0])
        compute(b + 1, came[1], done[1])
        return c

    lax.fori_loop(0, blocks // 2, step, 0)
    pairs = ((q_out, q_far), (keys, keys_far), (vals, vals_far), (probs, probs_far))
    stores = [pltpu.make_async_copy(src, dst, sems.at[1 + n]) for n, (src, dst) in enumerate(pairs)]
    for store in stores:
        store.start()
    scatter(blocks - 1, done[1])

    across = lax.broadcasted_iota(jnp.int32, (128, 128), 0)
    eye = across == lax.broadcasted_iota(jnp.int32, (128, 128), 1)

    line = lax.broadcasted_iota(jnp.int32, (EXTRA, 6 * 128), 0)
    lane = lax.broadcasted_iota(jnp.int32, (EXTRA, 6 * 128), 1)
    pick = jnp.where(line == lane // 128, 1.0, 0.0).astype(BF16)

    def send(b):
        msg[b, 0:256, :] = sent_all[even(b * 256, 256), :].astype(BF16)
        parts = []
        for half in range(2):
            parts += split3(jnp.where(eye, sent_all[odd(b * 256 + half * 128, 128), :], 0.0))
        tail = jnp.dot(pick, jnp.concatenate(parts, axis=0), preferred_element_type=F32)
        msg[b, 256:, :] = tail.astype(BF16)

    repeat(length // 256, send)
    for store in stores:
        store.wait()


def attend(order, mine, other, bias):
    length = order.shape[0]
    kept = [(length, DH), (length + SPAN, DH), (length + SPAN, DH), (length, DH)]
    return pl.pallas_call(
        attend_kernel,
        out_shape=[sd((length // 256, 256 + EXTRA, DH), BF16)] + [sd(shape, BF16) for shape in kept],
        in_specs=[pl.BlockSpec(memory_space=pltpu.SMEM)] + vm(2) + anywhere(1),
        out_specs=vm(1) + anywhere(4),
        scratch_shapes=[pltpu.VMEM((2 * length, DH), F32)] * 2
        + [pltpu.VMEM((2 * BLOCK, DH), F32)] * 4
        + [pltpu.VMEM(shape, BF16) for shape in kept]
        + [pltpu.VMEM((length, 2 * SPAN), BF16), pltpu.SemaphoreType.DMA((5,))],
        compiler_params=params(60),
        name="attend",
        cost_estimate=takes(35),
    )(order, mine, other, bias)


def back_kernel(order, msg, *refs):
    far, (keep, give, came_all, sent_all, first_u, first_v, late), slots = refs[:4], refs[4:11], refs[11:15]
    near, sems = refs[15:19], refs[19]
    q_in, keys, vals, probs = near
    loads = [pltpu.make_async_copy(src, dst, sems.at[n]) for n, (src, dst) in enumerate(zip(far, near))]
    for load in loads:
        load.start()
    length = probs.shape[0]
    blocks = length // BLOCK
    core = lax.axis_index("seq") % 2
    came, done = slots[0:2], slots[2:4]
    late_u, late_v, late_q = late.at[0], late.at[1], late.at[2]
    across = lax.broadcasted_iota(jnp.int32, (128, 128), 0)
    eye = across == lax.broadcasted_iota(jnp.int32, (128, 128), 1)
    ones = jnp.ones((128, 128), BF16)

    def widen(b):
        came_all[even(b * 256, 256), :] = msg[b, 0:256, :].astype(F32)
        t = msg[b, 256:, :].astype(F32)
        for half in range(2):
            total = jnp.zeros((128, 128), F32)
            for k in range(3):
                row = half * 3 + k
                spot = jnp.where(eye, jnp.broadcast_to(t[row : row + 1], (128, 128)), 0.0).astype(BF16)
                total = total + jnp.dot(spot, ones, preferred_element_type=F32)
            came_all[odd(b * 256 + half * 128, 128), :] = total

    repeat(length // 256, widen)

    def scatter(b, slot):
        base = jnp.where(b == 0, length, b * BLOCK) - SPAN
        for u in range(BLOCK):
            if u == SPAN:
                base = b * BLOCK - SPAN
            sent_all[pl.ds(pl.multiple_of(2 * order[base + u], 2), 2), :] = slot[2 * u : 2 * u + 2, :]

    gather_pairs(order, 0, came_all, came[0])
    for load in loads:
        load.wait()
    late[...] = jnp.zeros(late.shape, F32)
    spans = range(BLOCK // SPAN)
    cut = lambda a, u, n=1: a[u * SPAN : (u + n) * SPAN]

    def whole(direct, unit_grad, q):
        q = q.astype(F32)
        r = lax.rsqrt(jnp.sum(q * q, axis=1, keepdims=True) + EPS_KEY)
        along = jnp.sum(q * unit_grad, axis=1, keepdims=True)
        return direct + r * unit_grad - q * (r * r * r * along)

    def compute(b, slot, out):
        base = pl.multiple_of(b * BLOCK, BLOCK)
        g = slot[even(0, BLOCK), :].astype(BF16)
        p = probs[pl.ds(base, BLOCK), :]
        v = vals[pl.ds(base, BLOCK + SPAN), :]
        k = keys[pl.ds(base, BLOCK + SPAN), :]
        q = q_in[pl.ds(base, BLOCK), :]
        back = q_in[pl.ds(pl.multiple_of(jnp.maximum(base - SPAN, 0), SPAN), SPAN), :]
        gp = [lax.dot_general(cut(g, u), cut(v, u, 2), ACROSS, preferred_element_type=F32) for u in spans]
        wide_v = [lax.dot_general(cut(p, u), cut(g, u), FLIP, preferred_element_type=F32) for u in spans]
        gs = p.astype(F32) * (jnp.concatenate(gp, axis=0) - slot[odd(0, BLOCK), :])
        d = (gs * SCALE).astype(BF16)
        direct = [jnp.dot(cut(d, u), cut(k, u, 2), preferred_element_type=F32) for u in spans]
        wide_u = [lax.dot_general(cut(d, u), cut(q, u), FLIP, preferred_element_type=F32) for u in spans]

        @pl.when(b == 0)
        def _():
            first_u[...] = wide_u[0][:SPAN]
            first_v[...] = wide_v[0][:SPAN]

        folded_u = [late_u[...] + wide_u[0][:SPAN]] + [wide_u[u - 1][SPAN:] + wide_u[u][:SPAN] for u in spans[1:]]
        folded_v = [late_v[...] + wide_v[0][:SPAN]] + [wide_v[u - 1][SPAN:] + wide_v[u][:SPAN] for u in spans[1:]]
        straight = jnp.concatenate([late_q[...]] + direct[:-1], axis=0)
        behind = jnp.concatenate([back, q[: BLOCK - SPAN]], axis=0)
        out[even(0, BLOCK), :] = whole(straight, jnp.concatenate(folded_u, axis=0), behind)
        out[odd(0, BLOCK), :] = jnp.concatenate(folded_v, axis=0)
        late_u[...] = wide_u[-1][SPAN:]
        late_v[...] = wide_v[-1][SPAN:]
        late_q[...] = direct[-1]

    def step(i, c):
        b = 2 * i
        scatter(jnp.maximum(b - 1, 0), done[1])
        gather_pairs(order, (b + 1) * BLOCK, came_all, came[1])
        compute(b, came[0], done[0])
        scatter(b, done[0])
        gather_pairs(order, jnp.minimum(b + 2, blocks - 1) * BLOCK, came_all, came[0])
        compute(b + 1, came[1], done[1])
        return c

    lax.fori_loop(0, blocks // 2, step, 0)
    scatter(blocks - 1, done[1])
    done[0][even(0, SPAN), :] = whole(late_q[...], late_u[...] + first_u[...], q_in[length - SPAN : length, :])
    done[0][odd(0, SPAN), :] = late_v[...] + first_v[...]
    for u in range(SPAN):
        place = 2 * order[length - SPAN + u]
        sent_all[pl.ds(place, 1), :] = done[0][2 * u : 2 * u + 1, :]
        sent_all[pl.ds(place + 1, 1), :] = done[0][2 * u + 1 : 2 * u + 2, :]

    def narrow(j):
        for out, side in ((keep, core), (give, 1 - core)):
            first = pl.multiple_of((2 * j + side) * 256, 256)
            out[j, :, :DH] = sent_all[even(first, 256), :].astype(BF16)
            out[j, :, DH:] = sent_all[odd(first, 256), :].astype(BF16)

    repeat(keep.shape[0], narrow)


def attend_back(order, msg, q_in, keys, vals, probs):
    length = probs.shape[0]
    half = length // 512
    kept = [array.shape for array in (q_in, keys, vals, probs)]
    return pl.pallas_call(
        back_kernel,
        out_shape=[sd((half, 256, 2 * DH), BF16)] * 2,
        in_specs=[pl.BlockSpec(memory_space=pltpu.SMEM)] + vm(1) + anywhere(4),
        out_specs=vm(2),
        scratch_shapes=[pltpu.VMEM((2 * length, DH), F32)] * 2
        + [pltpu.VMEM((SPAN, DH), F32)] * 2
        + [pltpu.VMEM((3, SPAN, DH), F32)]
        + [pltpu.VMEM((2 * BLOCK, DH), F32)] * 4
        + [pltpu.VMEM(shape, BF16) for shape in kept]
        + [pltpu.SemaphoreType.DMA((4,))],
        compiler_params=params(60),
        name="attend_back",
        cost_estimate=takes(36),
    )(order, msg, q_in, keys, vals, probs)


def prepare(bucket_row, ends):
    length = bucket_row.shape[0]
    places = jnp.arange(length, dtype=jnp.int32)
    _, order = lax.sort((bucket_row * length + places, places), num_keys=1)
    pos = order.reshape(-1, SPAN)
    start = jnp.max(jnp.where(ends <= pos[..., None], ends, 0), axis=-1)
    window = jnp.concatenate([jnp.roll(pos, 1, 0), pos], axis=1)
    k, q = window[:, None, :], pos[:, :, None]
    bias = jnp.where((k >= start[:, :, None]) & (k <= q), jnp.where(k == q, -1000.0, 0.0), -1e9)
    return order, bias.astype(BF16).reshape(length, 2 * SPAN)


def combine_kernel(
    msg, x, w_out, gain, offset, mix, first_out, first_low, normed, weights, keep, give, low_mix, turned
):
    rows = x.shape[0]
    for half in range(2):
        logs = []
        for r in range(ROUNDS):
            lines = []
            for h in range(HEADS):
                tail = msg[h * ROUNDS + r, rows : rows + EXTRA, :].astype(F32)
                k = half * 3
                lines.append(tail[k : k + 1] + tail[k + 1 : k + 2] + tail[k + 2 : k + 3])
            logs.append(jnp.concatenate(lines, axis=0))
        top = jnp.maximum(jnp.maximum(logs[0], logs[1]), jnp.maximum(logs[2], logs[3]))
        powers = [jnp.exp(v - top) for v in logs]
        inverse = 1.0 / (powers[0] + powers[1] + powers[2] + powers[3])
        lines = [v * inverse for v in powers]
        lines.append(jnp.zeros((128 - HEADS * ROUNDS, 128), F32))
        weights[half * 128 : half * 128 + 128, :] = jnp.transpose(jnp.concatenate(lines, axis=0))
    for h in range(HEADS):
        total = jnp.zeros((rows, DH), F32)
        for r in range(ROUNDS):
            j = r * HEADS + h
            total = total + weights[:, j : j + 1] * msg[h * ROUNDS + r, 0:rows, :].astype(F32)
        mix[:, h * DH : (h + 1) * DH] = total
        low_mix[:, h * DH : (h + 1) * DH] = total.astype(BF16)
    first = x[...].astype(F32) + jnp.dot(low_mix[...], w_out[...], preferred_element_type=F32)
    first_out[...] = first
    first_low[...] = first.astype(BF16)
    normed[...] = layer_rows(first, gain[...], offset[...]).astype(BF16)
    turned[...] = jnp.transpose(mix[...]).astype(BF16)
    split_by_core(turned, keep, give)


def combine(msg, x, w_out, gain, offset):
    rows, width = x.shape
    return pl.pallas_call(
        combine_kernel,
        out_shape=[
            sd((rows, width), F32),
            sd((rows, width), F32),
            sd((rows, width), BF16),
            sd((rows, width), BF16),
            sd((rows, 128), F32),
            sd((width // 64, 32, rows), BF16),
            sd((width // 64, 32, rows), BF16),
        ],
        in_specs=vm(5),
        out_specs=vm(7),
        scratch_shapes=[pltpu.VMEM((rows, width), BF16), pltpu.VMEM((width, rows), BF16)],
        compiler_params=params(60),
        name="combine",
        cost_estimate=takes(6),
    )(msg, x, w_out, gain, offset)


def far_copies(own, far, to, sems, first, flip, pieces):
    out = []
    for i in pieces:
        dst = to.at[(i + 1) // 2, pl.ds((i - 1) % 2 * 512, 512)] if i else to.at[0]
        src = (far[i + 5] if flip else far[i - 1]).at[pl.ds(0, 512)] if i else own
        out.append(pltpu.make_async_copy(src, dst, sems.at[first + i]))
    return out


def start_copies(copies):
    core = lax.axis_index("seq") % 2
    for side in range(2):

        @pl.when(core == side)
        def _():
            for c in copies(side == 1):
                c.start()


def wait_copies(own, far, to, sems, first, k):
    for c in far_copies(own, far, to, sems, first, False, (2 * k - 1, 2 * k) if k else (0,)):
        c.wait()


def gelu_both(act, grad):
    share = 0.5 + 0.5 * lax.erf(act * 0.7071067811865476)
    slope = share + act * (jnp.exp(act * act * -0.5) * 0.3989422804014327)
    return (act * share).astype(BF16), (grad * slope).astype(BF16)


def middle_kernel(*refs):
    normed, g_two, up0, down0, far = refs[0], refs[1], refs[2], refs[3], refs[4:16]
    grad_normed, hid, pre0, up, down, pre, sems = refs[16:]
    pieces = range(7)
    start_copies(
        lambda flip: far_copies(up0, far, up, sems, 0, flip, pieces)
        + far_copies(down0, far, down, sems, 7, not flip, pieces)
    )
    for k in range(4):
        wait_copies(up0, far, up, sems, 0, k)
        wait_copies(down0, far, down, sems, 7, k)

        def hidden_part(i, c):
            for u in range(2):
                at = pl.ds(pl.multiple_of(i * 512 + u * 256, 256), 256)
                act = jnp.dot(normed[...], up[k, :, at], preferred_element_type=F32)
                grad = jnp.dot(g_two[...], down[k, :, at], preferred_element_type=F32)
                hid[k, :, at], pre[k, :, at] = gelu_both(act, grad)
            return c

        lax.fori_loop(0, 2, hidden_part, 0)
    pre0[...] = pre[0]
    grad_normed[...] = jnp.zeros(grad_normed.shape, F32)

    def up_back(k, c):
        grad_normed[...] += lax.dot_general(pre[k], up[k], ACROSS, preferred_element_type=F32)
        return c

    lax.fori_loop(0, 4, up_back, 0)


def middle(normed, g_two, up0, down0, far):
    rows, width = normed.shape
    return pl.pallas_call(
        middle_kernel,
        out_shape=[sd((rows, width), F32), sd((4, rows, 1024), BF16), sd((rows, 1024), BF16)],
        in_specs=vm(2) + anywhere(14),
        out_specs=vm(3),
        scratch_shapes=[
            pltpu.VMEM((4, width, 1024), BF16),
            pltpu.VMEM((4, width, 1024), BF16),
            pltpu.VMEM((4, rows, 1024), BF16),
            pltpu.SemaphoreType.DMA((14,)),
        ],
        compiler_params=params(28),
        name="middle",
        cost_estimate=takes(16),
    )(normed, g_two, up0, down0, *far)


def uncombine_kernel(
    grad_normed, mix, first, weights, g_one, w_out, gain, grad_first, sent, grad_gain, grad_offset, low_first
):
    rows = g_one.shape[0]
    grad_x, gg, go = layer_back(first[...], grad_normed[...], gain[...])
    grad_gain[...] = gg
    grad_offset[...] = go
    grad_x = grad_x + g_one[...].astype(F32)
    grad_first[...] = grad_x
    low_first[...] = grad_x.astype(BF16)
    lane = lax.broadcasted_iota(jnp.int32, (rows, 128), 1)
    inner = jnp.zeros((rows, 128), F32)
    for h in range(HEADS):
        at = slice(h * DH, (h + 1) * DH)
        grad_mix = lax.dot_general(low_first[...], w_out[at, :], ACROSS, preferred_element_type=F32)
        dots = jnp.sum(grad_mix * mix[:, at], axis=1, keepdims=True)
        inner = jnp.where(lane % HEADS == h, dots, inner)
        for r in range(ROUNDS):
            j = r * HEADS + h
            sent[h * ROUNDS + r, 0:rows, :] = (weights[:, j : j + 1] * grad_mix).astype(BF16)
    inner = inner * weights[...]
    low_lines = [p.astype(F32) for p in split3(jnp.transpose(inner[0:128]))]
    high_lines = [p.astype(F32) for p in split3(jnp.transpose(inner[128:256]))]
    blank = jnp.zeros((EXTRA - 6, 128), F32)
    for h in range(HEADS):
        for r in range(ROUNDS):
            j = r * HEADS + h
            tail = [p[j : j + 1] for p in low_lines + high_lines] + [blank]
            sent[h * ROUNDS + r, rows : rows + EXTRA, :] = jnp.concatenate(tail, axis=0).astype(BF16)


def uncombine(grad_normed, mix, first, weights, g_one, w_out, gain):
    rows, width = g_one.shape
    return pl.pallas_call(
        uncombine_kernel,
        out_shape=[
            sd((rows, width), F32),
            sd((HEADS * ROUNDS, rows + EXTRA, DH), BF16),
            sd((1, width), F32),
            sd((1, width), F32),
            sd((rows, width), BF16),
        ],
        in_specs=vm(7),
        out_specs=vm(5),
        compiler_params=params(16),
        name="uncombine",
        cost_estimate=takes(8),
    )(grad_normed, mix, first, weights, g_one, w_out, gain)


def down_out_kernel(*refs):
    hid, x, down0, far = refs[0], refs[1], refs[2], refs[3:15]
    out, down, summed, sems = refs[15:]
    start_copies(lambda flip: far_copies(down0, far, down, sems, 0, not flip, range(7)))
    summed[...] = x[...].astype(F32)
    for k in range(4):
        wait_copies(down0, far, down, sems, 0, k)
        summed[...] += lax.dot_general(hid[k], down[k], ACROSS, preferred_element_type=F32)
    out[...] = summed[...].astype(BF16)


def down_out(hid, x, down0, far):
    rows, width = x.shape
    return pl.pallas_call(
        down_out_kernel,
        out_shape=sd((rows, width), BF16),
        in_specs=vm(2) + anywhere(13),
        out_specs=pl.BlockSpec(memory_space=pltpu.VMEM),
        scratch_shapes=[
            pltpu.VMEM((4, width, 1024), BF16),
            pltpu.VMEM((rows, width), F32),
            pltpu.SemaphoreType.DMA((7,)),
        ],
        compiler_params=params(60),
        name="down_out",
        cost_estimate=takes(6),
    )(hid, x, down0, *far)


def begin(moves, sems):
    copies = [pltpu.make_async_copy(src, dst, sems.at[i]) for i, (src, dst) in enumerate(moves)]
    for c in copies:
        c.start()
    return copies


def last_rows(array, to, k):
    rows = to.shape[1]
    return (array.at[pl.ds(array.shape[0] - rows, rows)], to.at[k])


def peer_hidden(rows_in, grads_in, k, up, down, hid, pre, to):
    def hidden_part(i, c):
        for u in range(2):
            at = pl.ds(pl.multiple_of(i * 512 + u * 256, 256), 256)
            act = jnp.dot(rows_in[k], up[:, at], preferred_element_type=F32)
            grad = jnp.dot(grads_in[k], down[:, at], preferred_element_type=F32)
            hid[to, :, at], pre[to, :, at] = gelu_both(act, grad)
        return c

    lax.fori_loop(0, 2, hidden_part, 0)


def peers_kernel(*refs):
    normed, grads, ahead, behind, g1, g3, g2, weights_up, weights_down = refs[:9]
    hid, pre, turned_grads, turned_rows, rows_in, grads_in, up, down, sems = refs[9:]
    moves = [(weights_up, up), (weights_down, down)]
    moves += [(ahead, rows_in.at[1]), last_rows(g1, grads_in, 1)]
    moves += [(behind, rows_in.at[2]), last_rows(g3, grads_in, 2)]
    moves += [(normed, rows_in.at[0]), (grads, grads_in.at[0]), last_rows(g2, grads_in, 3)]
    copies = begin(moves, sems)
    for k, ready in ((1, copies[:4]), (2, copies[4:6])):
        for c in ready:
            c.wait()
        peer_hidden(rows_in, grads_in, k, up, down, hid, pre, k - 1)
    for c in copies[6:]:
        c.wait()
    count, rows, width = grads_in.shape
    turned_grads[...] = jnp.transpose(grads_in[...].reshape(count * rows, width))
    turned_rows[...] = jnp.transpose(rows_in[...].reshape((count - 1) * rows, width))


def peers(normed, grads, ahead, behind, g1, g3, g2, up, down):
    rows, width = normed.shape
    return pl.pallas_call(
        peers_kernel,
        out_shape=[sd((2, rows, 1024), BF16)] * 2 + [sd((width, 4 * rows), BF16), sd((width, 3 * rows), BF16)],
        in_specs=anywhere(9),
        out_specs=vm(4),
        scratch_shapes=[pltpu.VMEM((3, rows, 1024), BF16), pltpu.VMEM((4, rows, 1024), BF16)]
        + [pltpu.VMEM((width, 1024), BF16)] * 2
        + [pltpu.SemaphoreType.DMA((9,))],
        compiler_params=params(60),
        name="peers",
        cost_estimate=takes(9),
    )(normed, grads, ahead, behind, g1, g3, g2, up, down)


def feed_kernel(*refs):
    (hid_own, pre_own, hid_near, pre_near, left_grads, left_rows, g2) = refs[:7]
    across, weights_up, weights_down, out = refs[7:11]
    rows_in, grads_in, hid, pre, up, down, turned_grads, turned_rows, sems = refs[11:]
    rows = pre_own.shape[0]
    moves = [(weights_up, up), (weights_down, down), (across, rows_in.at[0]), last_rows(g2, grads_in, 0)]
    moves += [(left_rows, turned_rows.at[:, pl.ds(0, 3 * rows)]), (pre_own, pre.at[0])]
    moves += [(pre_near, pre.at[pl.ds(1, 2)]), (left_grads, turned_grads), (hid_own.at[0], hid.at[0])]
    moves += [(hid_near, hid.at[pl.ds(1, 2)])]
    copies = begin(moves, sems)
    for c in copies[:4]:
        c.wait()
    peer_hidden(rows_in, grads_in, 0, up, down, hid, pre, 3)
    for c in copies[4:7]:
        c.wait()
    turned_rows[:, 3 * rows :] = jnp.transpose(rows_in[0])
    for first, turned, rights in ((0, turned_rows, pre), (1024, turned_grads, hid)):
        if first:
            for c in copies[7:]:
                c.wait()

        def piece(i, c):
            left = turned[pl.ds(pl.multiple_of(i * 256, 256), 256), :]
            total = jnp.dot(left, rights[...].reshape(4 * rows, 1024), preferred_element_type=F32).astype(BF16)
            for j in range(8):
                out[j * 4 + i, :, first : first + 1024] = total[j * 32 : j * 32 + 32]
            return c

        lax.fori_loop(0, 4, piece, 0)


def feed(hid_own, pre_own, hid_near, pre_near, left_grads, left_rows, g2, across, up, down):
    rows, width = pre_own.shape[0], up.shape[0]
    return pl.pallas_call(
        feed_kernel,
        out_shape=sd((width // 32, 32, 2048), BF16),
        in_specs=anywhere(10),
        out_specs=pl.BlockSpec(memory_space=pltpu.VMEM),
        scratch_shapes=[pltpu.VMEM((1, rows, 1024), BF16)] * 2
        + [pltpu.VMEM((4, rows, 1024), BF16)] * 2
        + [pltpu.VMEM((width, 1024), BF16)] * 2
        + [pltpu.VMEM((width, 4 * rows), BF16)] * 2
        + [pltpu.SemaphoreType.DMA((10,))],
        compiler_params=params(60),
        name="feed",
        cost_estimate=takes(12),
    )(hid_own, pre_own, hid_near, pre_near, left_grads, left_rows, g2, across, up, down)


def sum_rounds_kernel(back, out):
    for h in range(HEADS):
        total = back[2 * h].astype(F32) + back[2 * h + 1].astype(F32)
        for half in range(2):
            at = slice(half * HEADS * DH + h * DH, half * HEADS * DH + (h + 1) * DH)
            out[:, at] = total[:, half * DH : (half + 1) * DH].astype(BF16)


def sum_rounds(back):
    rows = back.shape[1]
    return pl.pallas_call(
        sum_rounds_kernel,
        out_shape=sd((rows, 2 * HEADS * DH), BF16),
        in_specs=vm(1),
        out_specs=pl.BlockSpec(memory_space=pltpu.VMEM),
        compiler_params=params(60),
        name="sum_rounds",
        cost_estimate=takes(3),
    )(back)


def finish_kernel(grads, x, gain, w_qk, w_value, grad_two, gain_two, offset_two, grad_second, small, near, far):
    width = x.shape[1]
    grad_normed = lax.dot_general(grads[:, :width], w_qk[...], ACROSS, preferred_element_type=F32)
    grad_normed = grad_normed + lax.dot_general(grads[:, width:], w_value[...], ACROSS, preferred_element_type=F32)
    grad_x, gg, go = layer_back(x[...].astype(F32), grad_normed, gain[...])
    grad_second[...] = grad_x + grad_two[...].astype(F32)
    lines = []
    for line in (gg, go, gain_two[...], offset_two[...]):
        high = line.astype(BF16).astype(F32)
        lines += [high, line - high]
    blank = jnp.zeros((8, width), F32)
    rest = jnp.zeros((112, width), F32)
    near[...] = jnp.transpose(jnp.concatenate(lines + [blank, rest], axis=0))
    far[...] = jnp.transpose(jnp.concatenate([blank] + lines + [rest], axis=0))
    core = lax.axis_index("seq") % 2
    for j in range(small.shape[0]):
        a = near[pl.ds(pl.multiple_of(j * 64 + core * 32, 32), 32), :]
        b = far[pl.ds(pl.multiple_of(j * 64 + (1 - core) * 32, 32), 32), :]
        small[j] = (a + b).astype(BF16)


def finish(grads, x, gain, w_qk, w_value, grad_two, gain_two, offset_two):
    rows, width = x.shape
    return pl.pallas_call(
        finish_kernel,
        out_shape=[sd((rows, width), F32), sd((width // 64, 32, 128), BF16)],
        in_specs=vm(8),
        out_specs=vm(2),
        scratch_shapes=[pltpu.VMEM((width, 128), F32)] * 2,
        compiler_params=params(60),
        name="finish",
        cost_estimate=takes(5),
    )(grads, x, gain, w_qk, w_value, grad_two, gain_two, offset_two)


def pair_kernel(left, left_other, right, right_other, *rest):
    blocks, lines, rows = left.shape
    out, width = rest[-1], right.shape[1]
    total = jnp.dot(left[...].reshape(blocks * lines, rows), right[...], preferred_element_type=F32)
    total = total + jnp.dot(left_other[...].reshape(blocks * lines, rows), right_other[...], preferred_element_type=F32)
    out[:, :, :width] = total.astype(BF16).reshape(blocks, lines, width)
    for extra in rest[:-1]:
        out[:, :, width : width + extra.shape[2]] = extra[...]
        width += extra.shape[2]


def pair(left, left_other, right, right_other, *extra):
    blocks, lines, rows = left.shape
    width = right.shape[1] + sum(e.shape[2] for e in extra)
    return pl.pallas_call(
        pair_kernel,
        out_shape=sd((blocks, lines, width), BF16),
        in_specs=vm(4 + len(extra)),
        out_specs=pl.BlockSpec(memory_space=pltpu.VMEM),
        compiler_params=params(60),
        name="pair",
        cost_estimate=takes(3),
    )(left, left_other, right, right_other, *extra)


def swap_seq(array):
    return lax.all_to_all(array, "seq", split_axis=0, concat_axis=0, tiled=True)


def same_core():
    count = lax.axis_size("seq")
    return [list(range(c, count, 2)) for c in range(2)]


def along_x_and_core():
    return [[y * 8 + x * 2 + c for x in range(4) for c in range(2)] for y in range(4)]


def along_y():
    return [[y * 8 + x * 2 + c for y in range(4)] for x in range(4) for c in range(2)]


def swap_chips(array):
    return lax.all_to_all(
        array, "seq", split_axis=0, concat_axis=0, tiled=True, axis_index_groups=same_core()
    )


def flip_bit(array, axis, bit):
    return lax.ppermute(array, axis, [(i, i ^ bit) for i in range(lax.axis_size(axis))])


def swap_cores(array):
    return flip_bit(array, "seq", 1)


def from_ahead(array, step):
    count = lax.axis_size("ffn")
    return lax.ppermute(array, "ffn", [((i + step) % count, i) for i in range(count)])


def tied(array, *others):
    return lax.optimization_barrier((array, others))[0]


def add_low(a, b):
    return (a.astype(F32) + b.astype(F32)).astype(BF16)


def shards(
    stream_one,
    stream_two,
    doc_lengths,
    bucket_ids,
    norm1_gain,
    norm1_bias,
    w_qk,
    w_value,
    w_out,
    norm2_gain,
    norm2_bias,
    w_up,
    w_down,
    grad_out_one,
    grad_out_two,
):
    rows, width = stream_one.shape[1:]
    seq, ffn = lax.axis_index("seq"), lax.axis_index("ffn")
    core = seq % 2
    gain_one, bias_one = norm1_gain.reshape(1, -1), norm1_bias.reshape(1, -1)
    gain_two, bias_two = norm2_gain.reshape(1, -1), norm2_bias.reshape(1, -1)

    msg, normed_one, keep_rows, give_rows = project(stream_two[0], gain_one, bias_one, w_qk, w_value)
    received = swap_chips(msg)
    top, low = [jnp.where(core == 0, w_up[at], w_down[at]) for at in (slice(0, 512), slice(512, 1024))]
    buckets, top, low = lax.optimization_barrier((bucket_ids[0, 0], top, low))
    top1, low3 = from_ahead(top, 1), from_ahead(low, 3)
    order, bias = prepare(buckets, jnp.cumsum(doc_lengths[0]))
    received, order, bias, top, low, top1, low3 = lax.optimization_barrier(
        (received, order, bias, top, low, top1, low3)
    )
    came = swap_cores(received)
    lowg1 = from_ahead(jnp.concatenate([low, grad_out_two[0]], axis=0), 1)
    topg3 = from_ahead(jnp.concatenate([top, grad_out_two[0]], axis=0), 3)
    other_rows = swap_cores(give_rows)
    top1_other, low3_other = swap_cores(top1), swap_cores(low3)
    sent, queries, keys, vals, probs = attend(order, received, came, bias)
    sent, top1, low3, lowg1, topg3, top1_other, low3_other, other_rows = lax.optimization_barrier(
        (sent, top1, low3, lowg1, topg3, top1_other, low3_other, other_rows)
    )
    per_round = swap_seq(sent)
    top2, low2 = from_ahead(top1, 1), from_ahead(low3, 3)
    lowg1_other, topg3_other = swap_cores(lowg1), swap_cores(topg3)
    per_round, top2, low2, lowg1_other, topg3_other = lax.optimization_barrier(
        (per_round, top2, low2, lowg1_other, topg3_other)
    )
    far_weights = [top1, lowg1, top2, low2, topg3, low3]
    far_weights += [top1_other, lowg1_other, swap_cores(top2), swap_cores(low2), topg3_other, low3_other]
    grads2 = from_ahead(topg3[512:], 3)
    mix, first, one_low, normed_two, weights, keep_mix, give_mix = combine(per_round, stream_one[0], w_out, gain_two, bias_two)
    ahead, behind = from_ahead(normed_two, 1), from_ahead(normed_two, 3)
    grad_normed, hid, pre0 = middle(normed_two, grad_out_two[0], w_up, w_down, far_weights)
    grad_normed, ahead, behind, grads2 = lax.optimization_barrier((grad_normed, ahead, behind, grads2))
    across = from_ahead(ahead, 1)
    grad_first, msg, grad_gain_two, grad_bias_two, low_first = uncombine(
        grad_normed, mix, first, weights, grad_out_one[0], w_out, gain_two
    )
    far = swap_seq(msg)
    part_out = pair(keep_mix, swap_cores(give_mix), low_first, swap_cores(low_first))
    peer_parts = peers(normed_two, grad_out_two[0], ahead, behind, lowg1, topg3, grads2, w_up, w_down)
    peer_parts, part_out = lax.optimization_barrier((peer_parts, part_out))
    part_out = part_out.reshape(-1, 4, 8, width)
    part_feed = feed(hid, pre0, *peer_parts, grads2, across, w_up, w_down)
    far, part_feed, part_out = lax.optimization_barrier((far, part_feed, part_out))
    keep, give = attend_back(order, far, queries, keys, vals, probs)
    near_feed = part_feed.reshape(-1, part_feed.shape[2])
    near_feed = lax.psum_scatter(near_feed, "seq", tiled=True, axis_index_groups=along_x_and_core())
    keep, give, near_feed = lax.optimization_barrier((keep, give, near_feed))
    near_feed = lax.psum_scatter(near_feed, "seq", tiled=True, axis_index_groups=along_y())
    part_out = tied(part_out, keep)
    blocks = [
        from_ahead(lax.dynamic_index_in_dim(part_out, (ffn + 4 - k) % 4, 1, keepdims=False), k) for k in (1, 2, 3)
    ]
    back = swap_chips(add_low(keep, swap_cores(give)))
    sums_out = lax.dynamic_index_in_dim(part_out, ffn, 1, keepdims=False).astype(F32)
    for block in blocks:
        sums_out = sums_out + block.astype(F32)
    sums_out = sums_out.astype(BF16).reshape(-1, 32, width // 4)
    back, sums_out = lax.optimization_barrier((back, sums_out))
    hid = tied(hid, keep)
    two_low = down_out(hid, stream_two[0], w_down, far_weights)
    grads = sum_rounds(back)
    grads, near_feed = lax.optimization_barrier((grads, near_feed))
    grads_other = swap_cores(grads)
    grad_second, small = finish(
        grads, stream_two[0], gain_one, w_qk, w_value, grad_out_two[0], grad_gain_two, grad_bias_two
    )
    part = pair(keep_rows, other_rows, grads, grads_other, small, sums_out)
    near = swap_chips(part)
    near, near_feed = lax.optimization_barrier((near, near_feed))
    near = near.astype(F32).sum(axis=0)
    near, near_out = near[:, : 2 * width + 128].reshape(4, 8, -1), near[:, 2 * width + 128 :]
    whole = lax.dynamic_index_in_dim(near, ffn, 0, keepdims=False)
    for k in (1, 2, 3):
        whole = whole + from_ahead(lax.dynamic_index_in_dim(near, (ffn + 4 - k) % 4, 0, keepdims=False), k)
    small = whole[:, 2 * width :]
    lines = small[:, :8] + swap_cores(small)[:, 8:16]
    lines = lines[:, 0::2] + lines[:, 1::2]
    near_feed = near_feed.astype(F32)
    return (
        one_low[None],
        two_low[None],
        grad_first[None],
        grad_second[None],
        lines[:, 0],
        lines[:, 1],
        whole[:, :width],
        whole[:, width : 2 * width],
        near_out.reshape(8, width),
        lines[:, 2],
        lines[:, 3],
        near_feed[:, :1024],
        near_feed[:, 1024:2048],
    )


def solution(mesh):
    return jax.shard_map(
        shards,
        mesh=mesh,
        in_specs=(
            P("ffn", "seq", None),
            P("ffn", "seq", None),
            P("ffn", None),
            P("ffn", "seq", None),
            P(),
            P(),
            P(),
            P(),
            P(),
            P(),
            P(),
            P(None, "ffn"),
            P(None, "ffn"),
            P("ffn", "seq", None),
            P("ffn", "seq", None),
        ),
        out_specs=(
            P("ffn", "seq", None),
            P("ffn", "seq", None),
            P("ffn", "seq", None),
            P("ffn", "seq", None),
            P(("seq", "ffn")),
            P(("seq", "ffn")),
            P(("seq", "ffn"), None),
            P(("seq", "ffn"), None),
            P(("seq", "ffn"), None),
            P(("seq", "ffn")),
            P(("seq", "ffn")),
            P("seq", "ffn"),
            P("seq", "ffn"),
        ),
        check_vma=False,
    )
```

```python
import jax
import jax.numpy as jnp
from jax import lax
from jax.experimental import pallas as pl
from jax.experimental.pallas import tpu as pltpu
from jax.sharding import PartitionSpec as P

HEADS = 8
DH = 128
ROUNDS = 4
SPAN = 64
EPS_NORM = 1e-05
EPS_KEY = 1e-06
SELF_PENALTY = 1000.0
SCALE = DH ** (-0.5)
EXTRA = 16
F32, BF16 = jnp.float32, jnp.bfloat16
ACROSS = (((1,), (1,)), ((), ()))
FLIP = (((0,), (0,)), ((), ()))


def vm(n):
    return [pl.BlockSpec(memory_space=pltpu.VMEM)] * n


def anywhere(n):
    return [pl.BlockSpec(memory_space=pl.ANY)] * n


def sd(shape, kind):
    return jax.ShapeDtypeStruct(shape, kind)


def params(mebibytes):
    return pltpu.CompilerParams(vmem_limit_bytes=mebibytes * 2**20)


def takes(us):
    return pl.CostEstimate(flops=0, transcendentals=0, bytes_accessed=int(us * 3.5e6))


def split3(x):
    a = x.astype(BF16)
    r = x - a.astype(F32)
    b = r.astype(BF16)
    c = (r - b.astype(F32)).astype(BF16)
    return a, b, c


def layer_rows(x, gain, offset):
    centred = x - jnp.mean(x, axis=1, keepdims=True)
    inverse = lax.rsqrt(jnp.mean(centred * centred, axis=1, keepdims=True) + EPS_NORM)
    return centred * inverse * gain + offset


def layer_back(x, grad, gain):
    centred = x - jnp.mean(x, axis=1, keepdims=True)
    inverse = lax.rsqrt(jnp.mean(centred * centred, axis=1, keepdims=True) + EPS_NORM)
    unit = centred * inverse
    grad_gain = jnp.sum(grad * unit, axis=0, keepdims=True)
    grad_offset = jnp.sum(grad, axis=0, keepdims=True)
    scaled = grad * gain
    inner = jnp.mean(scaled * unit, axis=1, keepdims=True)
    grad_x = inverse * (scaled - jnp.mean(scaled, axis=1, keepdims=True) - unit * inner)
    return grad_x, grad_gain, grad_offset


def split_by_core(turned, keep, give):
    core = lax.axis_index("seq") % 2
    for j in range(keep.shape[0]):
        keep[j] = turned[pl.ds(pl.multiple_of(j * 64 + core * 32, 32), 32), :]
        give[j] = turned[pl.ds(pl.multiple_of(j * 64 + (1 - core) * 32, 32), 32), :]


def project_kernel(x, gain, offset, w_qk, w_value, msg, normed_out, keep, give, turned):
    normed = layer_rows(x[...].astype(F32), gain[...], offset[...])
    low = normed.astype(BF16)
    normed_out[...] = low
    for h in range(HEADS):
        at = slice(h * DH, (h + 1) * DH)
        q = jnp.dot(low, w_qk[:, at], preferred_element_type=F32).astype(BF16)
        v = jnp.dot(low, w_value[:, at], preferred_element_type=F32).astype(BF16)
        for t in range(2):
            msg[h * 2 + t, :, :DH] = q
            msg[h * 2 + t, :, DH:] = v
    turned[...] = jnp.transpose(low.astype(F32)).astype(BF16)
    split_by_core(turned, keep, give)


def project(x, gain, offset, w_qk, w_value):
    rows, width = x.shape
    chips = 2 * HEADS
    return pl.pallas_call(
        project_kernel,
        out_shape=[
            sd((chips, rows, 2 * DH), BF16),
            sd((rows, width), BF16),
            sd((width // 64, 32, rows), BF16),
            sd((width // 64, 32, rows), BF16),
        ],
        in_specs=vm(5),
        out_specs=vm(4),
        scratch_shapes=[pltpu.VMEM((width, rows), BF16)],
        compiler_params=params(60),
        name="project",
        cost_estimate=takes(7),
    )(x, gain, offset, w_qk, w_value)


BLOCK = 8 * SPAN
SAFE = 60.0


def repeat(count, body, width=4):
    def several(i, c):
        for u in range(width):
            body(i * width + u)
        return c

    lax.fori_loop(0, count // width, several, 0)


def even(first, count):
    return pl.ds(2 * first, count, stride=2)


def odd(first, count):
    return pl.ds(2 * first + 1, count, stride=2)


def gather_pairs(order, base, src, slot):
    for u in range(BLOCK):
        place = 2 * order[base + u]
        slot[2 * u : 2 * u + 1, :] = src[pl.ds(place, 1), :]
        slot[2 * u + 1 : 2 * u + 2, :] = src[pl.ds(place + 1, 1), :]


def scatter_pairs(order, base, slot, dst):
    for u in range(BLOCK):
        dst[pl.ds(pl.multiple_of(2 * order[base + u], 2), 2), :] = slot[2 * u : 2 * u + 2, :]


def attend_kernel(order, mine, other, bias_in, msg, q_far, keys_far, vals_far, probs_far, came_all, sent_all, *rest):
    slots, (q_out, keys, vals, probs, bias, sems) = rest[:4], rest[4:]
    load = pltpu.make_async_copy(bias_in, bias, sems.at[0])
    load.start()
    length = q_out.shape[0]
    blocks = length // BLOCK
    core = lax.axis_index("seq") % 2
    came, done = slots[0:2], slots[2:4]

    def widen(j):
        for rows, side in ((mine, core), (other, 1 - core)):
            first = pl.multiple_of((2 * j + side) * 256, 256)
            came_all[even(first, 256), :] = rows[j, :, :DH].astype(F32)
            came_all[odd(first, 256), :] = rows[j, :, DH:].astype(F32)

    repeat(length // 512, widen, 2)

    def gather(b, slot):
        gather_pairs(order, b * BLOCK, came_all, slot)

    def scatter(b, slot):
        scatter_pairs(order, b * BLOCK, slot, sent_all)

    def ready(b, slot):
        q = slot[even(0, BLOCK), :]
        unit = q * lax.rsqrt(jnp.sum(q * q, axis=1, keepdims=True) + EPS_KEY)
        ahead = pl.ds(pl.multiple_of(b * BLOCK + SPAN, SPAN), BLOCK)
        keys[ahead, :] = unit.astype(BF16)
        vals[ahead, :] = slot[odd(0, BLOCK), :].astype(BF16)
        return q.astype(BF16)

    load.wait()
    gather(blocks - 1, came[1])
    ready(blocks - 1, came[1])
    keys[0:SPAN, :] = keys[length : length + SPAN, :]
    vals[0:SPAN, :] = vals[length : length + SPAN, :]
    gather(0, came[0])

    def compute(b, slot, out):
        base = pl.multiple_of(b * BLOCK, BLOCK)
        q = ready(b, slot)
        q_out[pl.ds(base, BLOCK), :] = q
        k = keys[pl.ds(base, BLOCK + SPAN), :]
        v = vals[pl.ds(base, BLOCK + SPAN), :]
        spans = range(BLOCK // SPAN)
        s = [
            lax.dot_general(
                q[u * SPAN : u * SPAN + SPAN], k[u * SPAN : u * SPAN + 2 * SPAN], ACROSS, preferred_element_type=F32
            )
            for u in spans
        ]
        s = jnp.concatenate(s, axis=0) * SCALE + bias[pl.ds(base, BLOCK), :].astype(F32)
        top = jnp.max(s, axis=1, keepdims=True)
        e = jnp.exp(s - top)
        total = jnp.sum(e, axis=1, keepdims=True)
        p = (e * (1.0 / total)).astype(BF16)
        probs[pl.ds(base, BLOCK), :] = p
        for u in spans:
            out[even(u * SPAN, SPAN), :] = jnp.dot(
                p[u * SPAN : u * SPAN + SPAN], v[u * SPAN : u * SPAN + 2 * SPAN], preferred_element_type=F32
            )
        out[odd(0, BLOCK), :] = jnp.broadcast_to(top + jnp.log(total), (BLOCK, DH))

    def step(i, c):
        b = 2 * i
        scatter(jnp.maximum(b - 1, 0), done[1])
        gather(b + 1, came[1])
        compute(b, came[0], done[0])
        scatter(b, done[0])
        gather(jnp.minimum(b + 2, blocks - 1), came[0])
        compute(b + 1, came[1], done[1])
        return c

    lax.fori_loop(0, blocks // 2, step, 0)
    pairs = ((q_out, q_far), (keys, keys_far), (vals, vals_far), (probs, probs_far))
    stores = [pltpu.make_async_copy(src, dst, sems.at[1 + n]) for n, (src, dst) in enumerate(pairs)]
    for store in stores:
        store.start()
    scatter(blocks - 1, done[1])

    across = lax.broadcasted_iota(jnp.int32, (128, 128), 0)
    eye = across == lax.broadcasted_iota(jnp.int32, (128, 128), 1)

    line = lax.broadcasted_iota(jnp.int32, (EXTRA, 6 * 128), 0)
    lane = lax.broadcasted_iota(jnp.int32, (EXTRA, 6 * 128), 1)
    pick = jnp.where(line == lane // 128, 1.0, 0.0).astype(BF16)

    def send(b):
        msg[b, 0:256, :] = sent_all[even(b * 256, 256), :].astype(BF16)
        parts = []
        for half in range(2):
            parts += split3(jnp.where(eye, sent_all[odd(b * 256 + half * 128, 128), :], 0.0))
        tail = jnp.dot(pick, jnp.concatenate(parts, axis=0), preferred_element_type=F32)
        msg[b, 256:, :] = tail.astype(BF16)

    repeat(length // 256, send)
    for store in stores:
        store.wait()


def attend(order, mine, other, bias):
    length = order.shape[0]
    kept = [(length, DH), (length + SPAN, DH), (length + SPAN, DH), (length, DH)]
    return pl.pallas_call(
        attend_kernel,
        out_shape=[sd((length // 256, 256 + EXTRA, DH), BF16)] + [sd(shape, BF16) for shape in kept],
        in_specs=[pl.BlockSpec(memory_space=pltpu.SMEM)] + vm(2) + anywhere(1),
        out_specs=vm(1) + anywhere(4),
        scratch_shapes=[pltpu.VMEM((2 * length, DH), F32)] * 2
        + [pltpu.VMEM((2 * BLOCK, DH), F32)] * 4
        + [pltpu.VMEM(shape, BF16) for shape in kept]
        + [pltpu.VMEM((length, 2 * SPAN), BF16), pltpu.SemaphoreType.DMA((5,))],
        compiler_params=params(60),
        name="attend",
        cost_estimate=takes(35),
    )(order, mine, other, bias)


def back_kernel(order, msg, *refs):
    far, (keep, give, came_all, sent_all, first_u, first_v, late), slots = refs[:4], refs[4:11], refs[11:15]
    near, sems = refs[15:19], refs[19]
    q_in, keys, vals, probs = near
    loads = [pltpu.make_async_copy(src, dst, sems.at[n]) for n, (src, dst) in enumerate(zip(far, near))]
    for load in loads:
        load.start()
    length = probs.shape[0]
    blocks = length // BLOCK
    core = lax.axis_index("seq") % 2
    came, done = slots[0:2], slots[2:4]
    late_u, late_v, late_q = late.at[0], late.at[1], late.at[2]
    across = lax.broadcasted_iota(jnp.int32, (128, 128), 0)
    eye = across == lax.broadcasted_iota(jnp.int32, (128, 128), 1)
    ones = jnp.ones((128, 128), BF16)

    def widen(b):
        came_all[even(b * 256, 256), :] = msg[b, 0:256, :].astype(F32)
        t = msg[b, 256:, :].astype(F32)
        for half in range(2):
            total = jnp.zeros((128, 128), F32)
            for k in range(3):
                row = half * 3 + k
                spot = jnp.where(eye, jnp.broadcast_to(t[row : row + 1], (128, 128)), 0.0).astype(BF16)
                total = total + jnp.dot(spot, ones, preferred_element_type=F32)
            came_all[odd(b * 256 + half * 128, 128), :] = total

    repeat(length // 256, widen)

    def scatter(b, slot):
        base = jnp.where(b == 0, length, b * BLOCK) - SPAN
        for u in range(BLOCK):
            if u == SPAN:
                base = b * BLOCK - SPAN
            sent_all[pl.ds(pl.multiple_of(2 * order[base + u], 2), 2), :] = slot[2 * u : 2 * u + 2, :]

    gather_pairs(order, 0, came_all, came[0])
    for load in loads:
        load.wait()
    late[...] = jnp.zeros(late.shape, F32)
    spans = range(BLOCK // SPAN)
    cut = lambda a, u, n=1: a[u * SPAN : (u + n) * SPAN]

    def whole(direct, unit_grad, q):
        q = q.astype(F32)
        r = lax.rsqrt(jnp.sum(q * q, axis=1, keepdims=True) + EPS_KEY)
        along = jnp.sum(q * unit_grad, axis=1, keepdims=True)
        return direct + r * unit_grad - q * (r * r * r * along)

    def compute(b, slot, out):
        base = pl.multiple_of(b * BLOCK, BLOCK)
        g = slot[even(0, BLOCK), :].astype(BF16)
        p = probs[pl.ds(base, BLOCK), :]
        v = vals[pl.ds(base, BLOCK + SPAN), :]
        k = keys[pl.ds(base, BLOCK + SPAN), :]
        q = q_in[pl.ds(base, BLOCK), :]
        back = q_in[pl.ds(pl.multiple_of(jnp.maximum(base - SPAN, 0), SPAN), SPAN), :]
        gp = [lax.dot_general(cut(g, u), cut(v, u, 2), ACROSS, preferred_element_type=F32) for u in spans]
        wide_v = [lax.dot_general(cut(p, u), cut(g, u), FLIP, preferred_element_type=F32) for u in spans]
        gs = p.astype(F32) * (jnp.concatenate(gp, axis=0) - slot[odd(0, BLOCK), :])
        d = (gs * SCALE).astype(BF16)
        direct = [jnp.dot(cut(d, u), cut(k, u, 2), preferred_element_type=F32) for u in spans]
        wide_u = [lax.dot_general(cut(d, u), cut(q, u), FLIP, preferred_element_type=F32) for u in spans]

        @pl.when(b == 0)
        def _():
            first_u[...] = wide_u[0][:SPAN]
            first_v[...] = wide_v[0][:SPAN]

        folded_u = [late_u[...] + wide_u[0][:SPAN]] + [wide_u[u - 1][SPAN:] + wide_u[u][:SPAN] for u in spans[1:]]
        folded_v = [late_v[...] + wide_v[0][:SPAN]] + [wide_v[u - 1][SPAN:] + wide_v[u][:SPAN] for u in spans[1:]]
        straight = jnp.concatenate([late_q[...]] + direct[:-1], axis=0)
        behind = jnp.concatenate([back, q[: BLOCK - SPAN]], axis=0)
        out[even(0, BLOCK), :] = whole(straight, jnp.concatenate(folded_u, axis=0), behind)
        out[odd(0, BLOCK), :] = jnp.concatenate(folded_v, axis=0)
        late_u[...] = wide_u[-1][SPAN:]
        late_v[...] = wide_v[-1][SPAN:]
        late_q[...] = direct[-1]

    def step(i, c):
        b = 2 * i
        scatter(jnp.maximum(b - 1, 0), done[1])
        gather_pairs(order, (b + 1) * BLOCK, came_all, came[1])
        compute(b, came[0], done[0])
        scatter(b, done[0])
        gather_pairs(order, jnp.minimum(b + 2, blocks - 1) * BLOCK, came_all, came[0])
        compute(b + 1, came[1], done[1])
        return c

    lax.fori_loop(0, blocks // 2, step, 0)
    scatter(blocks - 1, done[1])
    done[0][even(0, SPAN), :] = whole(late_q[...], late_u[...] + first_u[...], q_in[length - SPAN : length, :])
    done[0][odd(0, SPAN), :] = late_v[...] + first_v[...]
    for u in range(SPAN):
        place = 2 * order[length - SPAN + u]
        sent_all[pl.ds(place, 1), :] = done[0][2 * u : 2 * u + 1, :]
        sent_all[pl.ds(place + 1, 1), :] = done[0][2 * u + 1 : 2 * u + 2, :]

    def narrow(j):
        for out, side in ((keep, core), (give, 1 - core)):
            first = pl.multiple_of((2 * j + side) * 256, 256)
            out[j, :, :DH] = sent_all[even(first, 256), :].astype(BF16)
            out[j, :, DH:] = sent_all[odd(first, 256), :].astype(BF16)

    repeat(keep.shape[0], narrow)


def attend_back(order, msg, q_in, keys, vals, probs):
    length = probs.shape[0]
    half = length // 512
    kept = [array.shape for array in (q_in, keys, vals, probs)]
    return pl.pallas_call(
        back_kernel,
        out_shape=[sd((half, 256, 2 * DH), BF16)] * 2,
        in_specs=[pl.BlockSpec(memory_space=pltpu.SMEM)] + vm(1) + anywhere(4),
        out_specs=vm(2),
        scratch_shapes=[pltpu.VMEM((2 * length, DH), F32)] * 2
        + [pltpu.VMEM((SPAN, DH), F32)] * 2
        + [pltpu.VMEM((3, SPAN, DH), F32)]
        + [pltpu.VMEM((2 * BLOCK, DH), F32)] * 4
        + [pltpu.VMEM(shape, BF16) for shape in kept]
        + [pltpu.SemaphoreType.DMA((4,))],
        compiler_params=params(60),
        name="attend_back",
        cost_estimate=takes(36),
    )(order, msg, q_in, keys, vals, probs)


def prepare(bucket_row, ends):
    length = bucket_row.shape[0]
    places = jnp.arange(length, dtype=jnp.int32)
    _, order = lax.sort((bucket_row * length + places, places), num_keys=1)
    pos = order.reshape(-1, SPAN)
    start = jnp.max(jnp.where(ends <= pos[..., None], ends, 0), axis=-1)
    window = jnp.concatenate([jnp.roll(pos, 1, 0), pos], axis=1)
    k, q = window[:, None, :], pos[:, :, None]
    bias = jnp.where((k >= start[:, :, None]) & (k <= q), jnp.where(k == q, -1000.0, 0.0), -1e9)
    return order, bias.astype(BF16).reshape(length, 2 * SPAN)


def combine_kernel(
    msg, x, w_out, gain, offset, mix, first_out, first_low, normed, weights, keep, give, low_mix, turned
):
    rows = x.shape[0]
    for half in range(2):
        logs = []
        for r in range(ROUNDS):
            lines = []
            for h in range(HEADS):
                tail = msg[h * ROUNDS + r, rows : rows + EXTRA, :].astype(F32)
                k = half * 3
                lines.append(tail[k : k + 1] + tail[k + 1 : k + 2] + tail[k + 2 : k + 3])
            logs.append(jnp.concatenate(lines, axis=0))
        top = jnp.maximum(jnp.maximum(logs[0], logs[1]), jnp.maximum(logs[2], logs[3]))
        powers = [jnp.exp(v - top) for v in logs]
        inverse = 1.0 / (powers[0] + powers[1] + powers[2] + powers[3])
        lines = [v * inverse for v in powers]
        lines.append(jnp.zeros((128 - HEADS * ROUNDS, 128), F32))
        weights[half * 128 : half * 128 + 128, :] = jnp.transpose(jnp.concatenate(lines, axis=0))
    for h in range(HEADS):
        total = jnp.zeros((rows, DH), F32)
        for r in range(ROUNDS):
            j = r * HEADS + h
            total = total + weights[:, j : j + 1] * msg[h * ROUNDS + r, 0:rows, :].astype(F32)
        mix[:, h * DH : (h + 1) * DH] = total
        low_mix[:, h * DH : (h + 1) * DH] = total.astype(BF16)
    first = x[...].astype(F32) + jnp.dot(low_mix[...], w_out[...], preferred_element_type=F32)
    first_out[...] = first
    first_low[...] = first.astype(BF16)
    normed[...] = layer_rows(first, gain[...], offset[...]).astype(BF16)
    turned[...] = jnp.transpose(mix[...]).astype(BF16)
    split_by_core(turned, keep, give)


def combine(msg, x, w_out, gain, offset):
    rows, width = x.shape
    return pl.pallas_call(
        combine_kernel,
        out_shape=[
            sd((rows, width), F32),
            sd((rows, width), F32),
            sd((rows, width), BF16),
            sd((rows, width), BF16),
            sd((rows, 128), F32),
            sd((width // 64, 32, rows), BF16),
            sd((width // 64, 32, rows), BF16),
        ],
        in_specs=vm(5),
        out_specs=vm(7),
        scratch_shapes=[pltpu.VMEM((rows, width), BF16), pltpu.VMEM((width, rows), BF16)],
        compiler_params=params(60),
        name="combine",
        cost_estimate=takes(6),
    )(msg, x, w_out, gain, offset)


def far_copies(own, far, to, sems, first, flip, pieces):
    out = []
    for i in pieces:
        dst = to.at[(i + 1) // 2, pl.ds((i - 1) % 2 * 512, 512)] if i else to.at[0]
        src = (far[i + 5] if flip else far[i - 1]).at[pl.ds(0, 512)] if i else own
        out.append(pltpu.make_async_copy(src, dst, sems.at[first + i]))
    return out


def start_copies(copies):
    core = lax.axis_index("seq") % 2
    for side in range(2):

        @pl.when(core == side)
        def _():
            for c in copies(side == 1):
                c.start()


def wait_copies(own, far, to, sems, first, k):
    for c in far_copies(own, far, to, sems, first, False, (2 * k - 1, 2 * k) if k else (0,)):
        c.wait()


def gelu_both(act, grad):
    share = 0.5 + 0.5 * lax.erf(act * 0.7071067811865476)
    slope = share + act * (jnp.exp(act * act * -0.5) * 0.3989422804014327)
    return (act * share).astype(BF16), (grad * slope).astype(BF16)


def middle_kernel(*refs):
    normed, g_two, up0, down0, far = refs[0], refs[1], refs[2], refs[3], refs[4:16]
    grad_normed, hid, pre0, up, down, pre, sems = refs[16:]
    pieces = range(7)
    start_copies(
        lambda flip: far_copies(up0, far, up, sems, 0, flip, pieces)
        + far_copies(down0, far, down, sems, 7, not flip, pieces)
    )
    for k in range(4):
        wait_copies(up0, far, up, sems, 0, k)
        wait_copies(down0, far, down, sems, 7, k)

        def hidden_part(i, c):
            for u in range(2):
                at = pl.ds(pl.multiple_of(i * 512 + u * 256, 256), 256)
                act = jnp.dot(normed[...], up[k, :, at], preferred_element_type=F32)
                grad = jnp.dot(g_two[...], down[k, :, at], preferred_element_type=F32)
                hid[k, :, at], pre[k, :, at] = gelu_both(act, grad)
            return c

        lax.fori_loop(0, 2, hidden_part, 0)
    pre0[...] = pre[0]
    grad_normed[...] = jnp.zeros(grad_normed.shape, F32)

    def up_back(k, c):
        grad_normed[...] += lax.dot_general(pre[k], up[k], ACROSS, preferred_element_type=F32)
        return c

    lax.fori_loop(0, 4, up_back, 0)


def middle(normed, g_two, up0, down0, far):
    rows, width = normed.shape
    return pl.pallas_call(
        middle_kernel,
        out_shape=[sd((rows, width), F32), sd((4, rows, 1024), BF16), sd((rows, 1024), BF16)],
        in_specs=vm(2) + anywhere(14),
        out_specs=vm(3),
        scratch_shapes=[
            pltpu.VMEM((4, width, 1024), BF16),
            pltpu.VMEM((4, width, 1024), BF16),
            pltpu.VMEM((4, rows, 1024), BF16),
            pltpu.SemaphoreType.DMA((14,)),
        ],
        compiler_params=params(28),
        name="middle",
        cost_estimate=takes(16),
    )(normed, g_two, up0, down0, *far)


def uncombine_kernel(
    grad_normed, mix, first, weights, g_one, w_out, gain, grad_first, sent, grad_gain, grad_offset, low_first
):
    rows = g_one.shape[0]
    grad_x, gg, go = layer_back(first[...], grad_normed[...], gain[...])
    grad_gain[...] = gg
    grad_offset[...] = go
    grad_x = grad_x + g_one[...].astype(F32)
    grad_first[...] = grad_x
    low_first[...] = grad_x.astype(BF16)
    lane = lax.broadcasted_iota(jnp.int32, (rows, 128), 1)
    inner = jnp.zeros((rows, 128), F32)
    for h in range(HEADS):
        at = slice(h * DH, (h + 1) * DH)
        grad_mix = lax.dot_general(low_first[...], w_out[at, :], ACROSS, preferred_element_type=F32)
        dots = jnp.sum(grad_mix * mix[:, at], axis=1, keepdims=True)
        inner = jnp.where(lane % HEADS == h, dots, inner)
        for r in range(ROUNDS):
            j = r * HEADS + h
            sent[h * ROUNDS + r, 0:rows, :] = (weights[:, j : j + 1] * grad_mix).astype(BF16)
    inner = inner * weights[...]
    low_lines = [p.astype(F32) for p in split3(jnp.transpose(inner[0:128]))]
    high_lines = [p.astype(F32) for p in split3(jnp.transpose(inner[128:256]))]
    blank = jnp.zeros((EXTRA - 6, 128), F32)
    for h in range(HEADS):
        for r in range(ROUNDS):
            j = r * HEADS + h
            tail = [p[j : j + 1] for p in low_lines + high_lines] + [blank]
            sent[h * ROUNDS + r, rows : rows + EXTRA, :] = jnp.concatenate(tail, axis=0).astype(BF16)


def uncombine(grad_normed, mix, first, weights, g_one, w_out, gain):
    rows, width = g_one.shape
    return pl.pallas_call(
        uncombine_kernel,
        out_shape=[
            sd((rows, width), F32),
            sd((HEADS * ROUNDS, rows + EXTRA, DH), BF16),
            sd((1, width), F32),
            sd((1, width), F32),
            sd((rows, width), BF16),
        ],
        in_specs=vm(7),
        out_specs=vm(5),
        compiler_params=params(16),
        name="uncombine",
        cost_estimate=takes(8),
    )(grad_normed, mix, first, weights, g_one, w_out, gain)


def down_out_kernel(*refs):
    hid, x, down0, far = refs[0], refs[1], refs[2], refs[3:15]
    out, down, summed, sems = refs[15:]
    start_copies(lambda flip: far_copies(down0, far, down, sems, 0, not flip, range(7)))
    summed[...] = x[...].astype(F32)
    for k in range(4):
        wait_copies(down0, far, down, sems, 0, k)
        summed[...] += lax.dot_general(hid[k], down[k], ACROSS, preferred_element_type=F32)
    out[...] = summed[...].astype(BF16)


def down_out(hid, x, down0, far):
    rows, width = x.shape
    return pl.pallas_call(
        down_out_kernel,
        out_shape=sd((rows, width), BF16),
        in_specs=vm(2) + anywhere(13),
        out_specs=pl.BlockSpec(memory_space=pltpu.VMEM),
        scratch_shapes=[
            pltpu.VMEM((4, width, 1024), BF16),
            pltpu.VMEM((rows, width), F32),
            pltpu.SemaphoreType.DMA((7,)),
        ],
        compiler_params=params(60),
        name="down_out",
        cost_estimate=takes(6),
    )(hid, x, down0, *far)


def begin(moves, sems):
    copies = [pltpu.make_async_copy(src, dst, sems.at[i]) for i, (src, dst) in enumerate(moves)]
    for c in copies:
        c.start()
    return copies


def last_rows(array, to, k):
    rows = to.shape[1]
    return (array.at[pl.ds(array.shape[0] - rows, rows)], to.at[k])


def peer_hidden(rows_in, grads_in, k, up, down, hid, pre, to):
    def hidden_part(i, c):
        for u in range(2):
            at = pl.ds(pl.multiple_of(i * 512 + u * 256, 256), 256)
            act = jnp.dot(rows_in[k], up[:, at], preferred_element_type=F32)
            grad = jnp.dot(grads_in[k], down[:, at], preferred_element_type=F32)
            hid[to, :, at], pre[to, :, at] = gelu_both(act, grad)
        return c

    lax.fori_loop(0, 2, hidden_part, 0)


def peers_kernel(*refs):
    normed, grads, ahead, behind, g1, g3, g2, weights_up, weights_down = refs[:9]
    hid, pre, turned_grads, turned_rows, rows_in, grads_in, up, down, sems = refs[9:]
    moves = [(weights_up, up), (weights_down, down)]
    moves += [(ahead, rows_in.at[1]), last_rows(g1, grads_in, 1)]
    moves += [(behind, rows_in.at[2]), last_rows(g3, grads_in, 2)]
    moves += [(normed, rows_in.at[0]), (grads, grads_in.at[0]), last_rows(g2, grads_in, 3)]
    copies = begin(moves, sems)
    for k, ready in ((1, copies[:4]), (2, copies[4:6])):
        for c in ready:
            c.wait()
        peer_hidden(rows_in, grads_in, k, up, down, hid, pre, k - 1)
    for c in copies[6:]:
        c.wait()
    count, rows, width = grads_in.shape
    turned_grads[...] = jnp.transpose(grads_in[...].reshape(count * rows, width))
    turned_rows[...] = jnp.transpose(rows_in[...].reshape((count - 1) * rows, width))


def peers(normed, grads, ahead, behind, g1, g3, g2, up, down):
    rows, width = normed.shape
    return pl.pallas_call(
        peers_kernel,
        out_shape=[sd((2, rows, 1024), BF16)] * 2 + [sd((width, 4 * rows), BF16), sd((width, 3 * rows), BF16)],
        in_specs=anywhere(9),
        out_specs=vm(4),
        scratch_shapes=[pltpu.VMEM((3, rows, 1024), BF16), pltpu.VMEM((4, rows, 1024), BF16)]
        + [pltpu.VMEM((width, 1024), BF16)] * 2
        + [pltpu.SemaphoreType.DMA((9,))],
        compiler_params=params(60),
        name="peers",
        cost_estimate=takes(9),
    )(normed, grads, ahead, behind, g1, g3, g2, up, down)


def feed_kernel(*refs):
    (hid_own, pre_own, hid_near, pre_near, left_grads, left_rows, g2) = refs[:7]
    across, weights_up, weights_down, out = refs[7:11]
    rows_in, grads_in, hid, pre, up, down, turned_grads, turned_rows, sems = refs[11:]
    rows = pre_own.shape[0]
    moves = [(weights_up, up), (weights_down, down), (across, rows_in.at[0]), last_rows(g2, grads_in, 0)]
    moves += [(left_rows, turned_rows.at[:, pl.ds(0, 3 * rows)]), (pre_own, pre.at[0])]
    moves += [(pre_near, pre.at[pl.ds(1, 2)]), (left_grads, turned_grads), (hid_own.at[0], hid.at[0])]
    moves += [(hid_near, hid.at[pl.ds(1, 2)])]
    copies = begin(moves, sems)
    for c in copies[:4]:
        c.wait()
    peer_hidden(rows_in, grads_in, 0, up, down, hid, pre, 3)
    for c in copies[4:7]:
        c.wait()
    turned_rows[:, 3 * rows :] = jnp.transpose(rows_in[0])
    for first, turned, rights in ((0, turned_rows, pre), (1024, turned_grads, hid)):
        if first:
            for c in copies[7:]:
                c.wait()

        def piece(i, c):
            left = turned[pl.ds(pl.multiple_of(i * 256, 256), 256), :]
            total = jnp.dot(left, rights[...].reshape(4 * rows, 1024), preferred_element_type=F32).astype(BF16)
            for j in range(8):
                out[j * 4 + i, :, first : first + 1024] = total[j * 32 : j * 32 + 32]
            return c

        lax.fori_loop(0, 4, piece, 0)


def feed(hid_own, pre_own, hid_near, pre_near, left_grads, left_rows, g2, across, up, down):
    rows, width = pre_own.shape[0], up.shape[0]
    return pl.pallas_call(
        feed_kernel,
        out_shape=sd((width // 32, 32, 2048), BF16),
        in_specs=anywhere(10),
        out_specs=pl.BlockSpec(memory_space=pltpu.VMEM),
        scratch_shapes=[pltpu.VMEM((1, rows, 1024), BF16)] * 2
        + [pltpu.VMEM((4, rows, 1024), BF16)] * 2
        + [pltpu.VMEM((width, 1024), BF16)] * 2
        + [pltpu.VMEM((width, 4 * rows), BF16)] * 2
        + [pltpu.SemaphoreType.DMA((10,))],
        compiler_params=params(60),
        name="feed",
        cost_estimate=takes(12),
    )(hid_own, pre_own, hid_near, pre_near, left_grads, left_rows, g2, across, up, down)


def sum_rounds_kernel(back, out):
    for h in range(HEADS):
        total = back[2 * h].astype(F32) + back[2 * h + 1].astype(F32)
        for half in range(2):
            at = slice(half * HEADS * DH + h * DH, half * HEADS * DH + (h + 1) * DH)
            out[:, at] = total[:, half * DH : (half + 1) * DH].astype(BF16)


def sum_rounds(back):
    rows = back.shape[1]
    return pl.pallas_call(
        sum_rounds_kernel,
        out_shape=sd((rows, 2 * HEADS * DH), BF16),
        in_specs=vm(1),
        out_specs=pl.BlockSpec(memory_space=pltpu.VMEM),
        compiler_params=params(8),
        name="sum_rounds",
        cost_estimate=takes(3),
    )(back)


def finish_kernel(grads, x, gain, w_qk, w_value, grad_two, gain_two, offset_two, grad_second, small, near, far):
    width = x.shape[1]
    grad_normed = lax.dot_general(grads[:, :width], w_qk[...], ACROSS, preferred_element_type=F32)
    grad_normed = grad_normed + lax.dot_general(grads[:, width:], w_value[...], ACROSS, preferred_element_type=F32)
    grad_x, gg, go = layer_back(x[...].astype(F32), grad_normed, gain[...])
    grad_second[...] = grad_x + grad_two[...].astype(F32)
    lines = []
    for line in (gg, go, gain_two[...], offset_two[...]):
        high = line.astype(BF16).astype(F32)
        lines += [high, line - high]
    blank = jnp.zeros((8, width), F32)
    rest = jnp.zeros((112, width), F32)
    near[...] = jnp.transpose(jnp.concatenate(lines + [blank, rest], axis=0))
    far[...] = jnp.transpose(jnp.concatenate([blank] + lines + [rest], axis=0))
    core = lax.axis_index("seq") % 2
    for j in range(small.shape[0]):
        a = near[pl.ds(pl.multiple_of(j * 64 + core * 32, 32), 32), :]
        b = far[pl.ds(pl.multiple_of(j * 64 + (1 - core) * 32, 32), 32), :]
        small[j] = (a + b).astype(BF16)


def finish(grads, x, gain, w_qk, w_value, grad_two, gain_two, offset_two):
    rows, width = x.shape
    return pl.pallas_call(
        finish_kernel,
        out_shape=[sd((rows, width), F32), sd((width // 64, 32, 128), BF16)],
        in_specs=vm(8),
        out_specs=vm(2),
        scratch_shapes=[pltpu.VMEM((width, 128), F32)] * 2,
        compiler_params=params(60),
        name="finish",
        cost_estimate=takes(5),
    )(grads, x, gain, w_qk, w_value, grad_two, gain_two, offset_two)


def pair_kernel(left, left_other, right, right_other, *rest):
    blocks, lines, rows = left.shape
    out, width = rest[-1], right.shape[1]
    total = jnp.dot(left[...].reshape(blocks * lines, rows), right[...], preferred_element_type=F32)
    total = total + jnp.dot(left_other[...].reshape(blocks * lines, rows), right_other[...], preferred_element_type=F32)
    out[:, :, :width] = total.astype(BF16).reshape(blocks, lines, width)
    for extra in rest[:-1]:
        out[:, :, width : width + extra.shape[2]] = extra[...]
        width += extra.shape[2]


def pair(left, left_other, right, right_other, *extra):
    blocks, lines, rows = left.shape
    width = right.shape[1] + sum(e.shape[2] for e in extra)
    return pl.pallas_call(
        pair_kernel,
        out_shape=sd((blocks, lines, width), BF16),
        in_specs=vm(4 + len(extra)),
        out_specs=pl.BlockSpec(memory_space=pltpu.VMEM),
        compiler_params=params(60),
        name="pair",
        cost_estimate=takes(3),
    )(left, left_other, right, right_other, *extra)


def swap_seq(array):
    return lax.all_to_all(array, "seq", split_axis=0, concat_axis=0, tiled=True)


def same_core():
    count = lax.axis_size("seq")
    return [list(range(c, count, 2)) for c in range(2)]


def along_x_and_core():
    return [[y * 8 + x * 2 + c for x in range(4) for c in range(2)] for y in range(4)]


def along_y():
    return [[y * 8 + x * 2 + c for y in range(4)] for x in range(4) for c in range(2)]


def swap_chips(array):
    return lax.all_to_all(
        array, "seq", split_axis=0, concat_axis=0, tiled=True, axis_index_groups=same_core()
    )


def flip_bit(array, axis, bit):
    return lax.ppermute(array, axis, [(i, i ^ bit) for i in range(lax.axis_size(axis))])


def swap_cores(array):
    return flip_bit(array, "seq", 1)


def from_ahead(array, step):
    count = lax.axis_size("ffn")
    return lax.ppermute(array, "ffn", [((i + step) % count, i) for i in range(count)])


def tied(array, *others):
    return lax.optimization_barrier((array, others))[0]


def add_low(a, b):
    return (a.astype(F32) + b.astype(F32)).astype(BF16)


def shards(
    stream_one,
    stream_two,
    doc_lengths,
    bucket_ids,
    norm1_gain,
    norm1_bias,
    w_qk,
    w_value,
    w_out,
    norm2_gain,
    norm2_bias,
    w_up,
    w_down,
    grad_out_one,
    grad_out_two,
):
    rows, width = stream_one.shape[1:]
    seq, ffn = lax.axis_index("seq"), lax.axis_index("ffn")
    core = seq % 2
    gain_one, bias_one = norm1_gain.reshape(1, -1), norm1_bias.reshape(1, -1)
    gain_two, bias_two = norm2_gain.reshape(1, -1), norm2_bias.reshape(1, -1)

    msg, normed_one, keep_rows, give_rows = project(stream_two[0], gain_one, bias_one, w_qk, w_value)
    received = swap_chips(msg)
    top, low = [jnp.where(core == 0, w_up[at], w_down[at]) for at in (slice(0, 512), slice(512, 1024))]
    buckets, top, low = lax.optimization_barrier((bucket_ids[0, 0], top, low))
    top1, low3 = from_ahead(top, 1), from_ahead(low, 3)
    order, bias = prepare(buckets, jnp.cumsum(doc_lengths[0]))
    received, order, bias, top, low, top1, low3 = lax.optimization_barrier(
        (received, order, bias, top, low, top1, low3)
    )
    came = swap_cores(received)
    lowg1 = from_ahead(jnp.concatenate([low, grad_out_two[0]], axis=0), 1)
    topg3 = from_ahead(jnp.concatenate([top, grad_out_two[0]], axis=0), 3)
    other_rows = swap_cores(give_rows)
    top1_other, low3_other = swap_cores(top1), swap_cores(low3)
    sent, queries, keys, vals, probs = attend(order, received, came, bias)
    sent, top1, low3, lowg1, topg3, top1_other, low3_other, other_rows = lax.optimization_barrier(
        (sent, top1, low3, lowg1, topg3, top1_other, low3_other, other_rows)
    )
    per_round = swap_seq(sent)
    top2, low2 = from_ahead(top1, 1), from_ahead(low3, 3)
    lowg1_other, topg3_other = swap_cores(lowg1), swap_cores(topg3)
    per_round, top2, low2, lowg1_other, topg3_other = lax.optimization_barrier(
        (per_round, top2, low2, lowg1_other, topg3_other)
    )
    far_weights = [top1, lowg1, top2, low2, topg3, low3]
    far_weights += [top1_other, lowg1_other, swap_cores(top2), swap_cores(low2), topg3_other, low3_other]
    grads2 = from_ahead(topg3[512:], 3)
    mix, first, one_low, normed_two, weights, keep_mix, give_mix = combine(per_round, stream_one[0], w_out, gain_two, bias_two)
    ahead, behind = from_ahead(normed_two, 1), from_ahead(normed_two, 3)
    grad_normed, hid, pre0 = middle(normed_two, grad_out_two[0], w_up, w_down, far_weights)
    grad_normed, ahead, behind, grads2 = lax.optimization_barrier((grad_normed, ahead, behind, grads2))
    across = from_ahead(ahead, 1)
    grad_first, msg, grad_gain_two, grad_bias_two, low_first = uncombine(
        grad_normed, mix, first, weights, grad_out_one[0], w_out, gain_two
    )
    far = swap_seq(msg)
    part_out = pair(keep_mix, swap_cores(give_mix), low_first, swap_cores(low_first))
    peer_parts = peers(normed_two, grad_out_two[0], ahead, behind, lowg1, topg3, grads2, w_up, w_down)
    peer_parts, part_out = lax.optimization_barrier((peer_parts, part_out))
    part_out = part_out.reshape(-1, 4, 8, width)
    part_feed = feed(hid, pre0, *peer_parts, grads2, across, w_up, w_down)
    far, part_feed, part_out = lax.optimization_barrier((far, part_feed, part_out))
    keep, give = attend_back(order, far, queries, keys, vals, probs)
    near_feed = part_feed.reshape(-1, part_feed.shape[2])
    near_feed = lax.psum_scatter(near_feed, "seq", tiled=True, axis_index_groups=along_x_and_core())
    low, near_feed = lax.optimization_barrier((add_low(keep, swap_cores(give)), near_feed))
    near_feed = lax.psum_scatter(near_feed, "seq", tiled=True, axis_index_groups=along_y())
    part_out = tied(part_out, keep)
    blocks = [
        from_ahead(lax.dynamic_index_in_dim(part_out, (ffn + 4 - k) % 4, 1, keepdims=False), k) for k in (1, 2, 3)
    ]
    back = swap_chips(low)
    sums_out = lax.dynamic_index_in_dim(part_out, ffn, 1, keepdims=False).astype(F32)
    for block in blocks:
        sums_out = sums_out + block.astype(F32)
    sums_out = sums_out.astype(BF16).reshape(-1, 32, width // 4)
    back, sums_out = lax.optimization_barrier((back, sums_out))
    hid = tied(hid, keep)
    two_low = down_out(hid, stream_two[0], w_down, far_weights)
    grads = sum_rounds(back)
    grads, near_feed = lax.optimization_barrier((grads, near_feed))
    grads_other = swap_cores(grads)
    grad_second, small = finish(
        grads, stream_two[0], gain_one, w_qk, w_value, grad_out_two[0], grad_gain_two, grad_bias_two
    )
    part = pair(keep_rows, other_rows, grads, grads_other, small, sums_out)
    near = swap_chips(part)
    near, near_feed = lax.optimization_barrier((near, near_feed))
    near = near.astype(F32).sum(axis=0)
    near, near_out = near[:, : 2 * width + 128].reshape(4, 8, -1), near[:, 2 * width + 128 :]
    whole = lax.dynamic_index_in_dim(near, ffn, 0, keepdims=False)
    for k in (1, 2, 3):
        whole = whole + from_ahead(lax.dynamic_index_in_dim(near, (ffn + 4 - k) % 4, 0, keepdims=False), k)
    small = whole[:, 2 * width :]
    lines = small[:, :8] + swap_cores(small)[:, 8:16]
    lines = lines[:, 0::2] + lines[:, 1::2]
    near_feed = near_feed.astype(F32)
    return (
        one_low[None],
        two_low[None],
        grad_first[None],
        grad_second[None],
        lines[:, 0],
        lines[:, 1],
        whole[:, :width],
        whole[:, width : 2 * width],
        near_out.reshape(8, width),
        lines[:, 2],
        lines[:, 3],
        near_feed[:, :1024],
        near_feed[:, 1024:2048],
    )


def solution(mesh):
    return jax.shard_map(
        shards,
        mesh=mesh,
        in_specs=(
            P("ffn", "seq", None),
            P("ffn", "seq", None),
            P("ffn", None),
            P("ffn", "seq", None),
            P(),
            P(),
            P(),
            P(),
            P(),
            P(),
            P(),
            P(None, "ffn"),
            P(None, "ffn"),
            P("ffn", "seq", None),
            P("ffn", "seq", None),
        ),
        out_specs=(
            P("ffn", "seq", None),
            P("ffn", "seq", None),
            P("ffn", "seq", None),
            P("ffn", "seq", None),
            P(("seq", "ffn")),
            P(("seq", "ffn")),
            P(("seq", "ffn"), None),
            P(("seq", "ffn"), None),
            P(("seq", "ffn"), None),
            P(("seq", "ffn")),
            P(("seq", "ffn")),
            P("seq", "ffn"),
            P("seq", "ffn"),
        ),
        check_vma=False,
    )
```

```python
import jax
import jax.numpy as jnp
from jax import lax
from jax.experimental import pallas as pl
from jax.experimental.pallas import tpu as pltpu
from jax.sharding import PartitionSpec as P

HEADS = 8
DH = 128
ROUNDS = 4
SPAN = 64
EPS_NORM = 1e-05
EPS_KEY = 1e-06
SELF_PENALTY = 1000.0
SCALE = DH ** (-0.5)
EXTRA = 16
F32, BF16 = jnp.float32, jnp.bfloat16
ACROSS = (((1,), (1,)), ((), ()))
FLIP = (((0,), (0,)), ((), ()))


def vm(n):
    return [pl.BlockSpec(memory_space=pltpu.VMEM)] * n


def anywhere(n):
    return [pl.BlockSpec(memory_space=pl.ANY)] * n


def sd(shape, kind):
    return jax.ShapeDtypeStruct(shape, kind)


def params(mebibytes):
    return pltpu.CompilerParams(vmem_limit_bytes=mebibytes * 2**20)


def takes(us):
    return pl.CostEstimate(flops=0, transcendentals=0, bytes_accessed=int(us * 3.5e6))


def split3(x):
    a = x.astype(BF16)
    r = x - a.astype(F32)
    b = r.astype(BF16)
    c = (r - b.astype(F32)).astype(BF16)
    return a, b, c


def layer_rows(x, gain, offset):
    centred = x - jnp.mean(x, axis=1, keepdims=True)
    inverse = lax.rsqrt(jnp.mean(centred * centred, axis=1, keepdims=True) + EPS_NORM)
    return centred * inverse * gain + offset


def layer_back(x, grad, gain):
    centred = x - jnp.mean(x, axis=1, keepdims=True)
    inverse = lax.rsqrt(jnp.mean(centred * centred, axis=1, keepdims=True) + EPS_NORM)
    unit = centred * inverse
    grad_gain = jnp.sum(grad * unit, axis=0, keepdims=True)
    grad_offset = jnp.sum(grad, axis=0, keepdims=True)
    scaled = grad * gain
    inner = jnp.mean(scaled * unit, axis=1, keepdims=True)
    grad_x = inverse * (scaled - jnp.mean(scaled, axis=1, keepdims=True) - unit * inner)
    return grad_x, grad_gain, grad_offset


def split_by_core(turned, keep, give):
    core = lax.axis_index("seq") % 2
    for j in range(keep.shape[0]):
        keep[j] = turned[pl.ds(pl.multiple_of(j * 64 + core * 32, 32), 32), :]
        give[j] = turned[pl.ds(pl.multiple_of(j * 64 + (1 - core) * 32, 32), 32), :]


def fetched(sources, targets, sems):
    copies = [pltpu.make_async_copy(a, b, sems.at[i]) for i, (a, b) in enumerate(zip(sources, targets))]
    for copy in copies:
        copy.start()
    return copies


def project_kernel(x, gain, offset, qk_far, value_far, msg, normed_out, keep, give, turned, w_qk, w_value, sems):
    copies = fetched((qk_far, value_far), (w_qk, w_value), sems)
    normed = layer_rows(x[...].astype(F32), gain[...], offset[...])
    low = normed.astype(BF16)
    normed_out[...] = low
    for copy in copies:
        copy.wait()
    for h in range(HEADS):
        at = slice(h * DH, (h + 1) * DH)
        q = jnp.dot(low, w_qk[:, at], preferred_element_type=F32).astype(BF16)
        v = jnp.dot(low, w_value[:, at], preferred_element_type=F32).astype(BF16)
        for t in range(2):
            msg[h * 2 + t, :, :DH] = q
            msg[h * 2 + t, :, DH:] = v
    turned[...] = jnp.transpose(low.astype(F32)).astype(BF16)
    split_by_core(turned, keep, give)


def project(x, gain, offset, w_qk, w_value):
    rows, width = x.shape
    chips = 2 * HEADS
    return pl.pallas_call(
        project_kernel,
        out_shape=[
            sd((chips, rows, 2 * DH), BF16),
            sd((rows, width), BF16),
            sd((width // 64, 32, rows), BF16),
            sd((width // 64, 32, rows), BF16),
        ],
        in_specs=vm(3) + anywhere(2),
        out_specs=vm(4),
        scratch_shapes=[pltpu.VMEM((width, rows), BF16)]
        + [pltpu.VMEM((width, width), BF16)] * 2
        + [pltpu.SemaphoreType.DMA((2,))],
        compiler_params=params(60),
        name="project",
        cost_estimate=takes(7),
    )(x, gain, offset, w_qk, w_value)


BLOCK = 8 * SPAN
SAFE = 60.0


def repeat(count, body, width=4):
    def several(i, c):
        for u in range(width):
            body(i * width + u)
        return c

    lax.fori_loop(0, count // width, several, 0)


def even(first, count):
    return pl.ds(2 * first, count, stride=2)


def odd(first, count):
    return pl.ds(2 * first + 1, count, stride=2)


def gather_pairs(order, base, src, slot):
    for u in range(BLOCK):
        place = 2 * order[base + u]
        slot[2 * u : 2 * u + 1, :] = src[pl.ds(place, 1), :]
        slot[2 * u + 1 : 2 * u + 2, :] = src[pl.ds(place + 1, 1), :]


def scatter_pairs(order, base, slot, dst):
    for u in range(BLOCK):
        dst[pl.ds(pl.multiple_of(2 * order[base + u], 2), 2), :] = slot[2 * u : 2 * u + 2, :]


def attend_kernel(order, mine, other, bias_in, msg, q_far, keys_far, vals_far, probs_far, came_all, sent_all, *rest):
    slots, (q_out, keys, vals, probs, bias, sems) = rest[:4], rest[4:]
    load = pltpu.make_async_copy(bias_in, bias, sems.at[0])
    load.start()
    length = q_out.shape[0]
    blocks = length // BLOCK
    core = lax.axis_index("seq") % 2
    came, done = slots[0:2], slots[2:4]

    def widen(j):
        for rows, side in ((mine, core), (other, 1 - core)):
            first = pl.multiple_of((2 * j + side) * 256, 256)
            came_all[even(first, 256), :] = rows[j, :, :DH].astype(F32)
            came_all[odd(first, 256), :] = rows[j, :, DH:].astype(F32)

    repeat(length // 512, widen, 2)

    def gather(b, slot):
        gather_pairs(order, b * BLOCK, came_all, slot)

    def scatter(b, slot):
        scatter_pairs(order, b * BLOCK, slot, sent_all)

    def ready(b, slot):
        q = slot[even(0, BLOCK), :]
        unit = q * lax.rsqrt(jnp.sum(q * q, axis=1, keepdims=True) + EPS_KEY)
        ahead = pl.ds(pl.multiple_of(b * BLOCK + SPAN, SPAN), BLOCK)
        keys[ahead, :] = unit.astype(BF16)
        vals[ahead, :] = slot[odd(0, BLOCK), :].astype(BF16)
        return q.astype(BF16)

    load.wait()
    gather(blocks - 1, came[1])
    ready(blocks - 1, came[1])
    keys[0:SPAN, :] = keys[length : length + SPAN, :]
    vals[0:SPAN, :] = vals[length : length + SPAN, :]
    gather(0, came[0])

    def compute(b, slot, out):
        base = pl.multiple_of(b * BLOCK, BLOCK)
        q = ready(b, slot)
        q_out[pl.ds(base, BLOCK), :] = q
        k = keys[pl.ds(base, BLOCK + SPAN), :]
        v = vals[pl.ds(base, BLOCK + SPAN), :]
        spans = range(BLOCK // SPAN)
        s = [
            lax.dot_general(
                q[u * SPAN : u * SPAN + SPAN], k[u * SPAN : u * SPAN + 2 * SPAN], ACROSS, preferred_element_type=F32
            )
            for u in spans
        ]
        s = jnp.concatenate(s, axis=0) * SCALE + bias[pl.ds(base, BLOCK), :].astype(F32)
        top = jnp.max(s, axis=1, keepdims=True)
        e = jnp.exp(s - top)
        total = jnp.sum(e, axis=1, keepdims=True)
        p = (e * (1.0 / total)).astype(BF16)
        probs[pl.ds(base, BLOCK), :] = p
        for u in spans:
            out[even(u * SPAN, SPAN), :] = jnp.dot(
                p[u * SPAN : u * SPAN + SPAN], v[u * SPAN : u * SPAN + 2 * SPAN], preferred_element_type=F32
            )
        out[odd(0, BLOCK), :] = jnp.broadcast_to(top + jnp.log(total), (BLOCK, DH))

    def step(i, c):
        b = 2 * i
        scatter(jnp.maximum(b - 1, 0), done[1])
        gather(b + 1, came[1])
        compute(b, came[0], done[0])
        scatter(b, done[0])
        gather(jnp.minimum(b + 2, blocks - 1), came[0])
        compute(b + 1, came[1], done[1])
        return c

    lax.fori_loop(0, blocks // 2, step, 0)
    pairs = ((q_out, q_far), (keys, keys_far), (vals, vals_far), (probs, probs_far))
    stores = [pltpu.make_async_copy(src, dst, sems.at[1 + n]) for n, (src, dst) in enumerate(pairs)]
    for store in stores:
        store.start()
    scatter(blocks - 1, done[1])

    across = lax.broadcasted_iota(jnp.int32, (128, 128), 0)
    eye = across == lax.broadcasted_iota(jnp.int32, (128, 128), 1)

    line = lax.broadcasted_iota(jnp.int32, (EXTRA, 6 * 128), 0)
    lane = lax.broadcasted_iota(jnp.int32, (EXTRA, 6 * 128), 1)
    pick = jnp.where(line == lane // 128, 1.0, 0.0).astype(BF16)

    def send(b):
        msg[b, 0:256, :] = sent_all[even(b * 256, 256), :].astype(BF16)
        parts = []
        for half in range(2):
            parts += split3(jnp.where(eye, sent_all[odd(b * 256 + half * 128, 128), :], 0.0))
        tail = jnp.dot(pick, jnp.concatenate(parts, axis=0), preferred_element_type=F32)
        msg[b, 256:, :] = tail.astype(BF16)

    repeat(length // 256, send)
    for store in stores:
        store.wait()


def attend(order, mine, other, bias):
    length = order.shape[0]
    kept = [(length, DH), (length + SPAN, DH), (length + SPAN, DH), (length, DH)]
    return pl.pallas_call(
        attend_kernel,
        out_shape=[sd((length // 256, 256 + EXTRA, DH), BF16)] + [sd(shape, BF16) for shape in kept],
        in_specs=[pl.BlockSpec(memory_space=pltpu.SMEM)] + vm(2) + anywhere(1),
        out_specs=vm(1) + anywhere(4),
        scratch_shapes=[pltpu.VMEM((2 * length, DH), F32)] * 2
        + [pltpu.VMEM((2 * BLOCK, DH), F32)] * 4
        + [pltpu.VMEM(shape, BF16) for shape in kept]
        + [pltpu.VMEM((length, 2 * SPAN), BF16), pltpu.SemaphoreType.DMA((5,))],
        compiler_params=params(60),
        name="attend",
        cost_estimate=takes(35),
    )(order, mine, other, bias)


def back_kernel(order, msg, *refs):
    far, (keep, give, came_all, sent_all, first_u, first_v, late), slots = refs[:4], refs[4:11], refs[11:15]
    near, sems = refs[15:19], refs[19]
    q_in, keys, vals, probs = near
    loads = [pltpu.make_async_copy(src, dst, sems.at[n]) for n, (src, dst) in enumerate(zip(far, near))]
    for load in loads:
        load.start()
    length = probs.shape[0]
    blocks = length // BLOCK
    core = lax.axis_index("seq") % 2
    came, done = slots[0:2], slots[2:4]
    late_u, late_v, late_q = late.at[0], late.at[1], late.at[2]
    across = lax.broadcasted_iota(jnp.int32, (128, 128), 0)
    eye = across == lax.broadcasted_iota(jnp.int32, (128, 128), 1)
    ones = jnp.ones((128, 128), BF16)

    def widen(b):
        came_all[even(b * 256, 256), :] = msg[b, 0:256, :].astype(F32)
        t = msg[b, 256:, :].astype(F32)
        for half in range(2):
            total = jnp.zeros((128, 128), F32)
            for k in range(3):
                row = half * 3 + k
                spot = jnp.where(eye, jnp.broadcast_to(t[row : row + 1], (128, 128)), 0.0).astype(BF16)
                total = total + jnp.dot(spot, ones, preferred_element_type=F32)
            came_all[odd(b * 256 + half * 128, 128), :] = total

    repeat(length // 256, widen)

    def scatter(b, slot):
        base = jnp.where(b == 0, length, b * BLOCK) - SPAN
        for u in range(BLOCK):
            if u == SPAN:
                base = b * BLOCK - SPAN
            sent_all[pl.ds(pl.multiple_of(2 * order[base + u], 2), 2), :] = slot[2 * u : 2 * u + 2, :]

    gather_pairs(order, 0, came_all, came[0])
    for load in loads:
        load.wait()
    late[...] = jnp.zeros(late.shape, F32)
    spans = range(BLOCK // SPAN)
    cut = lambda a, u, n=1: a[u * SPAN : (u + n) * SPAN]

    def whole(direct, unit_grad, q):
        q = q.astype(F32)
        r = lax.rsqrt(jnp.sum(q * q, axis=1, keepdims=True) + EPS_KEY)
        along = jnp.sum(q * unit_grad, axis=1, keepdims=True)
        return direct + r * unit_grad - q * (r * r * r * along)

    def compute(b, slot, out):
        base = pl.multiple_of(b * BLOCK, BLOCK)
        g = slot[even(0, BLOCK), :].astype(BF16)
        p = probs[pl.ds(base, BLOCK), :]
        v = vals[pl.ds(base, BLOCK + SPAN), :]
        k = keys[pl.ds(base, BLOCK + SPAN), :]
        q = q_in[pl.ds(base, BLOCK), :]
        back = q_in[pl.ds(pl.multiple_of(jnp.maximum(base - SPAN, 0), SPAN), SPAN), :]
        gp = [lax.dot_general(cut(g, u), cut(v, u, 2), ACROSS, preferred_element_type=F32) for u in spans]
        wide_v = [lax.dot_general(cut(p, u), cut(g, u), FLIP, preferred_element_type=F32) for u in spans]
        gs = p.astype(F32) * (jnp.concatenate(gp, axis=0) - slot[odd(0, BLOCK), :])
        d = (gs * SCALE).astype(BF16)
        direct = [jnp.dot(cut(d, u), cut(k, u, 2), preferred_element_type=F32) for u in spans]
        wide_u = [lax.dot_general(cut(d, u), cut(q, u), FLIP, preferred_element_type=F32) for u in spans]

        @pl.when(b == 0)
        def _():
            first_u[...] = wide_u[0][:SPAN]
            first_v[...] = wide_v[0][:SPAN]

        folded_u = [late_u[...] + wide_u[0][:SPAN]] + [wide_u[u - 1][SPAN:] + wide_u[u][:SPAN] for u in spans[1:]]
        folded_v = [late_v[...] + wide_v[0][:SPAN]] + [wide_v[u - 1][SPAN:] + wide_v[u][:SPAN] for u in spans[1:]]
        straight = jnp.concatenate([late_q[...]] + direct[:-1], axis=0)
        behind = jnp.concatenate([back, q[: BLOCK - SPAN]], axis=0)
        out[even(0, BLOCK), :] = whole(straight, jnp.concatenate(folded_u, axis=0), behind)
        out[odd(0, BLOCK), :] = jnp.concatenate(folded_v, axis=0)
        late_u[...] = wide_u[-1][SPAN:]
        late_v[...] = wide_v[-1][SPAN:]
        late_q[...] = direct[-1]

    def step(i, c):
        b = 2 * i
        scatter(jnp.maximum(b - 1, 0), done[1])
        gather_pairs(order, (b + 1) * BLOCK, came_all, came[1])
        compute(b, came[0], done[0])
        scatter(b, done[0])
        gather_pairs(order, jnp.minimum(b + 2, blocks - 1) * BLOCK, came_all, came[0])
        compute(b + 1, came[1], done[1])
        return c

    lax.fori_loop(0, blocks // 2, step, 0)
    scatter(blocks - 1, done[1])
    done[0][even(0, SPAN), :] = whole(late_q[...], late_u[...] + first_u[...], q_in[length - SPAN : length, :])
    done[0][odd(0, SPAN), :] = late_v[...] + first_v[...]
    for u in range(SPAN):
        place = 2 * order[length - SPAN + u]
        sent_all[pl.ds(place, 1), :] = done[0][2 * u : 2 * u + 1, :]
        sent_all[pl.ds(place + 1, 1), :] = done[0][2 * u + 1 : 2 * u + 2, :]

    def narrow(j):
        for out, side in ((keep, core), (give, 1 - core)):
            first = pl.multiple_of((2 * j + side) * 256, 256)
            out[j, :, :DH] = sent_all[even(first, 256), :].astype(BF16)
            out[j, :, DH:] = sent_all[odd(first, 256), :].astype(BF16)

    repeat(keep.shape[0], narrow)


def attend_back(order, msg, q_in, keys, vals, probs):
    length = probs.shape[0]
    half = length // 512
    kept = [array.shape for array in (q_in, keys, vals, probs)]
    return pl.pallas_call(
        back_kernel,
        out_shape=[sd((half, 256, 2 * DH), BF16)] * 2,
        in_specs=[pl.BlockSpec(memory_space=pltpu.SMEM)] + vm(1) + anywhere(4),
        out_specs=vm(2),
        scratch_shapes=[pltpu.VMEM((2 * length, DH), F32)] * 2
        + [pltpu.VMEM((SPAN, DH), F32)] * 2
        + [pltpu.VMEM((3, SPAN, DH), F32)]
        + [pltpu.VMEM((2 * BLOCK, DH), F32)] * 4
        + [pltpu.VMEM(shape, BF16) for shape in kept]
        + [pltpu.SemaphoreType.DMA((4,))],
        compiler_params=params(60),
        name="attend_back",
        cost_estimate=takes(36),
    )(order, msg, q_in, keys, vals, probs)


def prepare(bucket_row, ends):
    length = bucket_row.shape[0]
    places = jnp.arange(length, dtype=jnp.int32)
    _, order = lax.sort((bucket_row * length + places, places), num_keys=1)
    pos = order.reshape(-1, SPAN)
    start = jnp.max(jnp.where(ends <= pos[..., None], ends, 0), axis=-1)
    window = jnp.concatenate([jnp.roll(pos, 1, 0), pos], axis=1)
    k, q = window[:, None, :], pos[:, :, None]
    bias = jnp.where((k >= start[:, :, None]) & (k <= q), jnp.where(k == q, -1000.0, 0.0), -1e9)
    return order, bias.astype(BF16).reshape(length, 2 * SPAN)


def combine_kernel(
    msg, x, w_out, gain, offset, mix, first_out, first_low, normed, weights, keep, give, low_mix, turned
):
    rows = x.shape[0]
    for half in range(2):
        logs = []
        for r in range(ROUNDS):
            lines = []
            for h in range(HEADS):
                tail = msg[h * ROUNDS + r, rows : rows + EXTRA, :].astype(F32)
                k = half * 3
                lines.append(tail[k : k + 1] + tail[k + 1 : k + 2] + tail[k + 2 : k + 3])
            logs.append(jnp.concatenate(lines, axis=0))
        top = jnp.maximum(jnp.maximum(logs[0], logs[1]), jnp.maximum(logs[2], logs[3]))
        powers = [jnp.exp(v - top) for v in logs]
        inverse = 1.0 / (powers[0] + powers[1] + powers[2] + powers[3])
        lines = [v * inverse for v in powers]
        lines.append(jnp.zeros((128 - HEADS * ROUNDS, 128), F32))
        weights[half * 128 : half * 128 + 128, :] = jnp.transpose(jnp.concatenate(lines, axis=0))
    for h in range(HEADS):
        total = jnp.zeros((rows, DH), F32)
        for r in range(ROUNDS):
            j = r * HEADS + h
            total = total + weights[:, j : j + 1] * msg[h * ROUNDS + r, 0:rows, :].astype(F32)
        mix[:, h * DH : (h + 1) * DH] = total
        low_mix[:, h * DH : (h + 1) * DH] = total.astype(BF16)
    first = x[...].astype(F32) + jnp.dot(low_mix[...], w_out[...], preferred_element_type=F32)
    first_out[...] = first
    first_low[...] = first.astype(BF16)
    normed[...] = layer_rows(first, gain[...], offset[...]).astype(BF16)
    turned[...] = jnp.transpose(mix[...]).astype(BF16)
    split_by_core(turned, keep, give)


def combine(msg, x, w_out, gain, offset):
    rows, width = x.shape
    return pl.pallas_call(
        combine_kernel,
        out_shape=[
            sd((rows, width), F32),
            sd((rows, width), F32),
            sd((rows, width), BF16),
            sd((rows, width), BF16),
            sd((rows, 128), F32),
            sd((width // 64, 32, rows), BF16),
            sd((width // 64, 32, rows), BF16),
        ],
        in_specs=vm(5),
        out_specs=vm(7),
        scratch_shapes=[pltpu.VMEM((rows, width), BF16), pltpu.VMEM((width, rows), BF16)],
        compiler_params=params(60),
        name="combine",
        cost_estimate=takes(6),
    )(msg, x, w_out, gain, offset)


def far_copies(own, far, to, sems, first, flip, pieces):
    out = []
    for i in pieces:
        dst = to.at[(i + 1) // 2, pl.ds((i - 1) % 2 * 512, 512)] if i else to.at[0]
        src = (far[i + 5] if flip else far[i - 1]).at[pl.ds(0, 512)] if i else own
        out.append(pltpu.make_async_copy(src, dst, sems.at[first + i]))
    return out


def start_copies(copies):
    core = lax.axis_index("seq") % 2
    for side in range(2):

        @pl.when(core == side)
        def _():
            for c in copies(side == 1):
                c.start()


def wait_copies(own, far, to, sems, first, k):
    for c in far_copies(own, far, to, sems, first, False, (2 * k - 1, 2 * k) if k else (0,)):
        c.wait()


def gelu_both(act, grad):
    share = 0.5 + 0.5 * lax.erf(act * 0.7071067811865476)
    slope = share + act * (jnp.exp(act * act * -0.5) * 0.3989422804014327)
    return (act * share).astype(BF16), (grad * slope).astype(BF16)


def middle_kernel(*refs):
    normed, g_two, up0, down0, far = refs[0], refs[1], refs[2], refs[3], refs[4:16]
    grad_normed, hid, pre0, up, down, pre, sems = refs[16:]
    pieces = range(7)
    start_copies(
        lambda flip: far_copies(up0, far, up, sems, 0, flip, pieces)
        + far_copies(down0, far, down, sems, 7, not flip, pieces)
    )
    for k in range(4):
        wait_copies(up0, far, up, sems, 0, k)
        wait_copies(down0, far, down, sems, 7, k)

        def hidden_part(i, c):
            for u in range(2):
                at = pl.ds(pl.multiple_of(i * 512 + u * 256, 256), 256)
                act = jnp.dot(normed[...], up[k, :, at], preferred_element_type=F32)
                grad = jnp.dot(g_two[...], down[k, :, at], preferred_element_type=F32)
                hid[k, :, at], pre[k, :, at] = gelu_both(act, grad)
            return c

        lax.fori_loop(0, 2, hidden_part, 0)
    pre0[...] = pre[0]
    grad_normed[...] = jnp.zeros(grad_normed.shape, F32)

    def up_back(k, c):
        grad_normed[...] += lax.dot_general(pre[k], up[k], ACROSS, preferred_element_type=F32)
        return c

    lax.fori_loop(0, 4, up_back, 0)


def middle(normed, g_two, up0, down0, far):
    rows, width = normed.shape
    return pl.pallas_call(
        middle_kernel,
        out_shape=[sd((rows, width), F32), sd((4, rows, 1024), BF16), sd((rows, 1024), BF16)],
        in_specs=vm(2) + anywhere(14),
        out_specs=vm(3),
        scratch_shapes=[
            pltpu.VMEM((4, width, 1024), BF16),
            pltpu.VMEM((4, width, 1024), BF16),
            pltpu.VMEM((4, rows, 1024), BF16),
            pltpu.SemaphoreType.DMA((14,)),
        ],
        compiler_params=params(28),
        name="middle",
        cost_estimate=takes(16),
    )(normed, g_two, up0, down0, *far)


def uncombine_kernel(
    grad_normed, mix, first, weights, g_one, w_out, gain, grad_first, sent, grad_gain, grad_offset, low_first
):
    rows = g_one.shape[0]
    grad_x, gg, go = layer_back(first[...], grad_normed[...], gain[...])
    grad_gain[...] = gg
    grad_offset[...] = go
    grad_x = grad_x + g_one[...].astype(F32)
    grad_first[...] = grad_x
    low_first[...] = grad_x.astype(BF16)
    lane = lax.broadcasted_iota(jnp.int32, (rows, 128), 1)
    inner = jnp.zeros((rows, 128), F32)
    for h in range(HEADS):
        at = slice(h * DH, (h + 1) * DH)
        grad_mix = lax.dot_general(low_first[...], w_out[at, :], ACROSS, preferred_element_type=F32)
        dots = jnp.sum(grad_mix * mix[:, at], axis=1, keepdims=True)
        inner = jnp.where(lane % HEADS == h, dots, inner)
        for r in range(ROUNDS):
            j = r * HEADS + h
            sent[h * ROUNDS + r, 0:rows, :] = (weights[:, j : j + 1] * grad_mix).astype(BF16)
    inner = inner * weights[...]
    low_lines = [p.astype(F32) for p in split3(jnp.transpose(inner[0:128]))]
    high_lines = [p.astype(F32) for p in split3(jnp.transpose(inner[128:256]))]
    blank = jnp.zeros((EXTRA - 6, 128), F32)
    for h in range(HEADS):
        for r in range(ROUNDS):
            j = r * HEADS + h
            tail = [p[j : j + 1] for p in low_lines + high_lines] + [blank]
            sent[h * ROUNDS + r, rows : rows + EXTRA, :] = jnp.concatenate(tail, axis=0).astype(BF16)


def uncombine(grad_normed, mix, first, weights, g_one, w_out, gain):
    rows, width = g_one.shape
    return pl.pallas_call(
        uncombine_kernel,
        out_shape=[
            sd((rows, width), F32),
            sd((HEADS * ROUNDS, rows + EXTRA, DH), BF16),
            sd((1, width), F32),
            sd((1, width), F32),
            sd((rows, width), BF16),
        ],
        in_specs=vm(7),
        out_specs=vm(5),
        compiler_params=params(16),
        name="uncombine",
        cost_estimate=takes(8),
    )(grad_normed, mix, first, weights, g_one, w_out, gain)


def down_out_kernel(*refs):
    hid, x, down0, far = refs[0], refs[1], refs[2], refs[3:15]
    out, down, summed, sems = refs[15:]
    start_copies(lambda flip: far_copies(down0, far, down, sems, 0, not flip, range(7)))
    summed[...] = x[...].astype(F32)
    for k in range(4):
        wait_copies(down0, far, down, sems, 0, k)
        summed[...] += lax.dot_general(hid[k], down[k], ACROSS, preferred_element_type=F32)
    out[...] = summed[...].astype(BF16)


def down_out(hid, x, down0, far):
    rows, width = x.shape
    return pl.pallas_call(
        down_out_kernel,
        out_shape=sd((rows, width), BF16),
        in_specs=vm(2) + anywhere(13),
        out_specs=pl.BlockSpec(memory_space=pltpu.VMEM),
        scratch_shapes=[
            pltpu.VMEM((4, width, 1024), BF16),
            pltpu.VMEM((rows, width), F32),
            pltpu.SemaphoreType.DMA((7,)),
        ],
        compiler_params=params(60),
        name="down_out",
        cost_estimate=takes(6),
    )(hid, x, down0, *far)


def begin(moves, sems):
    copies = [pltpu.make_async_copy(src, dst, sems.at[i]) for i, (src, dst) in enumerate(moves)]
    for c in copies:
        c.start()
    return copies


def last_rows(array, to, k):
    rows = to.shape[1]
    return (array.at[pl.ds(array.shape[0] - rows, rows)], to.at[k])


def peer_hidden(rows_in, grads_in, k, up, down, hid, pre, to):
    def hidden_part(i, c):
        for u in range(2):
            at = pl.ds(pl.multiple_of(i * 512 + u * 256, 256), 256)
            act = jnp.dot(rows_in[k], up[:, at], preferred_element_type=F32)
            grad = jnp.dot(grads_in[k], down[:, at], preferred_element_type=F32)
            hid[to, :, at], pre[to, :, at] = gelu_both(act, grad)
        return c

    lax.fori_loop(0, 2, hidden_part, 0)


def peers_kernel(*refs):
    normed, grads, ahead, behind, g1, g3, g2, weights_up, weights_down = refs[:9]
    hid, pre, turned_grads, turned_rows, rows_in, grads_in, up, down, sems = refs[9:]
    moves = [(weights_up, up), (weights_down, down)]
    moves += [(ahead, rows_in.at[1]), last_rows(g1, grads_in, 1)]
    moves += [(behind, rows_in.at[2]), last_rows(g3, grads_in, 2)]
    moves += [(normed, rows_in.at[0]), (grads, grads_in.at[0]), last_rows(g2, grads_in, 3)]
    copies = begin(moves, sems)
    for k, ready in ((1, copies[:4]), (2, copies[4:6])):
        for c in ready:
            c.wait()
        peer_hidden(rows_in, grads_in, k, up, down, hid, pre, k - 1)
    for c in copies[6:]:
        c.wait()
    count, rows, width = grads_in.shape
    turned_grads[...] = jnp.transpose(grads_in[...].reshape(count * rows, width))
    turned_rows[...] = jnp.transpose(rows_in[...].reshape((count - 1) * rows, width))


def peers(normed, grads, ahead, behind, g1, g3, g2, up, down):
    rows, width = normed.shape
    return pl.pallas_call(
        peers_kernel,
        out_shape=[sd((2, rows, 1024), BF16)] * 2 + [sd((width, 4 * rows), BF16), sd((width, 3 * rows), BF16)],
        in_specs=anywhere(9),
        out_specs=vm(4),
        scratch_shapes=[pltpu.VMEM((3, rows, 1024), BF16), pltpu.VMEM((4, rows, 1024), BF16)]
        + [pltpu.VMEM((width, 1024), BF16)] * 2
        + [pltpu.SemaphoreType.DMA((9,))],
        compiler_params=params(60),
        name="peers",
        cost_estimate=takes(9),
    )(normed, grads, ahead, behind, g1, g3, g2, up, down)


def feed_kernel(*refs):
    (hid_own, pre_own, hid_near, pre_near, left_grads, left_rows, g2) = refs[:7]
    across, weights_up, weights_down, out = refs[7:11]
    rows_in, grads_in, hid, pre, up, down, turned_grads, turned_rows, sems = refs[11:]
    rows = pre_own.shape[0]
    moves = [(weights_up, up), (weights_down, down), (across, rows_in.at[0]), last_rows(g2, grads_in, 0)]
    moves += [(left_rows, turned_rows.at[:, pl.ds(0, 3 * rows)]), (pre_own, pre.at[0])]
    moves += [(pre_near, pre.at[pl.ds(1, 2)]), (left_grads, turned_grads), (hid_own.at[0], hid.at[0])]
    moves += [(hid_near, hid.at[pl.ds(1, 2)])]
    copies = begin(moves, sems)
    for c in copies[:4]:
        c.wait()
    peer_hidden(rows_in, grads_in, 0, up, down, hid, pre, 3)
    for c in copies[4:7]:
        c.wait()
    turned_rows[:, 3 * rows :] = jnp.transpose(rows_in[0])
    for first, turned, rights in ((0, turned_rows, pre), (1024, turned_grads, hid)):
        if first:
            for c in copies[7:]:
                c.wait()

        def piece(i, c):
            left = turned[pl.ds(pl.multiple_of(i * 256, 256), 256), :]
            total = jnp.dot(left, rights[...].reshape(4 * rows, 1024), preferred_element_type=F32).astype(BF16)
            for j in range(8):
                out[j * 4 + i, :, first : first + 1024] = total[j * 32 : j * 32 + 32]
            return c

        lax.fori_loop(0, 4, piece, 0)


def feed(hid_own, pre_own, hid_near, pre_near, left_grads, left_rows, g2, across, up, down):
    rows, width = pre_own.shape[0], up.shape[0]
    return pl.pallas_call(
        feed_kernel,
        out_shape=sd((width // 32, 32, 2048), BF16),
        in_specs=anywhere(10),
        out_specs=pl.BlockSpec(memory_space=pltpu.VMEM),
        scratch_shapes=[pltpu.VMEM((1, rows, 1024), BF16)] * 2
        + [pltpu.VMEM((4, rows, 1024), BF16)] * 2
        + [pltpu.VMEM((width, 1024), BF16)] * 2
        + [pltpu.VMEM((width, 4 * rows), BF16)] * 2
        + [pltpu.SemaphoreType.DMA((10,))],
        compiler_params=params(60),
        name="feed",
        cost_estimate=takes(12),
    )(hid_own, pre_own, hid_near, pre_near, left_grads, left_rows, g2, across, up, down)


def sum_rounds_kernel(back, out):
    for h in range(HEADS):
        total = back[2 * h].astype(F32) + back[2 * h + 1].astype(F32)
        for half in range(2):
            at = slice(half * HEADS * DH + h * DH, half * HEADS * DH + (h + 1) * DH)
            out[:, at] = total[:, half * DH : (half + 1) * DH].astype(BF16)


def sum_rounds(back):
    rows = back.shape[1]
    return pl.pallas_call(
        sum_rounds_kernel,
        out_shape=sd((rows, 2 * HEADS * DH), BF16),
        in_specs=vm(1),
        out_specs=pl.BlockSpec(memory_space=pltpu.VMEM),
        compiler_params=params(8),
        name="sum_rounds",
        cost_estimate=takes(3),
    )(back)


def finish_kernel(grads, x, gain, qk_far, value_far, grad_two, gain_two, offset_two, grad_second, small, *scratch):
    near, far, w_qk, w_value, sems = scratch
    width = x.shape[1]
    copies = fetched((qk_far, value_far), (w_qk, w_value), sems)
    copies[0].wait()
    grad_normed = lax.dot_general(grads[:, :width], w_qk[...], ACROSS, preferred_element_type=F32)
    copies[1].wait()
    grad_normed = grad_normed + lax.dot_general(grads[:, width:], w_value[...], ACROSS, preferred_element_type=F32)
    grad_x, gg, go = layer_back(x[...].astype(F32), grad_normed, gain[...])
    grad_second[...] = grad_x + grad_two[...].astype(F32)
    lines = []
    for line in (gg, go, gain_two[...], offset_two[...]):
        high = line.astype(BF16).astype(F32)
        lines += [high, line - high]
    blank = jnp.zeros((8, width), F32)
    rest = jnp.zeros((112, width), F32)
    near[...] = jnp.transpose(jnp.concatenate(lines + [blank, rest], axis=0))
    far[...] = jnp.transpose(jnp.concatenate([blank] + lines + [rest], axis=0))
    core = lax.axis_index("seq") % 2
    for j in range(small.shape[0]):
        a = near[pl.ds(pl.multiple_of(j * 64 + core * 32, 32), 32), :]
        b = far[pl.ds(pl.multiple_of(j * 64 + (1 - core) * 32, 32), 32), :]
        small[j] = (a + b).astype(BF16)


def finish(grads, x, gain, w_qk, w_value, grad_two, gain_two, offset_two):
    rows, width = x.shape
    return pl.pallas_call(
        finish_kernel,
        out_shape=[sd((rows, width), F32), sd((width // 64, 32, 128), BF16)],
        in_specs=vm(3) + anywhere(2) + vm(3),
        out_specs=vm(2),
        scratch_shapes=[pltpu.VMEM((width, 128), F32)] * 2
        + [pltpu.VMEM((width, width), BF16)] * 2
        + [pltpu.SemaphoreType.DMA((2,))],
        compiler_params=params(60),
        name="finish",
        cost_estimate=takes(5),
    )(grads, x, gain, w_qk, w_value, grad_two, gain_two, offset_two)


def pair_kernel(left, left_other, right, right_other, *rest):
    blocks, lines, rows = left.shape
    out, width = rest[-1], right.shape[1]
    total = jnp.dot(left[...].reshape(blocks * lines, rows), right[...], preferred_element_type=F32)
    total = total + jnp.dot(left_other[...].reshape(blocks * lines, rows), right_other[...], preferred_element_type=F32)
    out[:, :, :width] = total.astype(BF16).reshape(blocks, lines, width)
    for extra in rest[:-1]:
        out[:, :, width : width + extra.shape[2]] = extra[...]
        width += extra.shape[2]


def pair(left, left_other, right, right_other, *extra):
    blocks, lines, rows = left.shape
    width = right.shape[1] + sum(e.shape[2] for e in extra)
    return pl.pallas_call(
        pair_kernel,
        out_shape=sd((blocks, lines, width), BF16),
        in_specs=vm(4 + len(extra)),
        out_specs=pl.BlockSpec(memory_space=pltpu.VMEM),
        compiler_params=params(60),
        name="pair",
        cost_estimate=takes(3),
    )(left, left_other, right, right_other, *extra)


def swap_seq(array):
    return lax.all_to_all(array, "seq", split_axis=0, concat_axis=0, tiled=True)


def same_core():
    count = lax.axis_size("seq")
    return [list(range(c, count, 2)) for c in range(2)]


def along_x_and_core():
    return [[y * 8 + x * 2 + c for x in range(4) for c in range(2)] for y in range(4)]


def along_y():
    return [[y * 8 + x * 2 + c for y in range(4)] for x in range(4) for c in range(2)]


def swap_chips(array):
    return lax.all_to_all(
        array, "seq", split_axis=0, concat_axis=0, tiled=True, axis_index_groups=same_core()
    )


def flip_bit(array, axis, bit):
    return lax.ppermute(array, axis, [(i, i ^ bit) for i in range(lax.axis_size(axis))])


def swap_cores(array):
    return flip_bit(array, "seq", 1)


def from_ahead(array, step):
    count = lax.axis_size("ffn")
    return lax.ppermute(array, "ffn", [((i + step) % count, i) for i in range(count)])


def tied(array, *others):
    return lax.optimization_barrier((array, others))[0]


def add_low(a, b):
    return (a.astype(F32) + b.astype(F32)).astype(BF16)


def shards(
    stream_one,
    stream_two,
    doc_lengths,
    bucket_ids,
    norm1_gain,
    norm1_bias,
    w_qk,
    w_value,
    w_out,
    norm2_gain,
    norm2_bias,
    w_up,
    w_down,
    grad_out_one,
    grad_out_two,
):
    rows, width = stream_one.shape[1:]
    seq, ffn = lax.axis_index("seq"), lax.axis_index("ffn")
    core = seq % 2
    gain_one, bias_one = norm1_gain.reshape(1, -1), norm1_bias.reshape(1, -1)
    gain_two, bias_two = norm2_gain.reshape(1, -1), norm2_bias.reshape(1, -1)

    msg, normed_one, keep_rows, give_rows = project(stream_two[0], gain_one, bias_one, w_qk, w_value)
    received = swap_chips(msg)
    top, low = [jnp.where(core == 0, w_up[at], w_down[at]) for at in (slice(0, 512), slice(512, 1024))]
    buckets, top, low = lax.optimization_barrier((bucket_ids[0, 0], top, low))
    top1, low3 = from_ahead(top, 1), from_ahead(low, 3)
    order, bias = prepare(buckets, jnp.cumsum(doc_lengths[0]))
    received, order, bias, top, low, top1, low3 = lax.optimization_barrier(
        (received, order, bias, top, low, top1, low3)
    )
    came = swap_cores(received)
    lowg1 = from_ahead(jnp.concatenate([low, grad_out_two[0]], axis=0), 1)
    topg3 = from_ahead(jnp.concatenate([top, grad_out_two[0]], axis=0), 3)
    other_rows = swap_cores(give_rows)
    top1_other, low3_other = swap_cores(top1), swap_cores(low3)
    sent, queries, keys, vals, probs = attend(order, received, came, bias)
    sent, top1, low3, lowg1, topg3, top1_other, low3_other, other_rows = lax.optimization_barrier(
        (sent, top1, low3, lowg1, topg3, top1_other, low3_other, other_rows)
    )
    per_round = swap_seq(sent)
    top2, low2 = from_ahead(top1, 1), from_ahead(low3, 3)
    lowg1_other, topg3_other = swap_cores(lowg1), swap_cores(topg3)
    per_round, top2, low2, lowg1_other, topg3_other = lax.optimization_barrier(
        (per_round, top2, low2, lowg1_other, topg3_other)
    )
    far_weights = [top1, lowg1, top2, low2, topg3, low3]
    far_weights += [top1_other, lowg1_other, swap_cores(top2), swap_cores(low2), topg3_other, low3_other]
    grads2 = from_ahead(topg3[512:], 3)
    mix, first, one_low, normed_two, weights, keep_mix, give_mix = combine(per_round, stream_one[0], w_out, gain_two, bias_two)
    ahead, behind = from_ahead(normed_two, 1), from_ahead(normed_two, 3)
    grad_normed, hid, pre0 = middle(normed_two, grad_out_two[0], w_up, w_down, far_weights)
    grad_normed, ahead, behind, grads2 = lax.optimization_barrier((grad_normed, ahead, behind, grads2))
    across = from_ahead(ahead, 1)
    grad_first, msg, grad_gain_two, grad_bias_two, low_first = uncombine(
        grad_normed, mix, first, weights, grad_out_one[0], w_out, gain_two
    )
    far = swap_seq(msg)
    part_out = pair(keep_mix, swap_cores(give_mix), low_first, swap_cores(low_first))
    peer_parts = peers(normed_two, grad_out_two[0], ahead, behind, lowg1, topg3, grads2, w_up, w_down)
    peer_parts, part_out = lax.optimization_barrier((peer_parts, part_out))
    part_out = part_out.reshape(-1, 4, 8, width)
    part_feed = feed(hid, pre0, *peer_parts, grads2, across, w_up, w_down)
    far, part_feed, part_out = lax.optimization_barrier((far, part_feed, part_out))
    keep, give = attend_back(order, far, queries, keys, vals, probs)
    near_feed = part_feed.reshape(-1, part_feed.shape[2])
    near_feed = lax.psum_scatter(near_feed, "seq", tiled=True, axis_index_groups=along_x_and_core())
    low, near_feed = lax.optimization_barrier((add_low(keep, swap_cores(give)), near_feed))
    near_feed = lax.psum_scatter(near_feed, "seq", tiled=True, axis_index_groups=along_y())
    part_out = tied(part_out, keep)
    blocks = [
        from_ahead(lax.dynamic_index_in_dim(part_out, (ffn + 4 - k) % 4, 1, keepdims=False), k) for k in (1, 2, 3)
    ]
    back = swap_chips(low)
    sums_out = lax.dynamic_index_in_dim(part_out, ffn, 1, keepdims=False).astype(F32)
    for block in blocks:
        sums_out = sums_out + block.astype(F32)
    sums_out = sums_out.astype(BF16).reshape(-1, 32, width // 4)
    back, sums_out = lax.optimization_barrier((back, sums_out))
    hid = tied(hid, keep)
    two_low = down_out(hid, stream_two[0], w_down, far_weights)
    grads = sum_rounds(back)
    grads, near_feed = lax.optimization_barrier((grads, near_feed))
    grads_other = swap_cores(grads)
    grad_second, small = finish(
        grads, stream_two[0], gain_one, w_qk, w_value, grad_out_two[0], grad_gain_two, grad_bias_two
    )
    part = pair(keep_rows, other_rows, grads, grads_other, small, sums_out)
    near = swap_chips(part)
    near, near_feed = lax.optimization_barrier((near, near_feed))
    near = near.astype(F32).sum(axis=0)
    near, near_out = near[:, : 2 * width + 128].reshape(4, 8, -1), near[:, 2 * width + 128 :]
    whole = lax.dynamic_index_in_dim(near, ffn, 0, keepdims=False)
    for k in (1, 2, 3):
        whole = whole + from_ahead(lax.dynamic_index_in_dim(near, (ffn + 4 - k) % 4, 0, keepdims=False), k)
    small = whole[:, 2 * width :]
    lines = small[:, :8] + swap_cores(small)[:, 8:16]
    lines = lines[:, 0::2] + lines[:, 1::2]
    near_feed = near_feed.astype(F32)
    return (
        one_low[None],
        two_low[None],
        grad_first[None],
        grad_second[None],
        lines[:, 0],
        lines[:, 1],
        whole[:, :width],
        whole[:, width : 2 * width],
        near_out.reshape(8, width),
        lines[:, 2],
        lines[:, 3],
        near_feed[:, :1024],
        near_feed[:, 1024:2048],
    )


def solution(mesh):
    return jax.shard_map(
        shards,
        mesh=mesh,
        in_specs=(
            P("ffn", "seq", None),
            P("ffn", "seq", None),
            P("ffn", None),
            P("ffn", "seq", None),
            P(),
            P(),
            P(),
            P(),
            P(),
            P(),
            P(),
            P(None, "ffn"),
            P(None, "ffn"),
            P("ffn", "seq", None),
            P("ffn", "seq", None),
        ),
        out_specs=(
            P("ffn", "seq", None),
            P("ffn", "seq", None),
            P("ffn", "seq", None),
            P("ffn", "seq", None),
            P(("seq", "ffn")),
            P(("seq", "ffn")),
            P(("seq", "ffn"), None),
            P(("seq", "ffn"), None),
            P(("seq", "ffn"), None),
            P(("seq", "ffn")),
            P(("seq", "ffn")),
            P("seq", "ffn"),
            P("seq", "ffn"),
        ),
        check_vma=False,
    )
```
